32 devices in a mesh: dp: 8 (over z, y), tensor: 4 (over x, core).
Axes of the slice: x: 2, y: 2, z: 4, core: 2. Of those that a mesh axis runs over, the one named last changes fastest.
Arguments:
- image_codes: int32 [32, 256], P('dp'), may hold values from 0 to 1023
- labels: int32 [32], P('dp'), may hold values from 0 to 999
- mask_flags: int32 [32, 256], P('dp'), may hold values from 0 to 1, as said below
- attend_in: float32 [2, 768, 3, 768], P(None, 'dp', None, 'tensor'), may hold values from -0.21875 to 0.21875
- attend_in_one: float32 [2, 768, 3, 768], P(None, 'dp', None, 'tensor'), may hold values from -3.33786e-06 to 3.33786e-06
- attend_in_two: float32 [2, 768, 3, 768], P(None, 'dp', None, 'tensor'), may hold values from 1.0048232e-12 to 4.0192927e-12
- attend_out: float32 [2, 768, 768], P(None, 'tensor', 'dp'), may hold values from -1.25 to 1.25
- attend_out_one: float32 [2, 768, 768], P(None, 'tensor', 'dp'), may hold values from -3.33786e-06 to 3.33786e-06
- attend_out_two: float32 [2, 768, 768], P(None, 'tensor', 'dp'), may hold values from 1.0048232e-12 to 4.0192927e-12
- expand: float32 [2, 768, 3072], P(None, 'dp', 'tensor'), may hold values from -0.21875 to 0.21875
- expand_one: float32 [2, 768, 3072], P(None, 'dp', 'tensor'), may hold values from -3.33786e-06 to 3.33786e-06
- expand_two: float32 [2, 768, 3072], P(None, 'dp', 'tensor'), may hold values from 1.0048232e-12 to 4.0192927e-12
- contract: float32 [2, 3072, 768], P(None, 'tensor', 'dp'), may hold values from -0.109375 to 0.109375
- contract_one: float32 [2, 3072, 768], P(None, 'tensor', 'dp'), may hold values from -3.33786e-06 to 3.33786e-06
- contract_two: float32 [2, 3072, 768], P(None, 'tensor', 'dp'), may hold values from 1.0048232e-12 to 4.0192927e-12
- embed_table: float32 [2304, 768], P('dp'), may hold values from -4.2 to 4.2
- embed_one: float32 [2304, 768], P('dp'), may hold values from -3.33786e-06 to 3.33786e-06
- embed_two: float32 [2304, 768], P('dp'), may hold values from 1.0048232e-12 to 4.0192927e-12
- logit_table: float32 [768, 1024], P('dp', 'tensor'), may hold values from -2 to 2
- logit_one: float32 [768, 1024], P('dp', 'tensor'), may hold values from -2.2888184e-05 to 2.2888184e-05
- logit_two: float32 [768, 1024], P('dp', 'tensor'), may hold values from 5.086263e-11 to 2.0345052e-10
- norm_params: float32 [5, 2, 768], P(None, None, 'dp'), may hold values from -0.8 to 2.4
- norm_one: float32 [5, 2, 768], P(None, None, 'dp'), may hold values from -1.335144e-05 to 1.335144e-05
- norm_two: float32 [5, 2, 768], P(None, None, 'dp'), may hold values from 1.6148943e-11 to 6.579199e-11
Outputs:
- new_attend_in: float32 [2, 768, 3, 768], P(None, 'dp', None, 'tensor')
- new_attend_in_one: float32 [2, 768, 3, 768], P(None, 'dp', None, 'tensor')
- new_attend_in_two: float32 [2, 768, 3, 768], P(None, 'dp', None, 'tensor')
- new_attend_out: float32 [2, 768, 768], P(None, 'tensor', 'dp')
- new_attend_out_one: float32 [2, 768, 768], P(None, 'tensor', 'dp')
- new_attend_out_two: float32 [2, 768, 768], P(None, 'tensor', 'dp')
- new_expand: float32 [2, 768, 3072], P(None, 'dp', 'tensor')
- new_expand_one: float32 [2, 768, 3072], P(None, 'dp', 'tensor')
- new_expand_two: float32 [2, 768, 3072], P(None, 'dp', 'tensor')
- new_contract: float32 [2, 3072, 768], P(None, 'tensor', 'dp')
- new_contract_one: float32 [2, 3072, 768], P(None, 'tensor', 'dp')
- new_contract_two: float32 [2, 3072, 768], P(None, 'tensor', 'dp')
- new_embed: float32 [2304, 768], P('dp')
- new_embed_one: float32 [2304, 768], P('dp')
- new_embed_two: float32 [2304, 768], P('dp')
- new_logit: float32 [768, 1024], P('dp', 'tensor')
- new_logit_one: float32 [768, 1024], P('dp', 'tensor')
- new_logit_two: float32 [768, 1024], P('dp', 'tensor')
- new_norm: float32 [5, 2, 768], P(None, None, 'dp')
- new_norm_one: float32 [5, 2, 768], P(None, None, 'dp')
- new_norm_two: float32 [5, 2, 768], P(None, None, 'dp')
- loss_sum: float32 [], replicated
- loss_count: float32 [], replicated
- grad_norm: float32 [], replicated
The draws below stay inside these ranges and needn't reach their ends.
Inputs may be any that keep to these rules, and one draw needn't show every extreme that they name: `mask_flags`: every image has 1 to 256 masked positions, and in every draw some image has all 256 masked.
All inputs are finite; a program needn't handle non-finite values.
Results may differ from the reference program's by a relative error of at most 0.0044.
The reference program's roundings to bfloat16 on the way count: a program that leaves them out, or rounds other values in their place, can miss the bound.
Values may be sent and summed in bfloat16 or wider, within the bound.
A program may use at most 192 MiB of HBM per device.

```python
import math
import jax
import jax.numpy as jnp
from jax import lax

D = 768
HEADS = 16
FF = 3072
CODES = 1024
CLASSES = 1000
CODES_IMG = 256
LAYERS = 2
STEP = 10
IMG_DEV = 4
IMAGES = 32
SEQ = 257
NORMS = 5
ROWS = 2304
PARAMS = 16719360


def draw_mask_flags(key, part):
    key = jax.random.fold_in(key, 7)
    count_key, order_key = jax.random.split(key)
    group_index = jnp.arange(IMAGES) // IMG_DEV
    groups_all = IMAGES // IMG_DEV
    lowest_top = CODES_IMG // 3
    upper_count = lowest_top + (CODES_IMG - lowest_top) * group_index // max(groups_all - 1, 1)
    mask_counts = jax.random.randint(count_key, (IMAGES,), 1, upper_count + 1)
    mask_counts = mask_counts.at[IMAGES - 1].set(CODES_IMG)
    shuffled = jax.vmap(lambda single: jax.random.permutation(single, CODES_IMG))(jax.random.split(order_key, IMAGES))
    positions = jnp.argsort(shuffled, axis=1)
    return (positions < mask_counts[:, None]).astype(jnp.int32)


def draw_logit_table(key, part):
    key = jax.random.fold_in(key, 5)
    ramp_value = jnp.arange(CODES, dtype=jnp.float32) / (CODES - 1)
    column_scale = (1.0 + 2.0 * ramp_value) * D ** (-0.5)
    entries = jax.random.truncated_normal(key, -5.0, 5.0, (D, CODES))
    return (entries * column_scale[None, :]).astype(jnp.float32)


def draw_norm_params(key, part):
    key = jax.random.fold_in(key, 11)
    gain_key, offset_key = jax.random.split(key)
    ramp_value = jnp.arange(D, dtype=jnp.float32) / (D - 1)
    rising = 0.5 + ramp_value
    offsets = 0.2 * jax.random.truncated_normal(offset_key, -4.0, 4.0, (NORMS, D))
    gains = rising[None, :] * jax.random.uniform(gain_key, (NORMS, D), minval=0.8, maxval=1.2)
    return jnp.stack([gains, offsets], axis=1).astype(jnp.float32)


def set_ends(values, own_key, low, largest):
    longest = values.shape.index(max(values.shape))
    spots = []
    for shift in (0, 1):
        where = [jax.random.randint(jax.random.fold_in(own_key, axis), (), 0, length) for axis, length in enumerate(values.shape)]
        where[longest] = (where[longest] + shift) % values.shape[longest]
        spots.append(tuple(where))
    return values.at[spots[0]].set(low).at[spots[1]].set(largest)


def levels(own_key, dims, cuts, least, high):
    def one(position, blocks):
        steps = jax.random.uniform(jax.random.fold_in(jax.random.fold_in(own_key, 6), position), (blocks,), jnp.float32, least / len(cuts), high / len(cuts))
        return jnp.repeat(jnp.exp(steps), dims[position] // blocks).reshape((-1,) + (1,) * (len(dims) - position - 1))

    loudness = one(*cuts[0])
    for cut in cuts[1:]:
        loudness = loudness * one(*cut)
    return loudness


def gaussian(key, shape, spread, limit, cuts=(), held_as=jnp.bfloat16):
    loudness = levels(key, shape, cuts, -0.22, 0.18) if cuts else 1.0
    drawn = jax.random.normal(key, shape, jnp.float32) * spread * loudness
    return jnp.minimum(jnp.maximum(drawn, -limit), limit).astype(held_as)


def setup_inputs(seed: int = 0) -> dict:
    key_list = jax.random.split(jax.random.key(seed), 25)
    image_codes = set_ends(jax.random.randint(key_list[0], (IMAGES, CODES_IMG), 0, CODES), jax.random.fold_in(key_list[0], 1), 0, CODES - 1).astype(jnp.int32)
    labels = set_ends(jax.random.randint(key_list[1], (IMAGES,), 0, CLASSES), jax.random.fold_in(key_list[1], 1), 0, CLASSES - 1).astype(jnp.int32)
    mask_flags = draw_mask_flags(jax.random.fold_in(key_list[24], 71), 0)
    attend_in = gaussian(key_list[3], (LAYERS, D, 3, D), D ** -0.5, 0.21875, ((1, 8), (3, 4)), jnp.float32)
    attend_in_one = gaussian(key_list[4], (LAYERS, D, 3, D), (0.0022 / PARAMS ** 0.5), 3.337860107421875e-06, ((1, 8), (3, 4)), jnp.float32)
    attend_in_two = jnp.clip(jnp.exp(math.log(4.019292711154865e-12) - 1.3862944 * jax.random.uniform(key_list[5], (LAYERS, D, 3, D), jnp.float32) ** levels(key_list[5], (LAYERS, D, 3, D), ((1, 8), (3, 4)), -0.2, 0.2)), 1.0048231777887162e-12, 4.019292711154865e-12)
    attend_out = gaussian(key_list[6], (LAYERS, D, D), (D // 32) ** -0.5, 1.25, ((1, 4), (2, 8)), jnp.float32)
    attend_out_one = gaussian(key_list[7], (LAYERS, D, D), (0.0022 / PARAMS ** 0.5), 3.337860107421875e-06, ((1, 4), (2, 8)), jnp.float32)
    attend_out_two = jnp.clip(jnp.exp(math.log(4.019292711154865e-12) - 1.3862944 * jax.random.uniform(key_list[8], (LAYERS, D, D), jnp.float32) ** levels(key_list[8], (LAYERS, D, D), ((1, 4), (2, 8)), -0.2, 0.2)), 1.0048231777887162e-12, 4.019292711154865e-12)
    expand = gaussian(key_list[9], (LAYERS, D, FF), D ** -0.5, 0.21875, ((1, 8), (2, 4)), jnp.float32)
    expand_one = gaussian(key_list[10], (LAYERS, D, FF), (0.0022 / PARAMS ** 0.5), 3.337860107421875e-06, ((1, 8), (2, 4)), jnp.float32)
    expand_two = jnp.clip(jnp.exp(math.log(4.019292711154865e-12) - 1.3862944 * jax.random.uniform(key_list[11], (LAYERS, D, FF), jnp.float32) ** levels(key_list[11], (LAYERS, D, FF), ((1, 8), (2, 4)), -0.2, 0.2)), 1.0048231777887162e-12, 4.019292711154865e-12)
    contract = gaussian(key_list[12], (LAYERS, FF, D), FF ** -0.5, 0.109375, ((1, 4), (2, 8)), jnp.float32)
    contract_one = gaussian(key_list[13], (LAYERS, FF, D), (0.0022 / PARAMS ** 0.5), 3.337860107421875e-06, ((1, 4), (2, 8)), jnp.float32)
    contract_two = jnp.clip(jnp.exp(math.log(4.019292711154865e-12) - 1.3862944 * jax.random.uniform(key_list[14], (LAYERS, FF, D), jnp.float32) ** levels(key_list[14], (LAYERS, FF, D), ((1, 4), (2, 8)), -0.2, 0.2)), 1.0048231777887162e-12, 4.019292711154865e-12)
    embed_table = gaussian(key_list[15], (ROWS, D), 0.7, 4.2, ((0, 8),), jnp.float32)
    embed_one = gaussian(key_list[16], (ROWS, D), (0.0022 / PARAMS ** 0.5), 3.337860107421875e-06, ((0, 8),), jnp.float32)
    embed_two = jnp.clip(jnp.exp(math.log(4.019292711154865e-12) - 1.3862944 * jax.random.uniform(key_list[17], (ROWS, D), jnp.float32) ** levels(key_list[17], (ROWS, D), ((0, 8),), -0.2, 0.2)), 1.0048231777887162e-12, 4.019292711154865e-12)
    logit_table = draw_logit_table(jax.random.fold_in(key_list[24], 71), 0)
    logit_one = gaussian(key_list[19], (D, CODES), (0.0034 / (D * CODES) ** 0.5), 2.288818359375e-05, ((0, 8), (1, 4)), jnp.float32)
    logit_two = jnp.clip(jnp.exp(math.log(2.0345052031967015e-10) - 1.3862944 * jax.random.uniform(key_list[20], (D, CODES), jnp.float32) ** levels(key_list[20], (D, CODES), ((0, 8), (1, 4)), -0.2, 0.2)), 5.086263007991754e-11, 2.0345052031967015e-10)
    norm_params = draw_norm_params(jax.random.fold_in(key_list[24], 71), 0)
    norm_one = gaussian(key_list[22], (NORMS, 2, D), (0.0088 / PARAMS ** 0.5), 1.33514404296875e-05, ((2, 8),), jnp.float32)
    norm_two = jnp.clip(jnp.exp(math.log(6.579198991163437e-11) - 1.4046435 * jax.random.uniform(key_list[23], (NORMS, 2, D), jnp.float32) ** levels(key_list[23], (NORMS, 2, D), ((2, 8),), -0.2, 0.2)), 1.6148943293714524e-11, 6.579198991163437e-11)
    return {"image_codes": image_codes, "labels": labels, "mask_flags": mask_flags, "attend_in": attend_in, "attend_in_one": attend_in_one, "attend_in_two": attend_in_two, "attend_out": attend_out, "attend_out_one": attend_out_one, "attend_out_two": attend_out_two, "expand": expand, "expand_one": expand_one, "expand_two": expand_two, "contract": contract, "contract_one": contract_one, "contract_two": contract_two, "embed_table": embed_table, "embed_one": embed_one, "embed_two": embed_two, "logit_table": logit_table, "logit_one": logit_one, "logit_two": logit_two, "norm_params": norm_params, "norm_one": norm_one, "norm_two": norm_two}


@jax.custom_vjp
def low(v):
    return lax.optimization_barrier(v.astype(jnp.bfloat16)).astype(jnp.float32)

@jax.custom_vjp
def low_back(v):
    return v

def low_keep(v):
    return (low(v), None)

def low_pass(kept, grad):
    return (grad,)

def back_keep(v):
    return (v, None)

def back_low(kept, grad):
    return (low(grad),)
low.defvjp(low_keep, low_pass)
low_back.defvjp(back_keep, back_low)
highest = lax.Precision.HIGHEST
beta_one = 0.9
beta_two = 0.96
matrix_rate = 0.02
embed_rate = 0.5
vector_rate = 0.25
weight_decay = 0.045
epsilon = 1e-10
clip_limit = 0.02
norm_epsilon = 1e-06

def layer_norm(stream, scaling, offset):
    average = lax.optimization_barrier(jnp.mean(stream, axis=-1, keepdims=True))
    centred = stream - average
    variance = lax.optimization_barrier(jnp.mean(centred * centred, axis=-1, keepdims=True))
    return centred * lax.rsqrt(variance + norm_epsilon) * scaling + offset

def attend_image(block):
    queries, key_rows, values = block
    score_scale = queries.shape[-1] ** (-0.5)
    scores = low_back(jnp.einsum('qhd,khd->hqk', queries, key_rows, precision=highest) * score_scale)
    attention = jax.nn.softmax(scores, axis=-1)
    blended = jnp.einsum('hqk,khd->qhd', low(attention), values, precision=highest)
    return low(low_back(blended))

def forward(params, row_index, place_rows, targets, weights_loss, token_count):
    attend_in, attend_out, expand, contract, embed_rows, logit_table, norms = [low(weight) for weight in params]
    images = row_index.shape[0]
    stream = embed_rows[row_index] + embed_rows[place_rows]
    stream = stream.reshape(images * SEQ, D)
    for layer_index in range(LAYERS):
        normed = low(layer_norm(stream, norms[2 * layer_index, 0], norms[2 * layer_index, 1]))
        joined = jnp.dot(normed, attend_in[layer_index].reshape(D, 3 * D), precision=highest)
        joined = low(low_back(joined)).reshape(images, SEQ, 3, HEADS, D // HEADS)
        blended = lax.map(jax.checkpoint(attend_image), (joined[:, :, 0], joined[:, :, 1], joined[:, :, 2]))
        stream = stream + low_back(jnp.dot(blended.reshape(images * SEQ, D), attend_out[layer_index], precision=highest))
        normed = low(layer_norm(stream, norms[2 * layer_index + 1, 0], norms[2 * layer_index + 1, 1]))
        hidden = low_back(jnp.dot(normed, expand[layer_index], precision=highest))
        active = low(jax.nn.gelu(hidden, approximate=False))
        stream = stream + low_back(jnp.dot(active, contract[layer_index], precision=highest))
    final = low(layer_norm(stream, norms[2 * LAYERS, 0], norms[2 * LAYERS, 1]))
    logits = low_back(jnp.dot(final, logit_table, precision=highest))
    log_total = jax.nn.logsumexp(logits, axis=-1)
    picked = jnp.take_along_axis(logits, targets[:, None], axis=1)[:, 0]
    loss_sum = jnp.sum((log_total - picked) * weights_loss)
    return (loss_sum / token_count, loss_sum)

def adam_step(weight, moment_one, moment_two, gradient, factor, rate_here, decay_here):
    gradient = gradient * factor
    moment_one = beta_one * moment_one + (1.0 - beta_one) * gradient
    moment_two = beta_two * moment_two + (1.0 - beta_two) * gradient * gradient
    correct_one = 1.0 - beta_one ** STEP
    correct_two = 1.0 - beta_two ** STEP
    weight = weight - rate_here * (moment_one / correct_one / (jnp.sqrt(moment_two / correct_two) + epsilon) + decay_here * weight)
    return [weight, moment_one, moment_two]

def reference(image_codes, labels, mask_flags, attend_in, attend_in_one, attend_in_two, attend_out, attend_out_one, attend_out_two, expand, expand_one, expand_two, contract, contract_one, contract_two, embed_table, embed_one, embed_two, logit_table, logit_one, logit_two, norm_params, norm_one, norm_two):
    images = labels.shape[0]
    code_rows = jnp.where(mask_flags == 1, CODES, image_codes)
    row_index = jnp.concatenate([(CODES + 1 + labels)[:, None], code_rows], axis=1).astype(jnp.int32)
    place_rows = (CODES + 1 + CLASSES + jnp.arange(SEQ)).astype(jnp.int32)
    targets = jnp.concatenate([jnp.zeros((images, 1), jnp.int32), image_codes], axis=1).reshape(-1).astype(jnp.int32)
    weights_loss = jnp.concatenate([jnp.zeros((images, 1), jnp.float32), mask_flags.astype(jnp.float32)], axis=1).reshape(-1)
    token_count = jnp.sum(weights_loss)
    params = (attend_in, attend_out, expand, contract, embed_table, logit_table, norm_params)
    moments_one = (attend_in_one, attend_out_one, expand_one, contract_one, embed_one, logit_one, norm_one)
    moments_two = (attend_in_two, attend_out_two, expand_two, contract_two, embed_two, logit_two, norm_two)

    def objective(*weights):
        return forward(weights, row_index, place_rows, targets, weights_loss, token_count)
    mean_loss, pull, loss_sum = jax.vjp(objective, *params, has_aux=True)
    gradients = pull(jnp.ones((), jnp.float32))
    squares = jnp.zeros((), jnp.float32)
    for gradient in gradients:
        squares = squares + jnp.sum(gradient * gradient)
    grad_norm = jnp.sqrt(squares)
    factor = clip_limit / jnp.maximum(grad_norm, clip_limit)
    results = []
    for index in range(7):
        rate_here = vector_rate if index == 6 else embed_rate if index == 4 else matrix_rate
        decay_here = 0.0 if index == 6 else weight_decay
        results.extend(adam_step(params[index], moments_one[index], moments_two[index], gradients[index], factor, rate_here, decay_here))
    return (results[0], results[1], results[2], results[3], results[4], results[5], results[6], results[7], results[8], results[9], results[10], results[11], results[12], results[13], results[14], results[15], results[16], results[17], results[18], results[19], results[20], loss_sum, token_count, grad_norm)
```

```python
import functools

import jax
import jax.numpy as jnp
from jax import lax
from jax.experimental import pallas as pl
from jax.experimental.pallas import tpu as pltpu
from jax.sharding import PartitionSpec as P

HEADS = 16
CODES = 1024
CLASSES = 1000
LAYERS = 2
STEP = 10
SEQ = 257

beta_one = 0.9
beta_two = 0.96
matrix_rate = 0.02
embed_rate = 0.5
vector_rate = 0.25
weight_decay = 0.045
epsilon = 1e-10
clip_limit = 0.02
norm_epsilon = 1e-06
low = jnp.bfloat16
full = jnp.float32


def matmul(left, right):
    return jnp.dot(left, right, preferred_element_type=full)


def matmul_left(left, right):
    return lax.dot_general(left, right, (((0,), (0,)), ((), ())), preferred_element_type=full)


def matmul_right(left, right):
    return lax.dot_general(left, right, (((1,), (1,)), ((), ())), preferred_element_type=full)


def layer_norm(stream, scaling, offset):
    average = jnp.mean(stream, axis=-1, keepdims=True)
    centred = stream - average
    variance = jnp.mean(centred * centred, axis=-1, keepdims=True)
    return centred * lax.rsqrt(variance + norm_epsilon) * scaling + offset


def norm_back(stream, scaling, offset, gradient):
    normed_out, pull = jax.vjp(layer_norm, stream, scaling, offset)
    return pull(gradient)


def gelu_exact(values):
    return jax.nn.gelu(values, approximate=False)


def attend_forward_kernel(images, heads, width, *refs):
    count = len(refs) // 2
    scale = width ** (-0.5)
    for joined, blended in zip(refs[:count], refs[count:]):
        for image in range(images):
            rows = pl.ds(image * SEQ, SEQ)
            for head in range(heads):
                at = head * width
                query = joined[rows, at : at + width]
                key = joined[rows, (heads * width + at) : (heads * width + at + width)]
                value = joined[rows, (2 * heads * width + at) : (2 * heads * width + at + width)]
                scores = matmul_right(query, key) * scale
                top = jnp.max(scores, axis=-1, keepdims=True)
                weights = jnp.exp(scores - top)
                weights = weights / jnp.sum(weights, axis=-1, keepdims=True)
                blended[rows, at : at + width] = matmul(weights.astype(low), value).astype(low)


def attend_forward(joined, images, heads, width):
    rows = joined[0].shape[0]
    return pl.pallas_call(
        functools.partial(attend_forward_kernel, images, heads, width),
        out_shape=[jax.ShapeDtypeStruct((rows, heads * width), low) for _ in joined],
        in_specs=[pl.BlockSpec(memory_space=pltpu.VMEM)] * len(joined),
        out_specs=[pl.BlockSpec(memory_space=pltpu.VMEM)] * len(joined),
        compiler_params=pltpu.CompilerParams(vmem_limit_bytes=32 * 1024 * 1024),
        cost_estimate=pl.CostEstimate(
            flops=len(joined) * images * heads * SEQ * SEQ * width * 4,
            bytes_accessed=len(joined) * rows * heads * width * 8,
            transcendentals=len(joined) * images * heads * SEQ * SEQ,
        ),
    )(*joined)


def attend_backward_kernel(images, heads, width, *refs):
    count = len(refs) // 3
    scale = width ** (-0.5)
    for joined, grad, out in zip(refs[:count], refs[count : 2 * count], refs[2 * count :]):
        for image in range(images):
            rows = pl.ds(image * SEQ, SEQ)
            for head in range(heads):
                at = head * width
                spots = [pl.ds(part * heads * width + at, width) for part in range(3)]
                query, key, value = [joined[rows, spot] for spot in spots]
                up = grad[rows, at : at + width]
                scores = matmul_right(query, key) * scale
                top = jnp.max(scores, axis=-1, keepdims=True)
                weights = jnp.exp(scores - top)
                weights = weights / jnp.sum(weights, axis=-1, keepdims=True)
                pulled = matmul_right(up, value)
                total = jnp.sum(weights * pulled, axis=-1, keepdims=True)
                moved = (weights * (pulled - total)).astype(low)
                out[rows, spots[0]] = (matmul(moved, key) * scale).astype(low)
                out[rows, spots[1]] = (matmul_left(moved, query) * scale).astype(low)
                out[rows, spots[2]] = matmul_left(weights.astype(low), up).astype(low)


def attend_backward(joined, grads, images, heads, width):
    return pl.pallas_call(
        functools.partial(attend_backward_kernel, images, heads, width),
        out_shape=[jax.ShapeDtypeStruct(block.shape, low) for block in joined],
        in_specs=[pl.BlockSpec(memory_space=pltpu.VMEM)] * (2 * len(joined)),
        out_specs=[pl.BlockSpec(memory_space=pltpu.VMEM)] * len(joined),
        compiler_params=pltpu.CompilerParams(vmem_limit_bytes=32 * 1024 * 1024),
        cost_estimate=pl.CostEstimate(
            flops=len(joined) * images * heads * SEQ * SEQ * width * 10,
            bytes_accessed=len(joined) * joined[0].shape[0] * heads * width * 14,
            transcendentals=len(joined) * images * heads * SEQ * SEQ,
        ),
    )(*joined, *grads)


MESH = pl.DeviceIdType.MESH


def factors(dp, tensor):
    return [("tensor", tensor // 2, 2), ("tensor", 2, 1), ("dp", dp // 2, 2), ("dp", 2, 1)]


OUTER, PAIR, LONG, NEAR = range(4)
ORDERS = {
    "a": (LONG, NEAR, OUTER, PAIR),
    "b": (LONG, OUTER, NEAR, PAIR),
    "d": (OUTER, LONG, NEAR, PAIR),
    "e": (NEAR, LONG, OUTER, PAIR),
}


def place_of(dims):
    return [(lax.axis_index(axis) // stride) % size for axis, size, stride in dims]


def peer_of(dims, here, dim, move):
    there = list(here)
    there[dim] = lax.rem(here[dim] + move, dims[dim][1])
    found = {"dp": 0, "tensor": 0}
    for (axis, size, stride), at in zip(dims, there):
        found[axis] = found[axis] + at * stride
    return (found["dp"], found["tensor"])


def greet(dims, here):
    barrier = pltpu.get_barrier_semaphore()
    count = 0
    for dim, (axis, size, stride) in enumerate(dims):
        for move in range(1, size):
            pl.semaphore_signal(
                barrier, inc=1, device_id=peer_of(dims, here, dim, move), device_id_type=MESH
            )
            count += 1
    pl.semaphore_wait(barrier, count)


def gather_units(rows):
    tiles = rows // 16
    if rows % 16 or tiles < 4:
        return [[(0, rows, "a")]]
    if tiles == 6:
        cuts = [[("a", 1), ("b", 1), ("d", 1)], [("a", 1), ("b", 1), ("e", 1)]]
    else:
        cuts = [[("a", 1), ("b", 1)], [("a", 1), ("b", 1), ("d", tiles - 4)]]
    units, row = [], 0
    for cut in cuts:
        unit = []
        for order, count in cut:
            unit.append((row, 16 * count, order))
            row += 16 * count
        units.append(unit)
    return units


def gather_kernel(dims, shapes, *refs):
    count = len(shapes)
    pieces, wholes, (send, recv, own) = refs[:count], refs[count : 2 * count], refs[2 * count :]
    here = place_of(dims)
    greet(dims, here)
    copies_own = [
        pltpu.make_async_copy(pieces[at], wholes[at].at[tuple(here)], own.at[at]) for at in range(count)
    ]
    for copy in copies_own:
        copy.start()
    slot, units = 0, []
    for chunk, (rows, width) in enumerate(shapes):
        for unit in gather_units(rows):
            stages = [[], [], [], []]
            for row, size, order in unit:
                span = (pl.ds(row, size),) if size != rows else ()
                for stage, dim in enumerate(ORDERS[order]):
                    done = ORDERS[order][:stage]
                    block = wholes[chunk].at[
                        tuple(slice(None) if at in done else here[at] for at in range(4)) + span
                    ]
                    source = block
                    if stage == 0:
                        source = pieces[chunk].at[span] if span else pieces[chunk]
                    for move in range(1, dims[dim][1]):
                        stages[stage].append(
                            pltpu.make_async_remote_copy(
                                src_ref=source,
                                dst_ref=block,
                                send_sem=send.at[slot],
                                recv_sem=recv.at[slot],
                                device_id=peer_of(dims, here, dim, move),
                                device_id_type=MESH,
                            )
                        )
                        slot += 1
            units.append((chunk, stages))
    ready = set()
    for tick in range(len(units) + 8):
        for at, (chunk, stages) in enumerate(units):
            if (tick - at) % 2 or not 0 <= tick - at <= 8:
                continue
            stage = (tick - at) // 2
            if stage:
                for copy in stages[stage - 1]:
                    copy.wait_recv()
            if stage == 1 and chunk not in ready:
                copies_own[chunk].wait()
                ready.add(chunk)
            if stage < 4:
                for copy in stages[stage]:
                    copy.start()
    for chunk, stages in units:
        for stage in stages:
            for copy in stage:
                copy.wait_send()


def gather_all(dims, pieces):
    shapes = [piece.shape for piece in pieces]
    sizes = [size for axis, size, stride in dims]
    slots = sum(sum(size - 1 for size in sizes) * len(u) for r, w in shapes for u in gather_units(r))
    wholes = pl.pallas_call(
        functools.partial(gather_kernel, dims, shapes),
        out_shape=[jax.ShapeDtypeStruct((*sizes, *shape), low) for shape in shapes],
        in_specs=[pl.BlockSpec(memory_space=pl.ANY)] * len(shapes),
        out_specs=[pl.BlockSpec(memory_space=pl.ANY)] * len(shapes),
        scratch_shapes=[
            pltpu.SemaphoreType.DMA((slots,)),
            pltpu.SemaphoreType.DMA((slots,)),
            pltpu.SemaphoreType.DMA((len(shapes),)),
        ],
        compiler_params=pltpu.CompilerParams(collective_id=0, has_side_effects=True),
    )(*pieces)
    return [whole.reshape(sizes[0] * sizes[1], -1, whole.shape[-1]) for whole in wholes]


def adam_step(weight, moment_one, moment_two, gradient, factor, rate_here, decay_here):
    gradient = gradient * factor
    moment_one = beta_one * moment_one + (1.0 - beta_one) * gradient
    moment_two = beta_two * moment_two + (1.0 - beta_two) * gradient * gradient
    correct_one = 1.0 - beta_one**STEP
    correct_two = 1.0 - beta_two**STEP
    weight = weight - rate_here * (
        moment_one / correct_one / (jnp.sqrt(moment_two / correct_two) + epsilon)
        + decay_here * weight
    )
    return [weight, moment_one, moment_two]


def masks_of(size):
    return [1 << bit for bit in reversed(range(size.bit_length() - 1))]


class Exchange:
    def __init__(self, dp, tensor):
        self.dp, self.tensor = dp, tensor
        self.dp_masks, self.tensor_masks = masks_of(dp), masks_of(tensor)

    def orders(self, kind):
        depth = [("dp", mask) for mask in self.dp_masks]
        outer = [("tensor", mask) for mask in self.tensor_masks]
        if kind == 0:
            return depth + outer
        return depth[:-1] + outer[:-1] + depth[-1:] + outer[-1:]

    def swap(self, value, axis, mask):
        size = self.dp if axis == "dp" else self.tensor
        return lax.ppermute(value, axis, [(at, at ^ mask) for at in range(size)])

    def reduce(self, blocks, kind, last=full):
        width = blocks[0].shape[-1]
        left = [("tensor", mask) for mask in self.tensor_masks] + [("dp", mask) for mask in self.dp_masks]
        value = jnp.stack(blocks).reshape((2,) * len(left) + (-1, width))
        order = self.orders(kind)[::-1]
        for step, (axis, mask) in enumerate(order):
            kind_here = last if step == len(order) - 1 else low
            bit = (lax.axis_index(axis) & mask) // mask
            place = left.index((axis, mask))
            left.remove((axis, mask))
            away = lax.dynamic_index_in_dim(value, 1 - bit, place, keepdims=False)
            kept = lax.dynamic_index_in_dim(value, bit, place, keepdims=False)
            value = kept + self.swap(away.astype(kind_here), axis, mask).astype(full)
        return value

    def spread(self, piece):
        held = piece[None]
        for mask in self.tensor_masks[::-1]:
            upper = (lax.axis_index("tensor") & mask) != 0
            other = self.swap(held, "tensor", mask)
            held = jnp.where(
                upper, jnp.concatenate([other, held], 0), jnp.concatenate([held, other], 0)
            )
        return held


def body(
    dp,
    tensor,
    image_codes,
    labels,
    mask_flags,
    attend_in,
    attend_in_one,
    attend_in_two,
    attend_out,
    attend_out_one,
    attend_out_two,
    expand,
    expand_one,
    expand_two,
    contract,
    contract_one,
    contract_two,
    embed_table,
    embed_one,
    embed_two,
    logit_table,
    logit_one,
    logit_two,
    norm_params,
    norm_one,
    norm_two,
):
    links = Exchange(dp, tensor)
    own = lax.axis_index("tensor")
    depth = attend_in.shape[1]
    model = depth * dp
    part = attend_in.shape[3]
    norms = norm_params.shape[0]

    share = embed_table.shape[0] // tensor
    embed_own = lax.dynamic_slice_in_dim(embed_table, own * share, share, 0).astype(low)
    norm_flat = norm_params.astype(low).reshape(-1)
    norm_rows = -(-norm_flat.shape[0] // model)
    norm_flat = jnp.pad(norm_flat, (0, norm_rows * model - norm_flat.shape[0])).reshape(norm_rows, model)
    lines = -(-(share + norm_rows) // 16) * 16
    embed_piece = jnp.concatenate(
        [embed_own, norm_flat, jnp.zeros((lines - share - norm_rows, model), low)], 0
    )
    attend_pieces, expand_pieces, contract_pieces = [], [], []
    for layer in range(LAYERS):
        planes = attend_in[layer].astype(low)
        attend_pieces.append(
            jnp.concatenate([planes[:, 0], planes[:, 1], planes[:, 2], attend_out[layer].astype(low).T], 1)
        )
        expand_pieces.append(expand[layer].astype(low))
        contract_pieces.append(contract[layer].astype(low).T)

    pieces = [embed_piece]
    for layer in range(LAYERS):
        pieces += [attend_pieces[layer], expand_pieces[layer], contract_pieces[layer]]
    gathered = gather_all(factors(dp, tensor), pieces + [logit_table.astype(low)])
    table_all, w_head = gathered[0], gathered[-1]
    w_attend, w_expand, w_contract = gathered[1:-1:3], gathered[2:-1:3], gathered[3:-1:3]
    spots = list(range(tensor))

    gains = table_all[0].reshape(dp, lines, model)[:, share : share + norm_rows].reshape(dp, -1)
    gains = gains[:, : norms * 2 * depth].reshape(dp, norms, 2, depth).transpose(1, 2, 0, 3)
    gains = gains.reshape(norms, 2, model).astype(full)
    table = jnp.concatenate(
        [
            table_all[at].reshape(dp, lines, model)[:, :share].reshape(-1, model)
            for at in spots
        ],
        0,
    )

    token_count = lax.psum(jnp.sum(mask_flags.astype(full)), "dp")
    images = labels.shape[0] // tensor
    codes_own = lax.dynamic_slice_in_dim(image_codes, own * images, images, 0)
    flags_own = lax.dynamic_slice_in_dim(mask_flags, own * images, images, 0)
    labels_own = lax.dynamic_slice_in_dim(labels, own * images, images, 0)
    code_rows = jnp.where(flags_own == 1, CODES, codes_own)
    row_index = jnp.concatenate([(CODES + 1 + labels_own)[:, None], code_rows], axis=1).reshape(-1)
    place_rows = jnp.tile(CODES + 1 + CLASSES + jnp.arange(SEQ, dtype=jnp.int32), images)
    targets = jnp.concatenate([jnp.zeros((images, 1), jnp.int32), codes_own], axis=1).reshape(-1)
    weights_loss = jnp.concatenate(
        [jnp.zeros((images, 1), full), flags_own.astype(full)], axis=1
    ).reshape(-1)

    def spot_of(rows):
        block, inside = rows // (share * tensor), rows % (share * tensor)
        return (inside // share) * (share * dp) + block * share + inside % share

    row_numbers = jnp.arange(table.shape[0], dtype=jnp.int32)[:, None]
    picks = (
        (row_numbers == spot_of(row_index)[None, :]).astype(full)
        + (row_numbers == spot_of(place_rows)[None, :]).astype(full)
    ).astype(low)

    head_count = HEADS // tensor
    head_width = model // HEADS
    stream = matmul_left(picks, table)
    saved_all = []
    for layer in range(LAYERS):
        gain, gain_two = gains[2 * layer], gains[2 * layer + 1]
        normed = layer_norm(stream, gain[0], gain[1]).astype(low)
        joined = [matmul(normed, w_attend[layer][at][:, : 3 * part]).astype(low) for at in spots]
        blended = attend_forward(joined, images, head_count, head_width)
        middle = stream + sum(
            matmul_right(blended[at], w_attend[layer][at][:, 3 * part :]) for at in spots
        )
        normed_two = layer_norm(middle, gain_two[0], gain_two[1]).astype(low)
        hidden = [matmul(normed_two, w_expand[layer][at]) for at in spots]
        active = [gelu_exact(block).astype(low) for block in hidden]
        result = middle + sum(matmul_right(active[at], w_contract[layer][at]) for at in spots)
        saved_all.append((stream, normed, joined, blended, middle, normed_two, hidden, active))
        stream = result

    final_gain = gains[2 * LAYERS]
    final = layer_norm(stream, final_gain[0], final_gain[1]).astype(low)
    logits = jnp.concatenate([matmul(final, w_head[at]) for at in spots], 1)
    local = logit_table.shape[1]
    code_ids = jnp.arange(local * tensor, dtype=jnp.int32)
    is_target = (targets[:, None] == code_ids[None, :]).astype(full)
    peak = jnp.max(logits, axis=1, keepdims=True)
    log_total = peak + jnp.log(jnp.sum(jnp.exp(logits - peak), axis=1, keepdims=True))
    picked = jnp.sum(is_target * logits, axis=1)
    loss_sum = lax.psum(jnp.sum((log_total[:, 0] - picked) * weights_loss), ("dp", "tensor"))
    grad_logits = (
        (jnp.exp(logits - log_total) - is_target) * (weights_loss / token_count)[:, None]
    ).astype(low)
    grad_logits = [grad_logits[:, at * local : (at + 1) * local] for at in spots]
    g_head = links.reduce([matmul_left(final, grad_logits[at]) for at in spots], 0)
    grad_final = sum(matmul_right(grad_logits[at], w_head[at]) for at in spots)
    gradient, final_scale, final_offset = norm_back(stream, final_gain[0], final_gain[1], grad_final)

    norm_grads = [None] * norms
    norm_grads[2 * LAYERS] = jnp.stack([final_scale, final_offset])
    g_attend, g_expand, g_contract = [None] * LAYERS, [None] * LAYERS, [None] * LAYERS
    for layer in reversed(range(LAYERS)):
        stream, normed, joined, blended, middle, normed_two, hidden, active = saved_all[layer]
        gain, gain_two = gains[2 * layer], gains[2 * layer + 1]
        grad_low = gradient.astype(low)
        g_contract[layer] = links.reduce([matmul_left(grad_low, active[at]) for at in spots], 1)
        grad_hidden = []
        for at in spots:
            grad_active = matmul(grad_low, w_contract[layer][at])
            gelu_out, gelu_pull = jax.vjp(gelu_exact, hidden[at])
            grad_hidden.append(gelu_pull(grad_active)[0].astype(low))
        g_expand[layer] = links.reduce([matmul_left(normed_two, grad_hidden[at]) for at in spots], 0)
        grad_normed = sum(matmul_right(grad_hidden[at], w_expand[layer][at]) for at in spots)
        grad_mid, scale_two, offset_two = norm_back(middle, gain_two[0], gain_two[1], grad_normed)
        gradient = gradient + grad_mid
        grad_low = gradient.astype(low)
        grad_blended = [matmul(grad_low, w_attend[layer][at][:, 3 * part :]).astype(low) for at in spots]
        grad_joined = attend_backward(joined, grad_blended, images, head_count, head_width)
        g_attend[layer] = links.reduce(
            [
                jnp.concatenate(
                    [matmul_left(normed, grad_joined[at]), matmul_left(grad_low, blended[at])], 1
                )
                for at in spots
            ],
            1,
        )
        grad_normed = sum(
            matmul_right(grad_joined[at], w_attend[layer][at][:, : 3 * part]) for at in spots
        )
        grad_first, scale_one, offset_one = norm_back(stream, gain[0], gain[1], grad_normed)
        gradient = gradient + grad_first
        norm_grads[2 * layer] = jnp.stack([scale_one, offset_one])
        norm_grads[2 * layer + 1] = jnp.stack([scale_two, offset_two])

    upper = gradient.astype(low)
    lower = (gradient - upper.astype(full)).astype(low)
    g_table = matmul(jnp.concatenate([picks, picks], 1), jnp.concatenate([upper, lower], 0))
    g_table = g_table.reshape(tensor, dp, share, model)
    g_norms = jnp.stack(norm_grads).reshape(norms, 2, dp, depth).transpose(2, 0, 1, 3).reshape(dp, -1)
    norm_size = g_norms.shape[1]
    norm_share = -(-norm_size // tensor)
    g_norms = jnp.pad(g_norms, ((0, 0), (0, norm_share * tensor - norm_size))).reshape(dp, tensor, norm_share)
    norm_lines = -(-norm_share // model)
    g_norms = jnp.pad(g_norms, ((0, 0), (0, 0), (0, norm_lines * model - norm_share)))
    g_norms = g_norms.reshape(dp, tensor, norm_lines, model)
    tail = links.reduce(
        [jnp.concatenate([g_table[at], g_norms[:, at]], 1).reshape(-1, model) for at in spots], 0
    )
    tail_all = links.spread(tail)
    g_embed = tail_all[:, :share].reshape(-1, model)
    g_norm = tail_all[:, share:].reshape(tensor, -1)[:, :norm_share].reshape(-1)[:norm_size]
    g_norm = g_norm.reshape(norms, 2, depth)

    squares = jnp.sum(tail * tail) + jnp.sum(g_head * g_head)
    for group in (g_attend, g_expand, g_contract):
        for block in group:
            squares = squares + jnp.sum(block * block)
    grad_norm = jnp.sqrt(lax.psum(squares, ("dp", "tensor")))
    factor = clip_limit / jnp.maximum(grad_norm, clip_limit)

    g_in = jnp.stack([block[:, : 3 * part].reshape(depth, 3, part) for block in g_attend])
    g_out = jnp.stack([block[:, 3 * part :].T for block in g_attend])
    gradients = (
        g_in,
        g_out,
        jnp.stack(g_expand),
        jnp.stack([block.T for block in g_contract]),
        g_embed,
        g_head,
        g_norm,
    )
    params = (attend_in, attend_out, expand, contract, embed_table, logit_table, norm_params)
    moments_one = (
        attend_in_one,
        attend_out_one,
        expand_one,
        contract_one,
        embed_one,
        logit_one,
        norm_one,
    )
    moments_two = (
        attend_in_two,
        attend_out_two,
        expand_two,
        contract_two,
        embed_two,
        logit_two,
        norm_two,
    )
    results = []
    for index in range(7):
        rate_here = vector_rate if index == 6 else embed_rate if index == 4 else matrix_rate
        decay_here = 0.0 if index == 6 else weight_decay
        results.extend(
            adam_step(
                params[index],
                moments_one[index],
                moments_two[index],
                gradients[index],
                factor,
                rate_here,
                decay_here,
            )
        )
    return (*results, loss_sum, token_count, grad_norm)


def solution(mesh):
    in_specs = (
        (P("dp", None), P("dp"), P("dp", None))
        + (P(None, "dp", None, "tensor"),) * 3
        + (P(None, "tensor", "dp"),) * 3
        + (P(None, "dp", "tensor"),) * 3
        + (P(None, "tensor", "dp"),) * 3
        + (P("dp", None),) * 3
        + (P("dp", "tensor"),) * 3
        + (P(None, None, "dp"),) * 3
    )
    return jax.shard_map(
        functools.partial(body, mesh.shape["dp"], mesh.shape["tensor"]),
        mesh=mesh,
        in_specs=in_specs,
        out_specs=in_specs[3:] + (P(), P(), P()),
        check_vma=False,
    )
```

```python
import functools

import jax
import jax.numpy as jnp
from jax import lax
from jax.experimental import pallas as pl
from jax.experimental.pallas import tpu as pltpu
from jax.sharding import PartitionSpec as P

HEADS = 16
CODES = 1024
CLASSES = 1000
LAYERS = 2
STEP = 10
SEQ = 257
ROWS_UP = 16

beta_one = 0.9
beta_two = 0.96
matrix_rate = 0.02
embed_rate = 0.5
vector_rate = 0.25
weight_decay = 0.045
epsilon = 1e-10
clip_limit = 0.02
norm_epsilon = 1e-06
low = jnp.bfloat16
full = jnp.float32


def matmul(left, right):
    return jnp.dot(left, right, preferred_element_type=full)


def matmul_left(left, right):
    return lax.dot_general(left, right, (((0,), (0,)), ((), ())), preferred_element_type=full)


def matmul_right(left, right):
    return lax.dot_general(left, right, (((1,), (1,)), ((), ())), preferred_element_type=full)


def layer_norm(stream, scaling, offset):
    average = jnp.mean(stream, axis=-1, keepdims=True)
    centred = stream - average
    variance = jnp.mean(centred * centred, axis=-1, keepdims=True)
    return centred * lax.rsqrt(variance + norm_epsilon) * scaling + offset


def norm_back(stream, scaling, offset, gradient):
    normed_out, pull = jax.vjp(layer_norm, stream, scaling, offset)
    return pull(gradient)


def gelu_exact(values):
    return jax.nn.gelu(values, approximate=False)


def branch_total(piece_sum):
    return lax.psum(piece_sum.astype(jnp.bfloat16), "tensor").astype(jnp.float32)


def input_total(piece_sum):
    return lax.psum(piece_sum.astype(jnp.bfloat16), "tensor").astype(jnp.float32)


def split_heads(joined, images, head_count):
    head_width = joined.shape[1] // (3 * head_count)
    sections = joined.reshape(images, SEQ, 3, head_count, head_width)
    return (sections[:, :, 0], sections[:, :, 1], sections[:, :, 2], head_width ** (-0.5))


def attend_forward(joined, images, head_count):
    queries, key_rows, values, score_scale = split_heads(joined, images, head_count)
    scores = (
        jnp.einsum("bqhd,bkhd->bhqk", queries, key_rows, preferred_element_type=jnp.float32)
        * score_scale
    )
    peak_value = jnp.max(scores, axis=-1, keepdims=True)
    log_total = peak_value + jnp.log(jnp.sum(jnp.exp(scores - peak_value), axis=-1, keepdims=True))
    attention = jnp.exp(scores - log_total).astype(jnp.bfloat16)
    blended = jnp.einsum("bhqk,bkhd->bqhd", attention, values, preferred_element_type=jnp.float32)
    return (blended.astype(jnp.bfloat16).reshape(joined.shape[0], -1), log_total)


def attend_backward(joined, log_total, grad_blended, images, head_count):
    queries, key_rows, values, score_scale = split_heads(joined, images, head_count)
    scores = (
        jnp.einsum("bqhd,bkhd->bhqk", queries, key_rows, preferred_element_type=jnp.float32)
        * score_scale
    )
    attention = jnp.exp(scores - log_total)
    grad_out = grad_blended.reshape(queries.shape)
    grad_attention = jnp.einsum(
        "bqhd,bkhd->bhqk", grad_out, values, preferred_element_type=jnp.float32
    )
    row_total = jnp.sum(attention * grad_attention, axis=-1, keepdims=True)
    grad_scores = (attention * (grad_attention - row_total)).astype(jnp.bfloat16)
    grad_queries = (
        jnp.einsum("bhqk,bkhd->bqhd", grad_scores, key_rows, preferred_element_type=jnp.float32)
        * score_scale
    )
    grad_keys = (
        jnp.einsum("bhqk,bqhd->bkhd", grad_scores, queries, preferred_element_type=jnp.float32)
        * score_scale
    )
    grad_values = jnp.einsum(
        "bhqk,bqhd->bkhd",
        attention.astype(jnp.bfloat16),
        grad_out,
        preferred_element_type=jnp.float32,
    )
    stacked = jnp.stack([grad_queries, grad_keys, grad_values], axis=2).astype(jnp.bfloat16)
    return stacked.reshape(joined.shape)


def layer_forward(stream, weights, gains, images, head_count):
    w_in, w_out, w_expand, w_contract = weights
    normed = layer_norm(stream, gains[0, 0], gains[0, 1]).astype(jnp.bfloat16)
    joined = matmul(normed, w_in.reshape(w_in.shape[0], -1)).astype(jnp.bfloat16)
    blended, log_total = attend_forward(joined, images, head_count)
    middle = stream + branch_total(matmul(blended, w_out))
    normed_two = layer_norm(middle, gains[1, 0], gains[1, 1]).astype(jnp.bfloat16)
    hidden = matmul(normed_two, w_expand)
    active = gelu_exact(hidden).astype(jnp.bfloat16)
    result = middle + branch_total(matmul(active, w_contract))
    return (
        result,
        (stream, normed, joined, blended, log_total, middle, normed_two, hidden, active),
    )


def layer_backward(gradient, saved, weights, gains, images, head_count):
    w_in, w_out, w_expand, w_contract = weights
    stream, normed, joined, blended, log_total, middle, normed_two, hidden, active = saved
    grad_low = gradient.astype(jnp.bfloat16)
    g_contract = matmul_left(active, grad_low)
    grad_active = matmul_right(grad_low, w_contract)
    gelu_out, gelu_pull = jax.vjp(gelu_exact, hidden)
    grad_hidden = gelu_pull(grad_active)[0].astype(jnp.bfloat16)
    g_expand = matmul_left(normed_two, grad_hidden)
    grad_normed = input_total(matmul_right(grad_hidden, w_expand))
    grad_mid, scale_two, offset_two = norm_back(middle, gains[1, 0], gains[1, 1], grad_normed)
    gradient = gradient + grad_mid
    grad_low = gradient.astype(jnp.bfloat16)
    g_out = matmul_left(blended, grad_low)
    grad_blended = matmul_right(grad_low, w_out).astype(jnp.bfloat16)
    grad_joined = attend_backward(joined, log_total, grad_blended, images, head_count)
    g_in = matmul_left(normed, grad_joined).reshape(w_in.shape)
    grad_normed = input_total(matmul_right(grad_joined, w_in.reshape(w_in.shape[0], -1)))
    grad_first, scale_one, offset_one = norm_back(stream, gains[0, 0], gains[0, 1], grad_normed)
    norm_grads = jnp.stack([jnp.stack([scale_one, offset_one]), jnp.stack([scale_two, offset_two])])
    return (gradient + grad_first, (g_in, g_out, g_expand, g_contract), norm_grads)


def plain_body(
    image_codes,
    labels,
    mask_flags,
    attend_in,
    attend_in_one,
    attend_in_two,
    attend_out,
    attend_out_one,
    attend_out_two,
    expand,
    expand_one,
    expand_two,
    contract,
    contract_one,
    contract_two,
    embed_table,
    embed_one,
    embed_two,
    logit_table,
    logit_one,
    logit_two,
    norm_params,
    norm_one,
    norm_two,
):
    w_in, w_out, w_expand, w_contract, embed_rows, head_table, gains_low = (
        lax.all_gather(attend_in.astype(jnp.bfloat16), "dp", axis=1, tiled=True),
        lax.all_gather(attend_out.astype(jnp.bfloat16), "dp", axis=2, tiled=True),
        lax.all_gather(expand.astype(jnp.bfloat16), "dp", axis=1, tiled=True),
        lax.all_gather(contract.astype(jnp.bfloat16), "dp", axis=2, tiled=True),
        lax.all_gather(embed_table.astype(jnp.bfloat16), "dp", axis=0, tiled=True),
        lax.all_gather(logit_table.astype(jnp.bfloat16), "dp", axis=0, tiled=True),
        lax.all_gather(norm_params.astype(jnp.bfloat16), "dp", axis=2, tiled=True),
    )
    gains = gains_low.astype(jnp.float32)
    images = labels.shape[0]
    head_count = HEADS // lax.axis_size("tensor")
    code_rows = jnp.where(mask_flags == 1, CODES, image_codes)
    row_index = jnp.concatenate([(CODES + 1 + labels)[:, None], code_rows], axis=1).reshape(-1)
    place_rows = jnp.tile(CODES + 1 + CLASSES + jnp.arange(SEQ), images)
    targets = jnp.concatenate([jnp.zeros((images, 1), jnp.int32), image_codes], axis=1).reshape(-1)
    weights_loss = jnp.concatenate(
        [jnp.zeros((images, 1), jnp.float32), mask_flags.astype(jnp.float32)], axis=1
    ).reshape(-1)
    stream = embed_rows[row_index].astype(jnp.float32) + embed_rows[place_rows].astype(jnp.float32)
    saved_all = []
    for layer_index in range(LAYERS):
        weights = (
            w_in[layer_index],
            w_out[layer_index],
            w_expand[layer_index],
            w_contract[layer_index],
        )
        stream, saved = layer_forward(
            stream, weights, gains[2 * layer_index : 2 * layer_index + 2], images, head_count
        )
        saved_all.append(saved)
    final_gain = gains[2 * LAYERS]
    final = layer_norm(stream, final_gain[0], final_gain[1]).astype(jnp.bfloat16)
    logits = matmul(final, head_table)
    local_codes = logits.shape[1]
    col_start = lax.axis_index("tensor") * local_codes
    is_target = (
        targets[:, None] == col_start + jnp.arange(local_codes, dtype=jnp.int32)[None, :]
    ).astype(jnp.float32)
    peak_value = jnp.max(logits, axis=1)
    exp_total = jnp.sum(jnp.exp(logits - peak_value[:, None]), axis=1)
    picked = jnp.sum(is_target * logits, axis=1)
    peak_all = lax.pmax(peak_value, "tensor")
    exp_all, picked_all = lax.psum((exp_total * jnp.exp(peak_value - peak_all), picked), "tensor")
    log_total = peak_all + jnp.log(exp_all)
    loss_terms = (log_total - picked_all) * weights_loss
    loss_sum, token_count = lax.psum((jnp.sum(loss_terms), jnp.sum(weights_loss)), "dp")
    grad_logits = (
        (jnp.exp(logits - log_total[:, None]) - is_target) * (weights_loss / token_count)[:, None]
    ).astype(jnp.bfloat16)
    g_head = matmul_left(final, grad_logits)
    grad_final = input_total(matmul_right(grad_logits, head_table))
    gradient, final_scale, final_offset = norm_back(
        stream, final_gain[0], final_gain[1], grad_final
    )
    layer_grads = [None] * LAYERS
    norm_grads = [None] * LAYERS
    for layer_index in reversed(range(LAYERS)):
        weights = (
            w_in[layer_index],
            w_out[layer_index],
            w_expand[layer_index],
            w_contract[layer_index],
        )
        gradient, found, gain_grads = layer_backward(
            gradient,
            saved_all[layer_index],
            weights,
            gains[2 * layer_index : 2 * layer_index + 2],
            images,
            head_count,
        )
        layer_grads[layer_index] = found
        norm_grads[layer_index] = gain_grads
    g_norms = jnp.concatenate(
        [
            jnp.stack(norm_grads).reshape(2 * LAYERS, 2, -1),
            jnp.stack([final_scale, final_offset])[None],
        ],
        axis=0,
    )
    g_table = jax.ops.segment_sum(
        jnp.concatenate([gradient, gradient], axis=0),
        jnp.concatenate([row_index, place_rows]),
        num_segments=embed_rows.shape[0],
    )
    g_in_all = jnp.stack([found[0] for found in layer_grads])
    g_out_all = jnp.stack([found[1] for found in layer_grads])
    g_expand_all = jnp.stack([found[2] for found in layer_grads])
    g_contract_all = jnp.stack([found[3] for found in layer_grads])
    g_in_all, g_out_all, g_expand_all, g_contract_all, g_table, g_head, g_norms = (
        lax.psum_scatter(g_in_all, "dp", scatter_dimension=1, tiled=True),
        lax.psum_scatter(g_out_all, "dp", scatter_dimension=2, tiled=True),
        lax.psum_scatter(g_expand_all, "dp", scatter_dimension=1, tiled=True),
        lax.psum_scatter(g_contract_all, "dp", scatter_dimension=2, tiled=True),
        lax.psum_scatter(g_table, "dp", scatter_dimension=0, tiled=True),
        lax.psum_scatter(g_head, "dp", scatter_dimension=0, tiled=True),
        lax.psum_scatter(g_norms, "dp", scatter_dimension=2, tiled=True),
    )
    gradients = (g_in_all, g_out_all, g_expand_all, g_contract_all, g_table, g_head, g_norms)
    first_rank = (lax.axis_index("tensor") == 0).astype(jnp.float32)
    split_squares = (
        jnp.sum(g_in_all * g_in_all)
        + jnp.sum(g_out_all * g_out_all)
        + jnp.sum(g_expand_all * g_expand_all)
        + jnp.sum(g_contract_all * g_contract_all)
        + jnp.sum(g_head * g_head)
    )
    shared_squares = jnp.sum(g_table * g_table) + jnp.sum(g_norms * g_norms)
    grad_norm = jnp.sqrt(lax.psum(split_squares + first_rank * shared_squares, ("dp", "tensor")))
    factor = clip_limit / jnp.maximum(grad_norm, clip_limit)
    params = (attend_in, attend_out, expand, contract, embed_table, logit_table, norm_params)
    moments_one = (
        attend_in_one,
        attend_out_one,
        expand_one,
        contract_one,
        embed_one,
        logit_one,
        norm_one,
    )
    moments_two = (
        attend_in_two,
        attend_out_two,
        expand_two,
        contract_two,
        embed_two,
        logit_two,
        norm_two,
    )
    results = []
    for index in range(7):
        rate_here = vector_rate if index == 6 else embed_rate if index == 4 else matrix_rate
        decay_here = 0.0 if index == 6 else weight_decay
        results.extend(
            adam_step(
                params[index],
                moments_one[index],
                moments_two[index],
                gradients[index],
                factor,
                rate_here,
                decay_here,
            )
        )
    return (
        results[0],
        results[1],
        results[2],
        results[3],
        results[4],
        results[5],
        results[6],
        results[7],
        results[8],
        results[9],
        results[10],
        results[11],
        results[12],
        results[13],
        results[14],
        results[15],
        results[16],
        results[17],
        results[18],
        results[19],
        results[20],
        loss_sum,
        token_count,
        grad_norm,
    )


MESH = pl.DeviceIdType.MESH


def factors(dp, tensor):
    return [("tensor", tensor // 2, 2), ("tensor", 2, 1), ("dp", dp // 2, 2), ("dp", 2, 1)]


OUTER, PAIR, LONG, NEAR = range(4)
ORDERS = {
    "a": (LONG, NEAR, OUTER, PAIR),
    "b": (LONG, OUTER, NEAR, PAIR),
    "d": (OUTER, LONG, NEAR, PAIR),
    "e": (NEAR, LONG, OUTER, PAIR),
}


def place_of(dims):
    return [(lax.axis_index(axis) // stride) % size for axis, size, stride in dims]


def peer_of(dims, here, dim, move):
    there = list(here)
    there[dim] = lax.rem(here[dim] + move, dims[dim][1])
    found = {"dp": 0, "tensor": 0}
    for (axis, size, stride), at in zip(dims, there):
        found[axis] = found[axis] + at * stride
    return (found["dp"], found["tensor"])


def greet(dims, here):
    barrier = pltpu.get_barrier_semaphore()
    count = 0
    for dim, (axis, size, stride) in enumerate(dims):
        for move in range(1, size):
            pl.semaphore_signal(
                barrier, inc=1, device_id=peer_of(dims, here, dim, move), device_id_type=MESH
            )
            count += 1
    pl.semaphore_wait(barrier, count)


def gather_units(rows):
    tiles = rows // 16
    if rows % 16 or tiles < 4:
        return [[(0, rows, "a")]]
    if tiles == 6:
        cuts = [[("a", 1), ("b", 1), ("d", 1)], [("a", 1), ("b", 1), ("e", 1)]]
    else:
        cuts = [[("a", 1), ("b", 1)], [("a", 1), ("b", 1), ("d", tiles - 4)]]
    units, row = [], 0
    for cut in cuts:
        unit = []
        for order, count in cut:
            unit.append((row, 16 * count, order))
            row += 16 * count
        units.append(unit)
    return units


def gather_kernel(dims, shapes, *refs):
    count = len(shapes)
    pieces, wholes, (send, recv, own) = refs[:count], refs[count : 2 * count], refs[2 * count :]
    here = place_of(dims)
    greet(dims, here)
    copies_own = [
        pltpu.make_async_copy(pieces[at], wholes[at].at[tuple(here)], own.at[at]) for at in range(count)
    ]
    for copy in copies_own:
        copy.start()
    slot, units = 0, []
    for chunk, (rows, width) in enumerate(shapes):
        for unit in gather_units(rows):
            stages = [[], [], [], []]
            for row, size, order in unit:
                span = (pl.ds(row, size),) if size != rows else ()
                for stage, dim in enumerate(ORDERS[order]):
                    done = ORDERS[order][:stage]
                    block = wholes[chunk].at[
                        tuple(slice(None) if at in done else here[at] for at in range(4)) + span
                    ]
                    source = block
                    if stage == 0:
                        source = pieces[chunk].at[span] if span else pieces[chunk]
                    for move in range(1, dims[dim][1]):
                        stages[stage].append(
                            pltpu.make_async_remote_copy(
                                src_ref=source,
                                dst_ref=block,
                                send_sem=send.at[slot],
                                recv_sem=recv.at[slot],
                                device_id=peer_of(dims, here, dim, move),
                                device_id_type=MESH,
                            )
                        )
                        slot += 1
            units.append((chunk, stages))
    ready = set()
    for tick in range(len(units) + 8):
        for at, (chunk, stages) in enumerate(units):
            if (tick - at) % 2 or not 0 <= tick - at <= 8:
                continue
            stage = (tick - at) // 2
            if stage:
                for copy in stages[stage - 1]:
                    copy.wait_recv()
            if stage == 1 and chunk not in ready:
                copies_own[chunk].wait()
                ready.add(chunk)
            if stage < 4:
                for copy in stages[stage]:
                    copy.start()
    for chunk, stages in units:
        for stage in stages:
            for copy in stage:
                copy.wait_send()


def gather_all(dims, pieces):
    shapes = [piece.shape for piece in pieces]
    sizes = [size for axis, size, stride in dims]
    slots = sum(sum(size - 1 for size in sizes) * len(u) for r, w in shapes for u in gather_units(r))
    wholes = pl.pallas_call(
        functools.partial(gather_kernel, dims, shapes),
        out_shape=[jax.ShapeDtypeStruct((*sizes, *shape), low) for shape in shapes],
        in_specs=[pl.BlockSpec(memory_space=pl.ANY)] * len(shapes),
        out_specs=[pl.BlockSpec(memory_space=pl.ANY)] * len(shapes),
        scratch_shapes=[
            pltpu.SemaphoreType.DMA((slots,)),
            pltpu.SemaphoreType.DMA((slots,)),
            pltpu.SemaphoreType.DMA((len(shapes),)),
        ],
        compiler_params=pltpu.CompilerParams(collective_id=0, has_side_effects=True),
    )(*pieces)
    return wholes


def adam_step(weight, moment_one, moment_two, gradient, factor, rate_here, decay_here):
    gradient = gradient * factor
    moment_one = beta_one * moment_one + (1.0 - beta_one) * gradient
    moment_two = beta_two * moment_two + (1.0 - beta_two) * gradient * gradient
    correct_one = 1.0 - beta_one**STEP
    correct_two = 1.0 - beta_two**STEP
    weight = weight - rate_here * (
        moment_one / correct_one / (jnp.sqrt(moment_two / correct_two) + epsilon)
        + decay_here * weight
    )
    return [weight, moment_one, moment_two]


TOKENS = -(-SEQ // 16) * 16


class Refs:
    pass


class Parts:
    def __init__(self):
        self.ins, self.outs, self.scratch = [], [], []

    def put(self, near=False, key=None, **named):
        for name, value in named.items():
            space = pltpu.VMEM if near else pl.ANY
            self.ins.append(((name, key), value, pl.BlockSpec(memory_space=space)))

    def out(self, kind, near=False, key=None, **named):
        for name, shape in named.items():
            space = pltpu.VMEM if near else pl.ANY
            self.outs.append(
                ((name, key), jax.ShapeDtypeStruct(shape, kind), pl.BlockSpec(memory_space=space))
            )

    def keep(self, key=None, **named):
        for name, scratch in named.items():
            self.scratch.append(((name, key), scratch))

    def refs(self, refs):
        found = Refs()
        for ((name, key), *rest), ref in zip(self.ins + self.outs + self.scratch, refs):
            if key is None:
                setattr(found, name, ref)
            else:
                found.__dict__.setdefault(name, {})[key] = ref
        return found

    def call(self, body, barrier=None):
        found = pl.pallas_call(
            lambda *refs: body(self.refs(refs)),
            out_shape=[shape for name, shape, spec in self.outs],
            in_specs=[spec for name, value, spec in self.ins],
            out_specs=[spec for name, shape, spec in self.outs],
            scratch_shapes=[scratch for name, scratch in self.scratch],
            compiler_params=pltpu.CompilerParams(
                collective_id=barrier,
                has_side_effects=barrier is not None,
                vmem_limit_bytes=60 * 1024 * 1024,
            ),
        )(*[value for name, value, spec in self.ins])
        return self.refs([None] * len(self.ins) + list(found))


class Reducer:
    def __init__(self, dims, chunks, cuts):
        self.dims, self.chunks = dims, chunks
        self.sizes = [size for axis, size, stride in dims]
        self.units, self.sides, counts = [], set(), {}
        self.slots = 0
        for chunk, (name, rows, width, wide) in enumerate(chunks):
            for unit in cuts(rows, width):
                found = []
                for row, size, order in unit:
                    stages = []
                    for stage in range(4):
                        dim = ORDERS[order][3 - stage]
                        key = (order, stage, size, width, wide)
                        stages.append((dim, key, counts.get(key, 0), self.slots))
                        self.sides.add((key, len(self.units) % 2))
                        counts[key] = counts.get(key, 0) + 1
                        self.slots += self.sizes[dim] - 1
                    found.append((row, size, order, stages, len(self.units) % 2))
                self.units.append((chunk, found))
        self.counts = counts
        self.started, self.busy = {}, {}

    def room(self, key):
        order, stage, size, width, wide = key
        gone = [ORDERS[order][3 - at] for at in range(stage + 1)]
        rest = tuple(self.sizes[dim] for dim in range(4) if dim not in gone)
        return (self.sizes[gone[-1]] - 1, *rest, size, width)

    def declare(self, parts):
        for key, count in self.counts.items():
            order, stage, size, width, wide = key
            kind = full if wide and stage == 3 else low
            parts.out(kind, key=key, came=(count, *self.room(key)))
            parts.keep(key=key, staged=pltpu.VMEM(self.room(key), kind), staged_sem=pltpu.SemaphoreType.DMA)
            for side in range(2):
                if stage == 2 and wide and (key, side) in self.sides:
                    parts.keep(key=(key, side), exact=pltpu.VMEM(self.room(key)[1:], full))
        parts.keep(
            send=pltpu.SemaphoreType.DMA((self.slots,)),
            recv=pltpu.SemaphoreType.DMA((self.slots,)),
            squares=pltpu.VMEM((8, 128), full),
        )

    def bind(self, refs, here, blocks, results):
        self.refs, self.here, self.blocks, self.results = refs, here, blocks, results
        refs.squares[...] = jnp.zeros_like(refs.squares)

    def turn(self, dim, move):
        return lax.rem(self.here[dim] + move, self.sizes[dim]) if move else self.here[dim]

    def block(self, chunk, part, stage, move):
        row, size, order, stages, side = part
        gone = [ORDERS[order][3 - at] for at in range(stage)]
        dim = ORDERS[order][3 - stage]
        spot = [
            self.turn(at, move) if at == dim else (self.here[at] if at in gone else slice(None))
            for at in range(4)
        ]
        return self.blocks[chunk].at[(*spot, pl.ds(row, size))]

    def exact(self, part, stage, move):
        row, size, order, stages, side = part
        left = sorted(ORDERS[order][: 4 - stage])
        dim = ORDERS[order][3 - stage]
        spot = [self.turn(at, move) if at == dim else slice(None) for at in left]
        return self.refs.exact[(stages[stage - 1][1], side)].at[tuple(spot)]

    def copies(self, chunk, part, stage):
        dim, key, count, slot = part[3][stage]
        wide = key[4] and stage == 3
        return [
            pltpu.make_async_remote_copy(
                src_ref=self.exact(part, stage, move) if wide else self.block(chunk, part, stage, move),
                dst_ref=self.refs.came[key].at[count, move - 1],
                send_sem=self.refs.send.at[slot + move - 1],
                recv_sem=self.refs.recv.at[slot + move - 1],
                device_id=peer_of(self.dims, self.here, dim, move),
                device_id_type=MESH,
            )
            for move in range(1, self.sizes[dim])
        ]

    def staged(self, part, stage):
        dim, key, count, slot = part[3][stage]
        return pltpu.make_async_copy(
            self.refs.came[key].at[count], self.refs.staged[key], self.refs.staged_sem[key]
        )

    def add(self, chunk, part, stage):
        row, size, order, stages, side = part
        dim, key, count, slot = stages[stage]
        held, came = self.block(chunk, part, stage, 0), self.refs.staged[key]
        if stage == 0:
            total = held[...]
            for move in range(self.sizes[dim] - 1):
                total = total + came[move]
            held[...] = total
            return
        exact = stage == 3 and key[4]
        total = (self.exact(part, stage, 0) if exact else held)[...].astype(full)
        for move in range(self.sizes[dim] - 1):
            total = total + came[move].astype(full)
        if stage < 3 and not (stage == 2 and key[4]):
            held[...] = total.astype(low)
            return
        if stage == 2:
            for copy in self.busy.pop((key, side), []):
                copy.wait_send()
            self.refs.exact[(key, side)][...] = total
            return
        self.results[chunk][pl.ds(row, size), :] = total
        square = total * total
        square = sum(square[at : at + 8] for at in range(0, size, 8))
        self.refs.squares[...] += sum(square[:, at : at + 128] for at in range(0, square.shape[1], 128))

    def tick(self, now):
        work = [
            (at, (now - at) // 2)
            for at in range(len(self.units))
            if (now - at) % 2 == 0 and 0 <= now - at <= 8
        ]
        for at, stage in work:
            chunk, found = self.units[at]
            if stage:
                for part in found:
                    for copy in self.copies(chunk, part, stage - 1):
                        copy.wait_recv()
                    self.staged(part, stage - 1).start()
        for at, stage in work:
            chunk, found = self.units[at]
            for part in found:
                if stage:
                    self.staged(part, stage - 1).wait()
                    self.add(chunk, part, stage - 1)
                if stage < 4:
                    dim, key, count, slot = part[3][stage]
                    copies = self.copies(chunk, part, stage)
                    for copy in copies:
                        copy.start()
                    if key[4] and stage == 3:
                        self.busy[(part[3][2][1], part[4])] = copies
                    else:
                        self.started.setdefault(chunk, []).extend(copies)

    def ticks(self):
        return len(self.units) + 8

    def finish(self):
        for chunk in list(self.started):
            self.release(chunk)
        for copy in sum(self.busy.values(), []):
            copy.wait_send()

    def release(self, chunk):
        for copy in self.started.pop(chunk):
            copy.wait_send()


def reduce_cuts(rows, width):
    tiles = rows // 16
    if tiles == 6 and width > 256:
        cuts = [[("a", 1), ("b", 1), ("d", 1)], [("a", 1), ("b", 1), ("e", 1)]]
    elif tiles == 6:
        cuts = [[("a", 3), ("b", 3)]]
    else:
        cuts = [[("a", 1), ("b", 1)], [("a", 1), ("b", 1), ("d", tiles - 4)]]
    units, row = [], 0
    for cut in cuts:
        unit = []
        for order, count in cut:
            unit.append((row, 16 * count, order))
            row += 16 * count
        units.append(unit)
    return units


def norm_back_rows(grad, grad_normed, source, gain, found, row):
    scaling = gain[...]

    def step(at, totals):
        rows = pl.ds(pl.multiple_of(at * 16, 16), 16)
        value, up = source[rows, :], grad_normed[rows, :]
        centred = value - jnp.mean(value, axis=-1, keepdims=True)
        spread = lax.rsqrt(jnp.mean(centred * centred, axis=-1, keepdims=True) + norm_epsilon)
        unit = centred * spread
        inner = up * scaling
        pulled = spread * (
            inner
            - jnp.mean(inner, axis=-1, keepdims=True)
            - unit * jnp.mean(inner * unit, axis=-1, keepdims=True)
        )
        grad[rows, :] = grad[rows, :] + pulled
        return totals[0] + up * unit, totals[1] + up

    zero = jnp.zeros((16, source.shape[1]), full)
    total = lax.fori_loop(0, source.shape[0] // 16, step, (zero, zero))
    found[pl.ds(row, 1), :] = jnp.sum(total[0], axis=0, keepdims=True)
    found[pl.ds(row + 1, 1), :] = jnp.sum(total[1], axis=0, keepdims=True)


def square_block(value):
    return value.reshape(-1, value.shape[-1])


HEAD, ATTEND, EXPAND, CONTRACT, TABLE = range(5)
SAVED = ((0, 1), (2, 3))


def backward_kernel(dims, reducer, layers, share, heads, width, norms, refs):
    here = place_of(dims)
    sizes = reducer.sizes
    sides = (sizes[2], sizes[3])
    names = [name for name, rows, across, wide in reducer.chunks]
    spots = sizes[0] * sizes[1]
    part = heads * width

    weights = {
        name: pltpu.make_async_copy(refs.weight[name], refs.slots.at[at], refs.weight_sem.at[at])
        for at, name in enumerate(names[1:-1])
    }
    mlp = (refs.slope, refs.active, refs.normed_two, refs.middle)
    mlp_near = (refs.near_slope, refs.near_active, refs.near_normed_two, refs.near_middle)
    attend = (refs.joined, refs.blended, refs.normed, refs.stream)
    attend_near = (refs.near_joined, refs.near_blended, refs.near_normed, refs.near_stream)

    def fetches(far, near, sem, layer):
        return [
            pltpu.make_async_copy(
                source[(layer, spot)], target.at[spot] if at < 2 else target, sem.at[at * spots + spot]
            )
            for at, (source, target) in enumerate(zip(far, near))
            for spot in range(spots if at < 2 else 1)
        ]

    def mlp_fetches(layer):
        return fetches(mlp, mlp_near, refs.mlp_sem, layer)

    def attend_fetches(layer):
        return fetches(attend, attend_near, refs.attend_sem, layer)

    order = names[1:-1]
    for copy in mlp_fetches(layers - 1):
        copy.start()
    for name in order[:2]:
        weights[name].start()
    for copy in attend_fetches(layers - 1):
        copy.start()
    for name in order[2:]:
        weights[name].start()
    greet(dims, here)

    lines = refs.total[(TABLE, 0)].shape[0]
    table_blocks = refs.slots.at[0, :, :, :, :, pl.ds(0, lines)]
    blocks = [refs.head_blocks] + [refs.slots.at[at] for at in range(len(order))] + [table_blocks]
    reducer.bind(refs, here, blocks, [refs.total[name] for name in names])
    clock = [0]

    def run(count):
        for _ in range(count):
            reducer.tick(clock[0])
            clock[0] += 1

    per_chunk = [0] * len(names)
    for chunk, found in reducer.units:
        per_chunk[chunk] += 1
    grad, grad_normed, norm_grads = refs.grad, refs.grad_normed, refs.norm_grads
    gains = refs.gains

    norm_grads[...] = jnp.zeros_like(norm_grads)
    norm_grads[pl.ds(4 * layers, 2), :] = refs.final_grads[...]
    grad[...] = refs.grad_top[...]
    turned = refs.final[...].T
    for spot in range(spots):
        across = refs.grad_logits.shape[1] // spots
        found = matmul(turned, refs.grad_logits[:, spot * across : (spot + 1) * across])
        refs.head_blocks[spot // sizes[1], spot % sizes[1]] = found.astype(low).reshape(*sides, -1, across)
    run(per_chunk[0])

    for layer in reversed(range(layers)):
        at_contract, at_expand, at_attend = [names.index((kind, layer)) for kind in (CONTRACT, EXPAND, ATTEND)]
        slot_contract, slot_expand, slot_attend = [
            refs.slots.at[at - 1] for at in (at_contract, at_expand, at_attend)
        ]

        for copy in mlp_fetches(layer):
            copy.wait()
        weights[(CONTRACT, layer)].wait()
        refs.grad_low[...] = grad[...].astype(low)
        refs.turned[...] = grad[...].astype(low).T

        def contract_step(spot, carry):
            outer, pair = spot // sizes[1], spot % sizes[1]
            held = square_block(slot_contract[outer, pair])
            pulled = matmul(refs.grad_low[...], held) * refs.near_slope[spot]
            refs.grad_hidden[spot] = pulled.astype(low)
            found = matmul(refs.turned[...], refs.near_active[spot]).astype(low)
            slot_contract[outer, pair] = found.reshape(*sides, -1, found.shape[-1])
            return carry

        lax.fori_loop(0, spots, contract_step, 0)
        run(per_chunk[at_contract])

        weights[(EXPAND, layer)].wait()
        refs.turned[...] = refs.near_normed_two[...].T
        grad_normed[...] = jnp.zeros_like(grad_normed)

        def expand_step(spot, carry):
            outer, pair = spot // sizes[1], spot % sizes[1]
            held = square_block(slot_expand[outer, pair])
            pulled = refs.grad_hidden[spot]
            grad_normed[...] += matmul_right(pulled, held)
            found = matmul(refs.turned[...], pulled).astype(low)
            slot_expand[outer, pair] = found.reshape(*sides, -1, found.shape[-1])
            return carry

        lax.fori_loop(0, spots, expand_step, 0)
        run(per_chunk[at_expand])
        norm_back_rows(
            grad, grad_normed, refs.near_middle, gains.at[pl.ds(4 * layer + 2, 1)], norm_grads, 4 * layer + 2
        )
        if layer:
            for copy in mlp_fetches(layer - 1):
                copy.start()

        for copy in attend_fetches(layer):
            copy.wait()
        weights[(ATTEND, layer)].wait()
        refs.grad_low[...] = grad[...].astype(low)
        refs.turned[...] = grad[...].astype(low).T
        refs.turned_two[...] = refs.near_normed[...].T
        grad_normed[...] = jnp.zeros_like(grad_normed)
        known = lax.broadcasted_iota(jnp.int32, (1, TOKENS), 1) < SEQ
        scale = width ** (-0.5)

        def attend_step(spot, carry):
            outer, pair = spot // sizes[1], spot % sizes[1]
            held = square_block(slot_attend[outer, pair])
            up_all = matmul(refs.grad_low[...], held[:, 3 * part :]).astype(low)
            pulled_all = []
            joined = refs.near_joined[spot]
            parts = [[], [], []]
            for head in range(heads):
                query, key, value = [
                    joined[:, (at * heads + head) * width : (at * heads + head + 1) * width] for at in range(3)
                ]
                up = up_all[:, head * width : (head + 1) * width]
                scores = jnp.where(known, matmul_right(query, key) * scale, -1e30)
                top = jnp.max(scores, axis=-1, keepdims=True)
                probs = jnp.exp(scores - top)
                probs = probs * (1.0 / jnp.sum(probs, axis=-1, keepdims=True))
                pulled = matmul_right(up, value)
                total = jnp.sum(probs * pulled, axis=-1, keepdims=True)
                moved = (probs * (pulled - total)).astype(low)
                parts[0].append((matmul(moved, key) * scale).astype(low))
                parts[1].append((matmul_left(moved, query) * scale).astype(low))
                parts[2].append(matmul_left(probs.astype(low), up).astype(low))
            pulled = jnp.concatenate(parts[0] + parts[1] + parts[2], axis=1)
            grad_normed[...] += matmul_right(pulled, held[:, : 3 * part])
            found = jnp.concatenate(
                [
                    matmul(refs.turned_two[...], pulled).astype(low),
                    matmul(refs.turned[...], refs.near_blended[spot]).astype(low),
                ],
                axis=1,
            )
            slot_attend[outer, pair] = found.reshape(*sides, -1, found.shape[-1])
            return carry

        lax.fori_loop(0, spots, attend_step, 0)
        run(per_chunk[at_attend])
        norm_back_rows(grad, grad_normed, refs.near_stream, gains.at[pl.ds(4 * layer, 1)], norm_grads, 4 * layer)
        if layer:
            for copy in attend_fetches(layer - 1):
                copy.start()

    upper = grad[...].astype(low)
    lower = (grad[...] - upper.astype(full)).astype(low)
    model = grad.shape[1]
    depth = refs.slots.shape[5]
    reducer.release(1)

    def table_step(block, carry):
        outer, pair = block // (sizes[1] * sizes[2] * sizes[3]), (block // (sizes[2] * sizes[3])) % sizes[1]
        far, near = (block // sizes[3]) % sizes[2], block % sizes[3]
        row = block * lines + lax.broadcasted_iota(jnp.int32, (lines, TOKENS), 0)
        picks = (row == refs.rows[0:1, :]).astype(full) + (row == refs.rows[1:2, :]).astype(full)
        picks = picks.astype(low)
        found = matmul(picks, upper) + matmul(picks, lower)
        table_blocks[outer, pair, far, near] = found.astype(low)
        return carry

    lax.fori_loop(0, spots * sizes[2] * sizes[3], table_step, 0)
    for far in range(sizes[2]):
        for near in range(sizes[3]):
            at = (far * sizes[3] + near) * depth
            lane = lax.broadcasted_iota(jnp.int32, (norms, 128), 1)
            cuts = []
            for kind in range(2):
                rows = jnp.concatenate(
                    [norm_grads[2 * norm + kind : 2 * norm + kind + 1, at : at + depth] for norm in range(norms)], axis=0
                )
                cuts.append(jnp.concatenate([rows, jnp.zeros((norms, 128 - depth), full)], axis=1))
            line = jnp.concatenate(
                cuts + [jnp.zeros((norms, model - 256), full)], axis=1
            )
            line = jnp.concatenate([line, jnp.zeros((lines - share - norms, line.shape[1]), full)], axis=0)
            base = share // 16 * 16
            old = table_blocks[0, 0, far, near, base:lines, :].astype(full)
            table_blocks[0, 0, far, near, base:lines, :] = jnp.concatenate(
                [old[: share - base], line], axis=0
            ).astype(low)
    run(reducer.ticks() - clock[0])
    finish_sums(dims, here, reducer, refs)
    reducer.finish()


def finish_sums(dims, here, reducer, refs):
    sizes = reducer.sizes
    own = pltpu.make_async_copy(refs.total[(TABLE, 0)], refs.spread.at[here[0], here[1]], refs.spread_own)
    own.start()
    refs.shared[0, :8] = refs.squares[...]
    refs.shared[0, 8:] = refs.loss[...]
    spread, slot, last = [], 0, []
    for step, dim in enumerate((OUTER, PAIR, NEAR, LONG)):
        copies = [
            pltpu.make_async_remote_copy(
                src_ref=refs.shared.at[step],
                dst_ref=refs.shared_came.at[step, move - 1],
                send_sem=refs.shared_send.at[step, move - 1],
                recv_sem=refs.shared_recv.at[step, move - 1],
                device_id=peer_of(dims, here, dim, move),
                device_id_type=MESH,
            )
            for move in range(1, sizes[dim])
        ]
        table = []
        if dim == OUTER:
            for move in range(1, sizes[dim]):
                target = refs.spread.at[here[0], here[1]]
                table.append((refs.total[(TABLE, 0)], target, move))
        if dim == PAIR:
            for move in range(1, sizes[dim]):
                table.append((refs.spread.at[:, here[1]], refs.spread.at[:, here[1]], move))
            own.wait()
            for copy in last:
                copy.wait_recv()
        if table:
            last = [
                pltpu.make_async_remote_copy(
                    src_ref=source,
                    dst_ref=target,
                    send_sem=refs.spread_send.at[slot + move],
                    recv_sem=refs.spread_recv.at[slot + move],
                    device_id=peer_of(dims, here, dim, move),
                    device_id_type=MESH,
                )
                for source, target, move in table
            ]
            slot += sizes[dim]
            spread += last
        for copy in copies + (last if table else []):
            copy.start()
        for copy in copies:
            copy.wait_recv()
        value = refs.shared[step]
        for move in range(1, sizes[dim]):
            value = value + refs.shared_came[step, move - 1]
        refs.shared[step + 1] = value
        spread += copies
    for copy in last:
        copy.wait_recv()
    refs.sums[...] = refs.shared[4]
    for copy in spread:
        copy.wait_send()


def backward_all(dims, layers, share, lines, norms, weights, saved, near, logit_width):
    sizes = tuple(size for axis, size, stride in dims)
    spots = sizes[0] * sizes[1]
    order = [(kind, layer) for layer in reversed(range(layers)) for kind in (CONTRACT, EXPAND, ATTEND)]
    depth, square = weights[order[0]].shape[-2:]
    model = depth * sizes[2] * sizes[3]
    chunks = [((HEAD, 0), depth, logit_width, False)]
    chunks += [(name, depth, square, name[0] == ATTEND) for name in order]
    chunks += [((TABLE, 0), lines, model, False)]
    reducer = Reducer(dims, chunks, reduce_cuts)
    parts = Parts()
    parts.put(True, **near)
    for name in order:
        parts.put(key=name, weight=weights[name])
    for name, values in saved.items():
        for key, value in values.items():
            parts.put(key=key, **{name: value})
    for name, height, across, wide in chunks:
        parts.out(full, True, key=name, total=(height, across))
    parts.out(full, True, spread=(sizes[0], sizes[1], lines, model), sums=(16, 128))
    reducer.declare(parts)
    largest = max(sizes)
    dma = pltpu.SemaphoreType.DMA
    parts.keep(
        slots=pltpu.VMEM((len(order), *sizes, depth, square), low),
        head_blocks=pltpu.VMEM((*sizes, depth, logit_width), low),
        weight_sem=dma((len(order),)),
        mlp_sem=dma((4 * spots,)),
        attend_sem=dma((4 * spots,)),
        grad=pltpu.VMEM((TOKENS, model), full),
        grad_normed=pltpu.VMEM((TOKENS, model), full),
        grad_low=pltpu.VMEM((TOKENS, model), low),
        turned=pltpu.VMEM((model, TOKENS), low),
        turned_two=pltpu.VMEM((model, TOKENS), low),
        grad_hidden=pltpu.VMEM((spots, TOKENS, square), low),
        norm_grads=pltpu.VMEM((16, model), full),
        shared=pltpu.VMEM((5, 16, 128), full),
        shared_came=pltpu.VMEM((4, largest, 16, 128), full),
        shared_send=dma((4, largest)),
        shared_recv=dma((4, largest)),
        spread_send=dma((2 * largest,)),
        spread_recv=dma((2 * largest,)),
        spread_own=dma,
    )
    for name, values in saved.items():
        value = values[(0, 0)]
        many = (spots,) if (0, 1) in values else ()
        parts.keep(**{"near_" + name: pltpu.VMEM((*many, *value.shape), value.dtype)})
    body = functools.partial(
        backward_kernel, dims, reducer, layers, share, HEADS // spots, model // HEADS, norms
    )
    return parts.call(body, 1)


def adam_kernel(layers, share, norms, part, refs):
    norm = jnp.sqrt(jnp.sum(refs.sums[:8]))
    factor = clip_limit / jnp.maximum(norm, clip_limit)
    refs.results[...] = jnp.concatenate(
        [jnp.full((8, 128), norm), jnp.full((8, 128), jnp.sum(refs.sums[8:]))], axis=0
    )

    def update(name, spot, gradient, rate_here, decay_here):
        found = adam_step(
            refs.weight[name][spot],
            refs.one[name][spot],
            refs.two[name][spot],
            gradient,
            factor,
            rate_here,
            decay_here,
        )
        for target, value in zip((refs.new_weight, refs.new_one, refs.new_two), found):
            target[name][spot] = value

    for layer in range(layers):
        attend = refs.total[(ATTEND, layer)]
        for at in range(3):
            update(0, (layer, at), attend[:, at * part : (at + 1) * part], matrix_rate, weight_decay)
        update(1, layer, attend[:, 3 * part :].T, matrix_rate, weight_decay)
        update(2, layer, refs.total[(EXPAND, layer)][...], matrix_rate, weight_decay)
        update(3, layer, refs.total[(CONTRACT, layer)][...], matrix_rate, weight_decay)
    for spot in range(refs.spread.shape[0]):
        update(4, pl.ds(spot * share, share), refs.spread[spot, :share], embed_rate, weight_decay)
    update(5, slice(None), refs.total[(HEAD, 0)][...], matrix_rate, weight_decay)
    depth = refs.weight[6].shape[2]
    for at in range(norms):
        line = refs.spread[0, share + at : share + at + 1]
        for kind in range(2):
            update(6, (at, pl.ds(kind, 1)), line[:, kind * 128 : kind * 128 + depth], vector_rate, 0.0)


def adam_all(layers, share, norms, found, params, moments_one, moments_two):
    parts = Parts()
    parts.put(True, sums=found.sums, spread=found.spread.reshape(-1, *found.spread.shape[2:]))
    for name, value in found.total.items():
        parts.put(True, key=name, total=value)
    for at in range(7):
        parts.put(True, key=at, weight=params[at], one=moments_one[at], two=moments_two[at])
        shape = params[at].shape
        parts.out(full, True, key=at, new_weight=shape, new_one=shape, new_two=shape)
    parts.out(full, True, results=(16, 128))
    return parts.call(functools.partial(adam_kernel, layers, share, norms, params[0].shape[3]))


def attend_heads_kernel(heads, width, *refs):
    count = len(refs) // 2
    scale = width ** (-0.5)
    known = lax.broadcasted_iota(jnp.int32, (1, TOKENS), 1) < SEQ
    real = lax.broadcasted_iota(jnp.int32, (TOKENS, 1), 0) < SEQ
    for joined, blended in zip(refs[:count], refs[count:]):
        for head in range(heads):
            at = head * width
            query = joined[:, at : at + width]
            key = joined[:, (heads * width + at) : (heads * width + at + width)]
            value = joined[:, (2 * heads * width + at) : (2 * heads * width + at + width)]
            scores = jnp.where(known, matmul_right(query, key) * scale, -1e30)
            top = jnp.max(scores, axis=-1, keepdims=True)
            weights = jnp.exp(scores - top)
            weights = weights * (1.0 / jnp.sum(weights, axis=-1, keepdims=True))
            out = jnp.where(real, matmul(weights.astype(low), value), 0.0)
            blended[:, at : at + width] = out.astype(low)


def attend_heads(joined, heads, width):
    rows = joined[0].shape[0]
    return pl.pallas_call(
        functools.partial(attend_heads_kernel, heads, width),
        out_shape=[jax.ShapeDtypeStruct((rows, heads * width), low) for _ in joined],
        in_specs=[pl.BlockSpec(memory_space=pltpu.VMEM)] * len(joined),
        out_specs=[pl.BlockSpec(memory_space=pltpu.VMEM)] * len(joined),
        compiler_params=pltpu.CompilerParams(vmem_limit_bytes=32 * 1024 * 1024),
        cost_estimate=pl.CostEstimate(
            flops=len(joined) * heads * rows * rows * width * 4,
            bytes_accessed=len(joined) * rows * heads * width * 8,
            transcendentals=len(joined) * heads * rows * rows,
        ),
    )(*joined)


def body(dp, tensor, *args):
    (image_codes, labels, mask_flags), state = args[:3], args[3:]
    params, moments_one, moments_two = state[0::3], state[1::3], state[2::3]
    attend_in, attend_out, expand, contract, embed_table, logit_table, norm_params = params
    dims = factors(dp, tensor)
    sizes = tuple(size for axis, size, stride in dims)
    spots = list(range(tensor))
    own = lax.axis_index("tensor")
    depth = attend_in.shape[1]
    model = depth * dp
    part = attend_in.shape[3]
    norms = norm_params.shape[0]

    share = embed_table.shape[0] // tensor
    lines = -(-(share + norms + 1) // 16) * 16
    embed_own = lax.dynamic_slice_in_dim(embed_table, own * share, share, 0).astype(low)
    norm_lines = jnp.pad(norm_params, ((0, 0), (0, 0), (0, 128 - depth))).reshape(norms, 256)
    count_own = jnp.sum(mask_flags)
    count_line = jnp.stack([count_own // 64, count_own % 64]).astype(full)[None]
    embed_piece = jnp.concatenate(
        [
            embed_own,
            jnp.pad(norm_lines, ((0, 0), (0, model - 256))).astype(low),
            jnp.pad(count_line, ((0, lines - share - norms - 1), (0, model - 2))).astype(low),
        ],
        0,
    )
    pieces = [embed_piece]
    for layer in range(LAYERS):
        planes = attend_in[layer].astype(low)
        pieces += [
            jnp.concatenate([planes[:, 0], planes[:, 1], planes[:, 2], attend_out[layer].astype(low).T], 1),
            expand[layer].astype(low),
            contract[layer].astype(low).T,
        ]
    gathered = gather_all(dims, pieces + [logit_table.astype(low)])
    weights = {}
    for layer in range(LAYERS):
        for at, kind in enumerate((ATTEND, EXPAND, CONTRACT)):
            weights[(kind, layer)] = gathered[1 + 3 * layer + at]
    flat = {name: value.reshape(tensor, model, -1) for name, value in weights.items()}
    w_head = gathered[-1].reshape(tensor, model, -1)
    table = gathered[0].reshape(-1, model)
    extra = gathered[0].reshape(tensor, dp, lines, model)[0, :, share:].astype(full)
    gains = jnp.stack([extra[:, :norms, :depth], extra[:, :norms, 128 : 128 + depth]], 1)
    gains = gains.transpose(2, 1, 0, 3).reshape(2 * norms, model)
    token_count = jnp.sum(extra[:, norms, 0]) * 64.0 + jnp.sum(extra[:, norms, 1])

    codes_own = lax.dynamic_slice_in_dim(image_codes, own, 1, 0)[0]
    flags_own = lax.dynamic_slice_in_dim(mask_flags, own, 1, 0)[0]
    label_own = lax.dynamic_slice_in_dim(labels, own, 1, 0)
    padding = TOKENS - SEQ
    row_index = jnp.concatenate([CODES + 1 + label_own, jnp.where(flags_own == 1, CODES, codes_own)])
    place_rows = CODES + 1 + CLASSES + jnp.arange(SEQ, dtype=jnp.int32)
    targets = jnp.pad(codes_own, (1, padding))
    weights_loss = jnp.pad(flags_own.astype(full), (1, padding))

    def spot_of(rows):
        block, inside = rows // (share * tensor), rows % (share * tensor)
        return (inside // share) * (lines * dp) + block * lines + inside % share

    rows = jnp.pad(jnp.stack([spot_of(row_index), spot_of(place_rows)]), ((0, 0), (0, padding)), constant_values=-1)
    numbers = jnp.arange(table.shape[0], dtype=jnp.int32)[:, None]
    picks = ((numbers == rows[0][None]).astype(full) + (numbers == rows[1][None]).astype(full)).astype(low)

    head_count = HEADS // tensor
    head_width = model // HEADS
    stream = matmul_left(picks, table)
    saved = {}
    for layer in range(LAYERS):
        gain = gains[4 * layer : 4 * layer + 4]
        attend, grow, shrink = [flat[(kind, layer)] for kind in (ATTEND, EXPAND, CONTRACT)]
        normed = layer_norm(stream, gain[0], gain[1]).astype(low)
        joined = [matmul(normed, attend[at][:, : 3 * part]).astype(low) for at in spots]
        blended = attend_heads(joined, head_count, head_width)
        middle = stream + sum(matmul_right(blended[at], attend[at][:, 3 * part :]) for at in spots)
        normed_two = layer_norm(middle, gain[2], gain[3]).astype(low)
        active, slope = [], []
        for at in spots:
            hidden = matmul(normed_two, grow[at])
            side = 0.5 * (1.0 + lax.erf(hidden * (0.5**0.5)))
            active.append((hidden * side).astype(low))
            slope.append(side + hidden * jnp.exp(-0.5 * hidden * hidden) * (0.5 / jnp.pi) ** 0.5)
        single = dict(stream=stream, normed=normed, middle=middle, normed_two=normed_two)
        several = dict(joined=joined, blended=blended, active=active, slope=slope)
        for name, value in single.items():
            saved.setdefault(name, {})[(layer, 0)] = value
        for name, value in several.items():
            saved.setdefault(name, {}).update({(layer, at): value[at] for at in spots})
        stream = middle + sum(matmul_right(active[at], shrink[at]) for at in spots)

    final_gain = gains[4 * LAYERS : 4 * LAYERS + 2]
    final = layer_norm(stream, final_gain[0], final_gain[1]).astype(low)
    logits = jnp.concatenate([matmul(final, w_head[at]) for at in spots], 1)
    is_target = (targets[:, None] == jnp.arange(logits.shape[1], dtype=jnp.int32)[None, :]).astype(full)
    peak = jnp.max(logits, axis=1, keepdims=True)
    log_total = peak + jnp.log(jnp.sum(jnp.exp(logits - peak), axis=1, keepdims=True))
    picked = jnp.sum(is_target * logits, axis=1)
    loss_own = jnp.sum((log_total[:, 0] - picked) * weights_loss)
    grad_logits = (
        (jnp.exp(logits - log_total) - is_target) * (weights_loss / token_count)[:, None]
    ).astype(low)
    local = logit_table.shape[1]
    grad_final = sum(
        matmul_right(grad_logits[:, at * local : (at + 1) * local], w_head[at]) for at in spots
    )
    gradient, final_scale, final_offset = norm_back(stream, final_gain[0], final_gain[1], grad_final)
    found = backward_all(
        dims,
        LAYERS,
        share,
        lines,
        norms,
        weights,
        saved,
        dict(
            rows=rows,
            gains=jnp.pad(gains, ((0, 16 - 2 * norms), (0, 0))),
            grad_top=gradient,
            final=final,
            grad_logits=grad_logits,
            final_grads=jnp.stack([final_scale, final_offset]),
            loss=jnp.pad(loss_own.reshape(1, 1), ((0, 7), (0, 127))),
        ),
        local,
    )

    def turn(values):
        return [
            values[0].transpose(0, 2, 1, 3),
            values[1],
            values[2],
            values[3].transpose(0, 2, 1),
            *values[4:],
        ]

    new = adam_all(LAYERS, share, norms, found, turn(params), turn(moments_one), turn(moments_two))
    results = []
    for index in range(7):
        for group in (new.new_weight, new.new_one, new.new_two):
            value = group[index]
            results.append(
                value.transpose(0, 2, 1, 3) if index == 0 else value.transpose(0, 2, 1) if index == 3 else value
            )
    return (*results, new.results[8, 0], token_count, new.results[0, 0])


def solution(mesh):
    dp, tensor = mesh.shape["dp"], mesh.shape["tensor"]
    in_specs = (
        (P("dp", None), P("dp"), P("dp", None))
        + (P(None, "dp", None, "tensor"),) * 3
        + (P(None, "tensor", "dp"),) * 3
        + (P(None, "dp", "tensor"),) * 3
        + (P(None, "tensor", "dp"),) * 3
        + (P("dp", None),) * 3
        + (P("dp", "tensor"),) * 3
        + (P(None, None, "dp"),) * 3
    )

    def either(*args):
        whole_tiles = args[3].shape[1] % 16 == 0 and args[1].shape[0] == tensor
        return body(dp, tensor, *args) if whole_tiles else plain_body(*args)

    return jax.shard_map(
        either,
        mesh=mesh,
        in_specs=in_specs,
        out_specs=in_specs[3:] + (P(), P(), P()),
        check_vma=False,
    )
```

```python
import functools

import jax
import jax.numpy as jnp
from jax import lax
from jax.experimental import pallas as pl
from jax.experimental.pallas import tpu as pltpu
from jax.sharding import PartitionSpec as P

HEADS = 16
CODES = 1024
CLASSES = 1000
LAYERS = 2
STEP = 10
SEQ = 257
ROWS_UP = 16

beta_one = 0.9
beta_two = 0.96
matrix_rate = 0.02
embed_rate = 0.5
vector_rate = 0.25
weight_decay = 0.045
epsilon = 1e-10
clip_limit = 0.02
norm_epsilon = 1e-06
low = jnp.bfloat16
full = jnp.float32


def matmul(left, right):
    return jnp.dot(left, right, preferred_element_type=full)


def matmul_left(left, right):
    return lax.dot_general(left, right, (((0,), (0,)), ((), ())), preferred_element_type=full)


def matmul_right(left, right):
    return lax.dot_general(left, right, (((1,), (1,)), ((), ())), preferred_element_type=full)


def layer_norm(stream, scaling, offset):
    average = jnp.mean(stream, axis=-1, keepdims=True)
    centred = stream - average
    variance = jnp.mean(centred * centred, axis=-1, keepdims=True)
    return centred * lax.rsqrt(variance + norm_epsilon) * scaling + offset


def norm_back(stream, scaling, offset, gradient):
    normed_out, pull = jax.vjp(layer_norm, stream, scaling, offset)
    return pull(gradient)


def gelu_exact(values):
    return jax.nn.gelu(values, approximate=False)


def branch_total(piece_sum):
    return lax.psum(piece_sum.astype(jnp.bfloat16), "tensor").astype(jnp.float32)


def input_total(piece_sum):
    return lax.psum(piece_sum.astype(jnp.bfloat16), "tensor").astype(jnp.float32)


def split_heads(joined, images, head_count):
    head_width = joined.shape[1] // (3 * head_count)
    sections = joined.reshape(images, SEQ, 3, head_count, head_width)
    return (sections[:, :, 0], sections[:, :, 1], sections[:, :, 2], head_width ** (-0.5))


def attend_forward(joined, images, head_count):
    queries, key_rows, values, score_scale = split_heads(joined, images, head_count)
    scores = (
        jnp.einsum("bqhd,bkhd->bhqk", queries, key_rows, preferred_element_type=jnp.float32)
        * score_scale
    )
    peak_value = jnp.max(scores, axis=-1, keepdims=True)
    log_total = peak_value + jnp.log(jnp.sum(jnp.exp(scores - peak_value), axis=-1, keepdims=True))
    attention = jnp.exp(scores - log_total).astype(jnp.bfloat16)
    blended = jnp.einsum("bhqk,bkhd->bqhd", attention, values, preferred_element_type=jnp.float32)
    return (blended.astype(jnp.bfloat16).reshape(joined.shape[0], -1), log_total)


def attend_backward(joined, log_total, grad_blended, images, head_count):
    queries, key_rows, values, score_scale = split_heads(joined, images, head_count)
    scores = (
        jnp.einsum("bqhd,bkhd->bhqk", queries, key_rows, preferred_element_type=jnp.float32)
        * score_scale
    )
    attention = jnp.exp(scores - log_total)
    grad_out = grad_blended.reshape(queries.shape)
    grad_attention = jnp.einsum(
        "bqhd,bkhd->bhqk", grad_out, values, preferred_element_type=jnp.float32
    )
    row_total = jnp.sum(attention * grad_attention, axis=-1, keepdims=True)
    grad_scores = (attention * (grad_attention - row_total)).astype(jnp.bfloat16)
    grad_queries = (
        jnp.einsum("bhqk,bkhd->bqhd", grad_scores, key_rows, preferred_element_type=jnp.float32)
        * score_scale
    )
    grad_keys = (
        jnp.einsum("bhqk,bqhd->bkhd", grad_scores, queries, preferred_element_type=jnp.float32)
        * score_scale
    )
    grad_values = jnp.einsum(
        "bhqk,bqhd->bkhd",
        attention.astype(jnp.bfloat16),
        grad_out,
        preferred_element_type=jnp.float32,
    )
    stacked = jnp.stack([grad_queries, grad_keys, grad_values], axis=2).astype(jnp.bfloat16)
    return stacked.reshape(joined.shape)


def layer_forward(stream, weights, gains, images, head_count):
    w_in, w_out, w_expand, w_contract = weights
    normed = layer_norm(stream, gains[0, 0], gains[0, 1]).astype(jnp.bfloat16)
    joined = matmul(normed, w_in.reshape(w_in.shape[0], -1)).astype(jnp.bfloat16)
    blended, log_total = attend_forward(joined, images, head_count)
    middle = stream + branch_total(matmul(blended, w_out))
    normed_two = layer_norm(middle, gains[1, 0], gains[1, 1]).astype(jnp.bfloat16)
    hidden = matmul(normed_two, w_expand)
    active = gelu_exact(hidden).astype(jnp.bfloat16)
    result = middle + branch_total(matmul(active, w_contract))
    return (
        result,
        (stream, normed, joined, blended, log_total, middle, normed_two, hidden, active),
    )


def layer_backward(gradient, saved, weights, gains, images, head_count):
    w_in, w_out, w_expand, w_contract = weights
    stream, normed, joined, blended, log_total, middle, normed_two, hidden, active = saved
    grad_low = gradient.astype(jnp.bfloat16)
    g_contract = matmul_left(active, grad_low)
    grad_active = matmul_right(grad_low, w_contract)
    gelu_out, gelu_pull = jax.vjp(gelu_exact, hidden)
    grad_hidden = gelu_pull(grad_active)[0].astype(jnp.bfloat16)
    g_expand = matmul_left(normed_two, grad_hidden)
    grad_normed = input_total(matmul_right(grad_hidden, w_expand))
    grad_mid, scale_two, offset_two = norm_back(middle, gains[1, 0], gains[1, 1], grad_normed)
    gradient = gradient + grad_mid
    grad_low = gradient.astype(jnp.bfloat16)
    g_out = matmul_left(blended, grad_low)
    grad_blended = matmul_right(grad_low, w_out).astype(jnp.bfloat16)
    grad_joined = attend_backward(joined, log_total, grad_blended, images, head_count)
    g_in = matmul_left(normed, grad_joined).reshape(w_in.shape)
    grad_normed = input_total(matmul_right(grad_joined, w_in.reshape(w_in.shape[0], -1)))
    grad_first, scale_one, offset_one = norm_back(stream, gains[0, 0], gains[0, 1], grad_normed)
    norm_grads = jnp.stack([jnp.stack([scale_one, offset_one]), jnp.stack([scale_two, offset_two])])
    return (gradient + grad_first, (g_in, g_out, g_expand, g_contract), norm_grads)


def plain_body(
    image_codes,
    labels,
    mask_flags,
    attend_in,
    attend_in_one,
    attend_in_two,
    attend_out,
    attend_out_one,
    attend_out_two,
    expand,
    expand_one,
    expand_two,
    contract,
    contract_one,
    contract_two,
    embed_table,
    embed_one,
    embed_two,
    logit_table,
    logit_one,
    logit_two,
    norm_params,
    norm_one,
    norm_two,
):
    w_in, w_out, w_expand, w_contract, embed_rows, head_table, gains_low = (
        lax.all_gather(attend_in.astype(jnp.bfloat16), "dp", axis=1, tiled=True),
        lax.all_gather(attend_out.astype(jnp.bfloat16), "dp", axis=2, tiled=True),
        lax.all_gather(expand.astype(jnp.bfloat16), "dp", axis=1, tiled=True),
        lax.all_gather(contract.astype(jnp.bfloat16), "dp", axis=2, tiled=True),
        lax.all_gather(embed_table.astype(jnp.bfloat16), "dp", axis=0, tiled=True),
        lax.all_gather(logit_table.astype(jnp.bfloat16), "dp", axis=0, tiled=True),
        lax.all_gather(norm_params.astype(jnp.bfloat16), "dp", axis=2, tiled=True),
    )
    gains = gains_low.astype(jnp.float32)
    images = labels.shape[0]
    head_count = HEADS // lax.axis_size("tensor")
    code_rows = jnp.where(mask_flags == 1, CODES, image_codes)
    row_index = jnp.concatenate([(CODES + 1 + labels)[:, None], code_rows], axis=1).reshape(-1)
    place_rows = jnp.tile(CODES + 1 + CLASSES + jnp.arange(SEQ), images)
    targets = jnp.concatenate([jnp.zeros((images, 1), jnp.int32), image_codes], axis=1).reshape(-1)
    weights_loss = jnp.concatenate(
        [jnp.zeros((images, 1), jnp.float32), mask_flags.astype(jnp.float32)], axis=1
    ).reshape(-1)
    stream = embed_rows[row_index].astype(jnp.float32) + embed_rows[place_rows].astype(jnp.float32)
    saved_all = []
    for layer_index in range(LAYERS):
        weights = (
            w_in[layer_index],
            w_out[layer_index],
            w_expand[layer_index],
            w_contract[layer_index],
        )
        stream, saved = layer_forward(
            stream, weights, gains[2 * layer_index : 2 * layer_index + 2], images, head_count
        )
        saved_all.append(saved)
    final_gain = gains[2 * LAYERS]
    final = layer_norm(stream, final_gain[0], final_gain[1]).astype(jnp.bfloat16)
    logits = matmul(final, head_table)
    local_codes = logits.shape[1]
    col_start = lax.axis_index("tensor") * local_codes
    is_target = (
        targets[:, None] == col_start + jnp.arange(local_codes, dtype=jnp.int32)[None, :]
    ).astype(jnp.float32)
    peak_value = jnp.max(logits, axis=1)
    exp_total = jnp.sum(jnp.exp(logits - peak_value[:, None]), axis=1)
    picked = jnp.sum(is_target * logits, axis=1)
    peak_all = lax.pmax(peak_value, "tensor")
    exp_all, picked_all = lax.psum((exp_total * jnp.exp(peak_value - peak_all), picked), "tensor")
    log_total = peak_all + jnp.log(exp_all)
    loss_terms = (log_total - picked_all) * weights_loss
    loss_sum, token_count = lax.psum((jnp.sum(loss_terms), jnp.sum(weights_loss)), "dp")
    grad_logits = (
        (jnp.exp(logits - log_total[:, None]) - is_target) * (weights_loss / token_count)[:, None]
    ).astype(jnp.bfloat16)
    g_head = matmul_left(final, grad_logits)
    grad_final = input_total(matmul_right(grad_logits, head_table))
    gradient, final_scale, final_offset = norm_back(
        stream, final_gain[0], final_gain[1], grad_final
    )
    layer_grads = [None] * LAYERS
    norm_grads = [None] * LAYERS
    for layer_index in reversed(range(LAYERS)):
        weights = (
            w_in[layer_index],
            w_out[layer_index],
            w_expand[layer_index],
            w_contract[layer_index],
        )
        gradient, found, gain_grads = layer_backward(
            gradient,
            saved_all[layer_index],
            weights,
            gains[2 * layer_index : 2 * layer_index + 2],
            images,
            head_count,
        )
        layer_grads[layer_index] = found
        norm_grads[layer_index] = gain_grads
    g_norms = jnp.concatenate(
        [
            jnp.stack(norm_grads).reshape(2 * LAYERS, 2, -1),
            jnp.stack([final_scale, final_offset])[None],
        ],
        axis=0,
    )
    g_table = jax.ops.segment_sum(
        jnp.concatenate([gradient, gradient], axis=0),
        jnp.concatenate([row_index, place_rows]),
        num_segments=embed_rows.shape[0],
    )
    g_in_all = jnp.stack([found[0] for found in layer_grads])
    g_out_all = jnp.stack([found[1] for found in layer_grads])
    g_expand_all = jnp.stack([found[2] for found in layer_grads])
    g_contract_all = jnp.stack([found[3] for found in layer_grads])
    g_in_all, g_out_all, g_expand_all, g_contract_all, g_table, g_head, g_norms = (
        lax.psum_scatter(g_in_all, "dp", scatter_dimension=1, tiled=True),
        lax.psum_scatter(g_out_all, "dp", scatter_dimension=2, tiled=True),
        lax.psum_scatter(g_expand_all, "dp", scatter_dimension=1, tiled=True),
        lax.psum_scatter(g_contract_all, "dp", scatter_dimension=2, tiled=True),
        lax.psum_scatter(g_table, "dp", scatter_dimension=0, tiled=True),
        lax.psum_scatter(g_head, "dp", scatter_dimension=0, tiled=True),
        lax.psum_scatter(g_norms, "dp", scatter_dimension=2, tiled=True),
    )
    gradients = (g_in_all, g_out_all, g_expand_all, g_contract_all, g_table, g_head, g_norms)
    first_rank = (lax.axis_index("tensor") == 0).astype(jnp.float32)
    split_squares = (
        jnp.sum(g_in_all * g_in_all)
        + jnp.sum(g_out_all * g_out_all)
        + jnp.sum(g_expand_all * g_expand_all)
        + jnp.sum(g_contract_all * g_contract_all)
        + jnp.sum(g_head * g_head)
    )
    shared_squares = jnp.sum(g_table * g_table) + jnp.sum(g_norms * g_norms)
    grad_norm = jnp.sqrt(lax.psum(split_squares + first_rank * shared_squares, ("dp", "tensor")))
    factor = clip_limit / jnp.maximum(grad_norm, clip_limit)
    params = (attend_in, attend_out, expand, contract, embed_table, logit_table, norm_params)
    moments_one = (
        attend_in_one,
        attend_out_one,
        expand_one,
        contract_one,
        embed_one,
        logit_one,
        norm_one,
    )
    moments_two = (
        attend_in_two,
        attend_out_two,
        expand_two,
        contract_two,
        embed_two,
        logit_two,
        norm_two,
    )
    results = []
    for index in range(7):
        rate_here = vector_rate if index == 6 else embed_rate if index == 4 else matrix_rate
        decay_here = 0.0 if index == 6 else weight_decay
        results.extend(
            adam_step(
                params[index],
                moments_one[index],
                moments_two[index],
                gradients[index],
                factor,
                rate_here,
                decay_here,
            )
        )
    return (
        results[0],
        results[1],
        results[2],
        results[3],
        results[4],
        results[5],
        results[6],
        results[7],
        results[8],
        results[9],
        results[10],
        results[11],
        results[12],
        results[13],
        results[14],
        results[15],
        results[16],
        results[17],
        results[18],
        results[19],
        results[20],
        loss_sum,
        token_count,
        grad_norm,
    )


def adam_step(weight, moment_one, moment_two, gradient, factor, rate_here, decay_here):
    gradient = gradient * factor
    moment_one = beta_one * moment_one + (1.0 - beta_one) * gradient
    moment_two = beta_two * moment_two + (1.0 - beta_two) * gradient * gradient
    correct_one = 1.0 - beta_one**STEP
    correct_two = 1.0 - beta_two**STEP
    weight = weight - rate_here * (
        moment_one / correct_one / (jnp.sqrt(moment_two / correct_two) + epsilon)
        + decay_here * weight
    )
    return [weight, moment_one, moment_two]


MESH = pl.DeviceIdType.MESH


def factors(dp, tensor):
    return [("tensor", tensor // 2, 2), ("tensor", 2, 1), ("dp", dp // 2, 2), ("dp", 2, 1)]


OUTER, PAIR, LONG, NEAR = range(4)
ORDERS = {
    "a": (LONG, NEAR, OUTER, PAIR),
    "b": (LONG, OUTER, NEAR, PAIR),
    "d": (OUTER, LONG, NEAR, PAIR),
    "e": (NEAR, LONG, OUTER, PAIR),
}


def place_of(dims):
    return [(lax.axis_index(axis) // stride) % size for axis, size, stride in dims]


def peer_of(dims, here, dim, move):
    there = list(here)
    there[dim] = lax.rem(here[dim] + move, dims[dim][1])
    found = {"dp": 0, "tensor": 0}
    for (axis, size, stride), at in zip(dims, there):
        found[axis] = found[axis] + at * stride
    return (found["dp"], found["tensor"])


def greet(dims, here):
    barrier = pltpu.get_barrier_semaphore()
    count = 0
    for dim, (axis, size, stride) in enumerate(dims):
        for move in range(1, size):
            pl.semaphore_signal(
                barrier, inc=1, device_id=peer_of(dims, here, dim, move), device_id_type=MESH
            )
            count += 1
    pl.semaphore_wait(barrier, count)


def gather_units(rows):
    tiles = rows // 16
    if rows % 16 or tiles < 4:
        return [[(0, rows, "a")]]
    if tiles == 6:
        cuts = [[("a", 1), ("b", 1), ("d", 1)], [("a", 1), ("b", 1), ("e", 1)]]
    else:
        cuts = [[("a", 1), ("b", 1)], [("a", 1), ("b", 1), ("d", tiles - 4)]]
    units, row = [], 0
    for cut in cuts:
        unit = []
        for order, count in cut:
            unit.append((row, 16 * count, order))
            row += 16 * count
        units.append(unit)
    return units


TOKENS = -(-SEQ // 16) * 16


class Refs:
    pass


class Parts:
    def __init__(self):
        self.ins, self.outs, self.scratch = [], [], []

    def put(self, near=False, key=None, **named):
        for name, value in named.items():
            space = pltpu.VMEM if near else pl.ANY
            self.ins.append(((name, key), value, pl.BlockSpec(memory_space=space)))

    def out(self, kind, near=False, key=None, **named):
        for name, shape in named.items():
            space = pltpu.VMEM if near else pl.ANY
            self.outs.append(
                ((name, key), jax.ShapeDtypeStruct(shape, kind), pl.BlockSpec(memory_space=space))
            )

    def keep(self, key=None, **named):
        for name, scratch in named.items():
            self.scratch.append(((name, key), scratch))

    def refs(self, refs):
        found = Refs()
        for ((name, key), *rest), ref in zip(self.ins + self.outs + self.scratch, refs):
            if key is None:
                setattr(found, name, ref)
            else:
                found.__dict__.setdefault(name, {})[key] = ref
        return found

    def call(self, body, barrier=None):
        found = pl.pallas_call(
            lambda *refs: body(self.refs(refs)),
            out_shape=[shape for name, shape, spec in self.outs],
            in_specs=[spec for name, value, spec in self.ins],
            out_specs=[spec for name, shape, spec in self.outs],
            scratch_shapes=[scratch for name, scratch in self.scratch],
            compiler_params=pltpu.CompilerParams(
                collective_id=barrier,
                has_side_effects=barrier is not None,
                vmem_limit_bytes=60 * 1024 * 1024,
            ),
        )(*[value for name, value, spec in self.ins])
        return self.refs([None] * len(self.ins) + list(found))


class Reducer:
    def __init__(self, dims, chunks, cuts):
        self.dims, self.chunks = dims, chunks
        self.sizes = [size for axis, size, stride in dims]
        self.units, self.sides, counts = [], set(), {}
        self.slots = 0
        for chunk, (name, rows, width, wide) in enumerate(chunks):
            for unit in cuts(rows, width):
                found = []
                for row, size, order in unit:
                    stages = []
                    for stage in range(4):
                        dim = ORDERS[order][3 - stage]
                        key = (order, stage, size, width, wide)
                        stages.append((dim, key, counts.get(key, 0), self.slots))
                        self.sides.add((key, len(self.units) % 2))
                        counts[key] = counts.get(key, 0) + 1
                        self.slots += self.sizes[dim] - 1
                    found.append((row, size, order, stages, len(self.units) % 2))
                self.units.append((chunk, found))
        self.counts = counts
        self.started, self.busy = {}, {}

    def room(self, key):
        order, stage, size, width, wide = key
        gone = [ORDERS[order][3 - at] for at in range(stage + 1)]
        rest = tuple(self.sizes[dim] for dim in range(4) if dim not in gone)
        return (self.sizes[gone[-1]] - 1, *rest, size, width)

    def declare(self, parts):
        for key, count in self.counts.items():
            order, stage, size, width, wide = key
            kind = full if wide and stage == 3 else low
            parts.out(kind, key=key, came=(count, *self.room(key)))
            parts.keep(key=key, staged=pltpu.VMEM(self.room(key), kind), staged_sem=pltpu.SemaphoreType.DMA)
            for side in range(2):
                if stage == 2 and wide and (key, side) in self.sides:
                    parts.keep(key=(key, side), exact=pltpu.VMEM(self.room(key)[1:], full))
        parts.keep(
            send=pltpu.SemaphoreType.DMA((self.slots,)),
            recv=pltpu.SemaphoreType.DMA((self.slots,)),
            squares=pltpu.VMEM((8, 128), full),
        )

    def bind(self, refs, here, blocks, results):
        self.refs, self.here, self.blocks, self.results = refs, here, blocks, results
        refs.squares[...] = jnp.zeros_like(refs.squares)

    def turn(self, dim, move):
        return lax.rem(self.here[dim] + move, self.sizes[dim]) if move else self.here[dim]

    def block(self, chunk, part, stage, move):
        row, size, order, stages, side = part
        gone = [ORDERS[order][3 - at] for at in range(stage)]
        dim = ORDERS[order][3 - stage]
        spot = [
            self.turn(at, move) if at == dim else (self.here[at] if at in gone else slice(None))
            for at in range(4)
        ]
        return self.blocks[chunk].at[(*spot, pl.ds(row, size))]

    def exact(self, part, stage, move):
        row, size, order, stages, side = part
        left = sorted(ORDERS[order][: 4 - stage])
        dim = ORDERS[order][3 - stage]
        spot = [self.turn(at, move) if at == dim else slice(None) for at in left]
        return self.refs.exact[(stages[stage - 1][1], side)].at[tuple(spot)]

    def copies(self, chunk, part, stage):
        dim, key, count, slot = part[3][stage]
        wide = key[4] and stage == 3
        return [
            pltpu.make_async_remote_copy(
                src_ref=self.exact(part, stage, move) if wide else self.block(chunk, part, stage, move),
                dst_ref=self.refs.came[key].at[count, move - 1],
                send_sem=self.refs.send.at[slot + move - 1],
                recv_sem=self.refs.recv.at[slot + move - 1],
                device_id=peer_of(self.dims, self.here, dim, move),
                device_id_type=MESH,
            )
            for move in range(1, self.sizes[dim])
        ]

    def staged(self, part, stage):
        dim, key, count, slot = part[3][stage]
        return pltpu.make_async_copy(
            self.refs.came[key].at[count], self.refs.staged[key], self.refs.staged_sem[key]
        )

    def add(self, chunk, part, stage):
        row, size, order, stages, side = part
        dim, key, count, slot = stages[stage]
        held, came = self.block(chunk, part, stage, 0), self.refs.staged[key]
        if stage == 0:
            total = held[...]
            for move in range(self.sizes[dim] - 1):
                total = total + came[move]
            held[...] = total
            return
        exact = stage == 3 and key[4]
        total = (self.exact(part, stage, 0) if exact else held)[...].astype(full)
        for move in range(self.sizes[dim] - 1):
            total = total + came[move].astype(full)
        if stage < 3 and not (stage == 2 and key[4]):
            held[...] = total.astype(low)
            return
        if stage == 2:
            for copy in self.busy.pop((key, side), []):
                copy.wait_send()
            self.refs.exact[(key, side)][...] = total
            return
        self.results[chunk][pl.ds(row, size), :] = total
        square = total * total
        square = sum(square[at : at + 8] for at in range(0, size, 8))
        self.refs.squares[...] += sum(square[:, at : at + 128] for at in range(0, square.shape[1], 128))

    def tick(self, now):
        work = [
            (at, (now - at) // 2)
            for at in range(len(self.units))
            if (now - at) % 2 == 0 and 0 <= now - at <= 8
        ]
        for at, stage in work:
            chunk, found = self.units[at]
            if stage:
                for part in found:
                    for copy in self.copies(chunk, part, stage - 1):
                        copy.wait_recv()
                    self.staged(part, stage - 1).start()
        for at, stage in work:
            chunk, found = self.units[at]
            for part in found:
                if stage:
                    self.staged(part, stage - 1).wait()
                    self.add(chunk, part, stage - 1)
                if stage < 4:
                    dim, key, count, slot = part[3][stage]
                    copies = self.copies(chunk, part, stage)
                    for copy in copies:
                        copy.start()
                    if key[4] and stage == 3:
                        self.busy[(part[3][2][1], part[4])] = copies
                    else:
                        self.started.setdefault(chunk, []).extend(copies)

    def ticks(self):
        return len(self.units) + 8

    def finish(self):
        for chunk in list(self.started):
            self.release(chunk)
        for copy in sum(self.busy.values(), []):
            copy.wait_send()

    def release(self, chunk):
        for copy in self.started.pop(chunk):
            copy.wait_send()


def reduce_cuts(rows, width):
    tiles = rows // 16
    if tiles == 6 and width > 256:
        cuts = [[("a", 1), ("b", 1), ("d", 1)], [("a", 1), ("b", 1), ("e", 1)]]
    elif tiles == 6:
        cuts = [[("a", 3), ("b", 3)]]
    else:
        cuts = [[("a", 1), ("b", 1)], [("a", 1), ("b", 1), ("d", tiles - 4)]]
    units, row = [], 0
    for cut in cuts:
        unit = []
        for order, count in cut:
            unit.append((row, 16 * count, order))
            row += 16 * count
        units.append(unit)
    return units


def norm_back_rows(grad, grad_normed, source, gain, found, row):
    scaling = gain[...]

    def step(at, totals):
        rows = pl.ds(pl.multiple_of(at * 16, 16), 16)
        value, up = source[rows, :], grad_normed[rows, :]
        centred = value - jnp.mean(value, axis=-1, keepdims=True)
        spread = lax.rsqrt(jnp.mean(centred * centred, axis=-1, keepdims=True) + norm_epsilon)
        unit = centred * spread
        inner = up * scaling
        pulled = spread * (
            inner
            - jnp.mean(inner, axis=-1, keepdims=True)
            - unit * jnp.mean(inner * unit, axis=-1, keepdims=True)
        )
        grad[rows, :] = grad[rows, :] + pulled
        return totals[0] + up * unit, totals[1] + up

    zero = jnp.zeros((16, source.shape[1]), full)
    total = lax.fori_loop(0, source.shape[0] // 16, step, (zero, zero))
    found[pl.ds(row, 1), :] = jnp.sum(total[0], axis=0, keepdims=True)
    found[pl.ds(row + 1, 1), :] = jnp.sum(total[1], axis=0, keepdims=True)


def square_block(value):
    return value.reshape(-1, value.shape[-1])


HEAD, ATTEND, EXPAND, CONTRACT, TABLE = range(5)


def backward_kernel(dims, reducer, layers, share, heads, width, norms, refs):
    here = place_of(dims)
    sizes = reducer.sizes
    sides = (sizes[2], sizes[3])
    names = [name for name, rows, across, wide in reducer.chunks]
    spots = sizes[0] * sizes[1]
    part = heads * width

    weights = {
        name: pltpu.make_async_copy(refs.weight[name], refs.slots.at[at], refs.weight_sem.at[at])
        for at, name in enumerate(names[1:-1])
    }
    mlp = (refs.slope, refs.active, refs.normed_two, refs.middle)
    mlp_near = (refs.near_slope, refs.near_active, refs.near_normed_two, refs.near_middle)
    attend = (refs.joined, refs.blended, refs.normed, refs.stream)
    attend_near = (refs.near_joined, refs.near_blended, refs.near_normed, refs.near_stream)

    def fetches(far, near, sem, layer):
        return [
            pltpu.make_async_copy(source.at[layer], target, sem.at[at])
            for at, (source, target) in enumerate(zip(far, near))
        ]

    def mlp_fetches(layer):
        return fetches(mlp, mlp_near, refs.mlp_sem, layer)

    def attend_fetches(layer):
        return fetches(attend, attend_near, refs.attend_sem, layer)

    order = names[1:-1]
    for copy in mlp_fetches(layers - 1):
        copy.start()
    for name in order[:2]:
        weights[name].start()
    for copy in attend_fetches(layers - 1):
        copy.start()
    for name in order[2:]:
        weights[name].start()
    greet(dims, here)

    lines = refs.total[(TABLE, 0)].shape[0]
    table_blocks = refs.slots.at[0, :, :, :, :, pl.ds(0, lines)]
    blocks = [refs.head_blocks] + [refs.slots.at[at] for at in range(len(order))] + [table_blocks]
    reducer.bind(refs, here, blocks, [refs.total[name] for name in names])
    clock = [0]

    def run(count):
        for _ in range(count):
            reducer.tick(clock[0])
            clock[0] += 1

    per_chunk = [0] * len(names)
    for chunk, found in reducer.units:
        per_chunk[chunk] += 1
    grad, grad_normed, norm_grads = refs.grad, refs.grad_normed, refs.norm_grads
    gains = refs.gains

    norm_grads[...] = jnp.zeros_like(norm_grads)
    norm_grads[pl.ds(4 * layers, 2), :] = refs.final_grads[...]
    grad[...] = refs.grad_top[...]
    turned = refs.final[...].T
    for spot in range(spots):
        across = refs.grad_logits.shape[1] // spots
        found = matmul(turned, refs.grad_logits[:, spot * across : (spot + 1) * across])
        refs.head_blocks[spot // sizes[1], spot % sizes[1]] = found.astype(low).reshape(*sides, -1, across)
    run(per_chunk[0])

    for layer in reversed(range(layers)):
        at_contract, at_expand, at_attend = [names.index((kind, layer)) for kind in (CONTRACT, EXPAND, ATTEND)]
        slot_contract, slot_expand, slot_attend = [
            refs.slots.at[at - 1] for at in (at_contract, at_expand, at_attend)
        ]

        for copy in mlp_fetches(layer):
            copy.wait()
        weights[(CONTRACT, layer)].wait()
        refs.grad_low[...] = grad[...].astype(low)
        refs.turned[...] = grad[...].astype(low).T

        def contract_step(spot, carry):
            outer, pair = spot // sizes[1], spot % sizes[1]
            held = square_block(slot_contract[outer, pair])
            pulled = matmul(refs.grad_low[...], held) * refs.near_slope[spot]
            refs.grad_hidden[spot] = pulled.astype(low)
            found = matmul(refs.turned[...], refs.near_active[spot]).astype(low)
            slot_contract[outer, pair] = found.reshape(*sides, -1, found.shape[-1])
            return carry

        lax.fori_loop(0, spots, contract_step, 0)
        run(per_chunk[at_contract])

        weights[(EXPAND, layer)].wait()
        refs.turned[...] = refs.near_normed_two[...].T
        grad_normed[...] = jnp.zeros_like(grad_normed)

        def expand_step(spot, carry):
            outer, pair = spot // sizes[1], spot % sizes[1]
            held = square_block(slot_expand[outer, pair])
            pulled = refs.grad_hidden[spot]
            grad_normed[...] += matmul_right(pulled, held)
            found = matmul(refs.turned[...], pulled).astype(low)
            slot_expand[outer, pair] = found.reshape(*sides, -1, found.shape[-1])
            return carry

        lax.fori_loop(0, spots, expand_step, 0)
        run(per_chunk[at_expand])
        norm_back_rows(
            grad, grad_normed, refs.near_middle, gains.at[pl.ds(4 * layer + 2, 1)], norm_grads, 4 * layer + 2
        )
        if layer:
            for copy in mlp_fetches(layer - 1):
                copy.start()

        for copy in attend_fetches(layer):
            copy.wait()
        weights[(ATTEND, layer)].wait()
        refs.grad_low[...] = grad[...].astype(low)
        refs.turned[...] = grad[...].astype(low).T
        refs.turned_two[...] = refs.near_normed[...].T
        grad_normed[...] = jnp.zeros_like(grad_normed)
        known = lax.broadcasted_iota(jnp.int32, (1, TOKENS), 1) < SEQ
        scale = width ** (-0.5)

        def attend_step(spot, carry):
            outer, pair = spot // sizes[1], spot % sizes[1]
            held = square_block(slot_attend[outer, pair])
            up_all = matmul(refs.grad_low[...], held[:, 3 * part :]).astype(low)
            pulled_all = []
            joined = refs.near_joined[spot]
            parts = [[], [], []]
            for head in range(heads):
                query, key, value = [
                    joined[:, (at * heads + head) * width : (at * heads + head + 1) * width] for at in range(3)
                ]
                up = up_all[:, head * width : (head + 1) * width]
                scores = jnp.where(known, matmul_right(query, key) * scale, -1e30)
                top = jnp.max(scores, axis=-1, keepdims=True)
                probs = jnp.exp(scores - top)
                probs = probs * (1.0 / jnp.sum(probs, axis=-1, keepdims=True))
                pulled = matmul_right(up, value)
                total = jnp.sum(probs * pulled, axis=-1, keepdims=True)
                moved = (probs * (pulled - total)).astype(low)
                parts[0].append((matmul(moved, key) * scale).astype(low))
                parts[1].append((matmul_left(moved, query) * scale).astype(low))
                parts[2].append(matmul_left(probs.astype(low), up).astype(low))
            pulled = jnp.concatenate(parts[0] + parts[1] + parts[2], axis=1)
            grad_normed[...] += matmul_right(pulled, held[:, : 3 * part])
            found = jnp.concatenate(
                [
                    matmul(refs.turned_two[...], pulled).astype(low),
                    matmul(refs.turned[...], refs.near_blended[spot]).astype(low),
                ],
                axis=1,
            )
            slot_attend[outer, pair] = found.reshape(*sides, -1, found.shape[-1])
            return carry

        lax.fori_loop(0, spots, attend_step, 0)
        run(per_chunk[at_attend])
        norm_back_rows(grad, grad_normed, refs.near_stream, gains.at[pl.ds(4 * layer, 1)], norm_grads, 4 * layer)
        if layer:
            for copy in attend_fetches(layer - 1):
                copy.start()

    upper = grad[...].astype(low)
    lower = (grad[...] - upper.astype(full)).astype(low)
    model = grad.shape[1]
    depth = refs.slots.shape[5]
    reducer.release(1)

    def table_step(block, carry):
        outer, pair = block // (sizes[1] * sizes[2] * sizes[3]), (block // (sizes[2] * sizes[3])) % sizes[1]
        far, near = (block // sizes[3]) % sizes[2], block % sizes[3]
        row = block * lines + lax.broadcasted_iota(jnp.int32, (lines, TOKENS), 0)
        picks = (row == refs.rows[0:1, :]).astype(full) + (row == refs.rows[1:2, :]).astype(full)
        picks = picks.astype(low)
        found = matmul(picks, upper) + matmul(picks, lower)
        table_blocks[outer, pair, far, near] = found.astype(low)
        return carry

    lax.fori_loop(0, spots * sizes[2] * sizes[3], table_step, 0)
    for far in range(sizes[2]):
        for near in range(sizes[3]):
            at = (far * sizes[3] + near) * depth
            lane = lax.broadcasted_iota(jnp.int32, (norms, 128), 1)
            cuts = []
            for kind in range(2):
                rows = jnp.concatenate(
                    [norm_grads[2 * norm + kind : 2 * norm + kind + 1, at : at + depth] for norm in range(norms)], axis=0
                )
                cuts.append(jnp.concatenate([rows, jnp.zeros((norms, 128 - depth), full)], axis=1))
            line = jnp.concatenate(
                cuts + [jnp.zeros((norms, model - 256), full)], axis=1
            )
            line = jnp.concatenate([line, jnp.zeros((lines - share - norms, line.shape[1]), full)], axis=0)
            base = share // 16 * 16
            old = table_blocks[0, 0, far, near, base:lines, :].astype(full)
            table_blocks[0, 0, far, near, base:lines, :] = jnp.concatenate(
                [old[: share - base], line], axis=0
            ).astype(low)
    run(reducer.ticks() - clock[0])
    finish_sums(dims, here, reducer, refs)
    reducer.finish()


def finish_sums(dims, here, reducer, refs):
    sizes = reducer.sizes
    own = pltpu.make_async_copy(refs.total[(TABLE, 0)], refs.spread.at[here[0], here[1]], refs.spread_own)
    own.start()
    refs.shared[0, :8] = refs.squares[...]
    refs.shared[0, 8:] = refs.loss[...]
    spread, slot, last = [], 0, []
    for step, dim in enumerate((OUTER, PAIR, NEAR, LONG)):
        copies = [
            pltpu.make_async_remote_copy(
                src_ref=refs.shared.at[step],
                dst_ref=refs.shared_came.at[step, move - 1],
                send_sem=refs.shared_send.at[step, move - 1],
                recv_sem=refs.shared_recv.at[step, move - 1],
                device_id=peer_of(dims, here, dim, move),
                device_id_type=MESH,
            )
            for move in range(1, sizes[dim])
        ]
        table = []
        if dim == OUTER:
            for move in range(1, sizes[dim]):
                target = refs.spread.at[here[0], here[1]]
                table.append((refs.total[(TABLE, 0)], target, move))
        if dim == PAIR:
            for move in range(1, sizes[dim]):
                table.append((refs.spread.at[:, here[1]], refs.spread.at[:, here[1]], move))
            own.wait()
            for copy in last:
                copy.wait_recv()
        if table:
            last = [
                pltpu.make_async_remote_copy(
                    src_ref=source,
                    dst_ref=target,
                    send_sem=refs.spread_send.at[slot + move],
                    recv_sem=refs.spread_recv.at[slot + move],
                    device_id=peer_of(dims, here, dim, move),
                    device_id_type=MESH,
                )
                for source, target, move in table
            ]
            slot += sizes[dim]
            spread += last
        for copy in copies + (last if table else []):
            copy.start()
        for copy in copies:
            copy.wait_recv()
        value = refs.shared[step]
        for move in range(1, sizes[dim]):
            value = value + refs.shared_came[step, move - 1]
        refs.shared[step + 1] = value
        spread += copies
    for copy in last:
        copy.wait_recv()
    refs.sums[...] = refs.shared[4]
    for copy in spread:
        copy.wait_send()


def backward_all(dims, layers, share, lines, norms, weights, saved, near, logit_width):
    sizes = tuple(size for axis, size, stride in dims)
    spots = sizes[0] * sizes[1]
    order = [(kind, layer) for layer in reversed(range(layers)) for kind in (CONTRACT, EXPAND, ATTEND)]
    depth, square = weights[order[0]].shape[-2:]
    model = depth * sizes[2] * sizes[3]
    chunks = [((HEAD, 0), depth, logit_width, False)]
    chunks += [(name, depth, square, name[0] == ATTEND) for name in order]
    chunks += [((TABLE, 0), lines, model, True)]
    reducer = Reducer(dims, chunks, reduce_cuts)
    parts = Parts()
    parts.put(True, **near)
    for name in order:
        parts.put(key=name, weight=weights[name])
    parts.put(**saved)
    for name, height, across, wide in chunks:
        parts.out(full, True, key=name, total=(height, across))
    parts.out(full, True, spread=(sizes[0], sizes[1], lines, model), sums=(16, 128))
    reducer.declare(parts)
    largest = max(sizes)
    dma = pltpu.SemaphoreType.DMA
    parts.keep(
        slots=pltpu.VMEM((len(order), *sizes, depth, square), low),
        head_blocks=pltpu.VMEM((*sizes, depth, logit_width), low),
        weight_sem=dma((len(order),)),
        mlp_sem=dma((4,)),
        attend_sem=dma((4,)),
        grad=pltpu.VMEM((TOKENS, model), full),
        grad_normed=pltpu.VMEM((TOKENS, model), full),
        grad_low=pltpu.VMEM((TOKENS, model), low),
        turned=pltpu.VMEM((model, TOKENS), low),
        turned_two=pltpu.VMEM((model, TOKENS), low),
        grad_hidden=pltpu.VMEM((spots, TOKENS, square), low),
        norm_grads=pltpu.VMEM((16, model), full),
        shared=pltpu.VMEM((5, 16, 128), full),
        shared_came=pltpu.VMEM((4, largest, 16, 128), full),
        shared_send=dma((4, largest)),
        shared_recv=dma((4, largest)),
        spread_send=dma((2 * largest,)),
        spread_recv=dma((2 * largest,)),
        spread_own=dma,
    )
    for name, value in saved.items():
        parts.keep(**{"near_" + name: pltpu.VMEM(value.shape[1:], value.dtype)})
    body = functools.partial(
        backward_kernel, dims, reducer, layers, share, HEADS // spots, model // HEADS, norms
    )
    return parts.call(body, 1)


def adam_kernel(layers, share, norms, part, refs):
    norm = jnp.sqrt(jnp.sum(refs.sums[:8]))
    factor = clip_limit / jnp.maximum(norm, clip_limit)
    refs.results[...] = jnp.concatenate(
        [jnp.full((8, 128), norm), jnp.full((8, 128), jnp.sum(refs.sums[8:]))], axis=0
    )

    def update(name, spot, gradient, rate_here, decay_here):
        found = adam_step(
            refs.weight[name][spot],
            refs.one[name][spot],
            refs.two[name][spot],
            gradient,
            factor,
            rate_here,
            decay_here,
        )
        for target, value in zip((refs.new_weight, refs.new_one, refs.new_two), found):
            target[name][spot] = value

    for layer in range(layers):
        attend = refs.total[(ATTEND, layer)]
        for at in range(3):
            update(0, (layer, at), attend[:, at * part : (at + 1) * part], matrix_rate, weight_decay)
        update(1, layer, attend[:, 3 * part :].T, matrix_rate, weight_decay)
        update(2, layer, refs.total[(EXPAND, layer)][...], matrix_rate, weight_decay)
        update(3, layer, refs.total[(CONTRACT, layer)][...], matrix_rate, weight_decay)
    for spot in range(refs.spread.shape[0]):
        update(4, pl.ds(spot * share, share), refs.spread[spot, :share], embed_rate, weight_decay)
    update(5, slice(None), refs.total[(HEAD, 0)][...], matrix_rate, weight_decay)
    depth = refs.weight[6].shape[2]
    for at in range(norms):
        line = refs.spread[0, share + at : share + at + 1]
        for kind in range(2):
            update(6, (at, pl.ds(kind, 1)), line[:, kind * 128 : kind * 128 + depth], vector_rate, 0.0)


def adam_all(layers, share, norms, found, params, moments_one, moments_two):
    parts = Parts()
    parts.put(True, sums=found.sums, spread=found.spread.reshape(-1, *found.spread.shape[2:]))
    for name, value in found.total.items():
        parts.put(True, key=name, total=value)
    for at in range(7):
        parts.put(True, key=at, weight=params[at], one=moments_one[at], two=moments_two[at])
        shape = params[at].shape
        parts.out(full, True, key=at, new_weight=shape, new_one=shape, new_two=shape)
    parts.out(full, True, results=(16, 128))
    return parts.call(functools.partial(adam_kernel, layers, share, norms, params[0].shape[3]))


class Gatherer:
    def __init__(self, dims, shapes):
        self.dims, self.shapes = dims, shapes
        self.sizes = [size for axis, size, stride in dims]
        self.units, self.slots = [], 0
        for chunk, (rows, width) in enumerate(shapes):
            for unit in gather_units(rows):
                found = []
                for row, size, order in unit:
                    found.append((row, size, order, self.slots))
                    self.slots += sum(size - 1 for size in self.sizes)
                self.units.append((chunk, found))

    def declare(self, parts, pieces):
        for at, piece in enumerate(pieces):
            parts.put(key=at, piece=piece)
            parts.out(low, key=at, whole=(*self.sizes, *piece.shape))
        parts.keep(
            send=pltpu.SemaphoreType.DMA((self.slots,)),
            recv=pltpu.SemaphoreType.DMA((self.slots,)),
            own=pltpu.SemaphoreType.DMA((len(pieces),)),
        )

    def bind(self, refs, here):
        self.refs, self.here, self.started = refs, here, []
        self.copies_own = [
            pltpu.make_async_copy(refs.piece[at], refs.whole[at].at[tuple(here)], refs.own.at[at])
            for at in range(len(self.shapes))
        ]
        for copy in self.copies_own:
            copy.start()
        self.ready = set()

    def copies(self, chunk, part, stage):
        row, size, order, slot = part
        dim, done = ORDERS[order][stage], ORDERS[order][:stage]
        slot += sum(self.sizes[at] - 1 for at in done)
        block = self.refs.whole[chunk].at[
            (*[slice(None) if at in done else self.here[at] for at in range(4)], pl.ds(row, size))
        ]
        source = block if stage else self.refs.piece[chunk].at[pl.ds(row, size)]
        return [
            pltpu.make_async_remote_copy(
                src_ref=source,
                dst_ref=block,
                send_sem=self.refs.send.at[slot + move - 1],
                recv_sem=self.refs.recv.at[slot + move - 1],
                device_id=peer_of(self.dims, self.here, dim, move),
                device_id_type=MESH,
            )
            for move in range(1, self.sizes[dim])
        ]

    def tick(self, now):
        for at, (chunk, found) in enumerate(self.units):
            if (now - at) % 2 or not 0 <= now - at <= 8:
                continue
            stage = (now - at) // 2
            for part in found:
                if stage:
                    for copy in self.copies(chunk, part, stage - 1):
                        copy.wait_recv()
            if stage == 1 and chunk not in self.ready:
                self.copies_own[chunk].wait()
                self.ready.add(chunk)
            for part in found:
                if stage < 4:
                    for copy in self.copies(chunk, part, stage):
                        copy.start()
                        self.started.append(copy)

    def complete(self, chunk):
        return max(at for at, (other, found) in enumerate(self.units) if other == chunk) + 8

    def finish(self):
        for copy in self.started:
            copy.wait_send()


def norm_rows(source, gain, offset, target):
    scaling, shift = gain[...], offset[...]

    def step(at, carry):
        rows = pl.ds(pl.multiple_of(at * 16, 16), 16)
        value = source[rows, :]
        centred = value - jnp.mean(value, axis=-1, keepdims=True)
        spread = lax.rsqrt(jnp.mean(centred * centred, axis=-1, keepdims=True) + norm_epsilon)
        target[rows, :] = (centred * spread * scaling + shift).astype(low)
        return carry

    lax.fori_loop(0, source.shape[0] // 16, step, 0)


def heads_forward(joined, heads, width):
    scale = width ** (-0.5)
    known = lax.broadcasted_iota(jnp.int32, (1, TOKENS), 1) < SEQ
    real = lax.broadcasted_iota(jnp.int32, (TOKENS, 1), 0) < SEQ
    found = []
    for head in range(heads):
        query, key, value = [
            joined[:, (at * heads + head) * width : (at * heads + head + 1) * width] for at in range(3)
        ]
        scores = jnp.where(known, matmul_right(query, key) * scale, -1e30)
        top = jnp.max(scores, axis=-1, keepdims=True)
        probs = jnp.exp(scores - top)
        probs = probs * (1.0 / jnp.sum(probs, axis=-1, keepdims=True))
        found.append(jnp.where(real, matmul(probs.astype(low), value), 0.0).astype(low))
    return jnp.concatenate(found, axis=1)


def forward_kernel(dims, gatherer, layers, share, heads, width, norms, refs):
    here = place_of(dims)
    sizes = gatherer.sizes
    spots = sizes[0] * sizes[1]
    part = heads * width
    gatherer.bind(refs, here)
    greet(dims, here)
    clock = [0]

    def run(until):
        while clock[0] <= until:
            gatherer.tick(clock[0])
            clock[0] += 1

    last = len(gatherer.shapes) - 1

    def load(chunk):
        run(gatherer.complete(chunk))
        near = refs.near_head if chunk == last else refs.slots.at[chunk % 3]
        if chunk == 0:
            near = near.at[:, :, :, :, pl.ds(0, gatherer.shapes[0][0])]
        copy = pltpu.make_async_copy(refs.whole[chunk], near, refs.load_sem.at[chunk])
        copy.start()
        copy.wait()
        return near

    def halves(near, step):
        def one(spot, carry):
            outer, pair = spot // sizes[1], spot % sizes[1]
            step(spot, square_block(near[outer, pair]))
            return carry

        lax.fori_loop(0, spots // 2, one, 0)
        run(min(clock[0], gatherer.complete(last)))
        lax.fori_loop(spots // 2, spots, one, 0)

    saves = []

    def save(near, far):
        copy = pltpu.make_async_copy(near, far, refs.save_sem.at[len(saves)])
        copy.start()
        saves.append(copy)

    near = load(0)
    lines = gatherer.shapes[0][0]
    block_rows = sizes[2] * sizes[3] * lines
    stream = refs.near_stream.at[0]
    stream[...] = jnp.zeros_like(stream)

    def table_step(spot, carry):
        column = spot * block_rows + lax.broadcasted_iota(jnp.int32, (TOKENS, block_rows), 1)
        picks = (column == refs.columns[:, 0:1]).astype(full) + (column == refs.columns[:, 1:2]).astype(full)
        stream[...] += matmul(picks.astype(low), square_block(near[spot // sizes[1], spot % sizes[1]]))
        return carry

    lax.fori_loop(0, spots, table_step, 0)
    save(stream, refs.stream.at[0])
    base = share // 16 * 16
    depth = gatherer.shapes[1][0]
    refs.gains[...] = jnp.zeros_like(refs.gains)
    count = jnp.zeros((1, 1), full)
    for far in range(sizes[2]):
        for close in range(sizes[3]):
            at = (far * sizes[3] + close) * depth
            rows = near[0, 0, far, close, base:lines, :256].astype(full)[share - base :]
            for norm in range(norms):
                for kind in range(2):
                    refs.gains[2 * norm + kind : 2 * norm + kind + 1, at : at + depth] = rows[
                        norm : norm + 1, kind * 128 : kind * 128 + depth
                    ]
            count = count + rows[norms : norms + 1, 0:1] * 64.0 + rows[norms : norms + 1, 1:2]
    refs.count[...] = jnp.broadcast_to(count, (8, 128))

    total = refs.running
    for layer in range(layers):
        stream, middle = refs.near_stream.at[layer], refs.near_middle.at[layer]
        gains = [refs.gains.at[pl.ds(4 * layer + at, 1)] for at in range(4)]

        normed = refs.near_normed.at[layer]
        norm_rows(stream, gains[0], gains[1], normed)
        save(normed, refs.normed.at[layer])
        middle[...] = stream[...]

        def attend_step(spot, held):
            joined = matmul(normed[...], held[:, : 3 * part]).astype(low)
            refs.near_joined[layer, spot] = joined
            blended = heads_forward(joined, heads, width)
            refs.near_blended[layer, spot] = blended
            middle[...] += matmul_right(blended, held[:, 3 * part :])

        halves(load(1 + 3 * layer), attend_step)
        save(refs.near_joined.at[layer], refs.joined.at[layer])
        save(refs.near_blended.at[layer], refs.blended.at[layer])
        save(middle, refs.middle.at[layer])
        normed_two = refs.near_normed_two.at[layer]
        norm_rows(middle, gains[2], gains[3], normed_two)
        save(normed_two, refs.normed_two.at[layer])

        def expand_step(spot, held):
            hidden = matmul(normed_two[...], held)
            side = 0.5 * (1.0 + lax.erf(hidden * (0.5**0.5)))
            refs.near_active[layer, spot] = (hidden * side).astype(low)
            refs.near_slope[layer, spot] = side + hidden * jnp.exp(-0.5 * hidden * hidden) * (0.5 / jnp.pi) ** 0.5

        halves(load(2 + 3 * layer), expand_step)
        save(refs.near_active.at[layer], refs.active.at[layer])
        save(refs.near_slope.at[layer], refs.slope.at[layer])
        after = refs.near_stream.at[layer + 1]
        after[...] = middle[...]

        def contract_step(spot, held):
            after[...] += matmul_right(refs.near_active[layer, spot], held)

        halves(load(3 + 3 * layer), contract_step)
        if layer + 1 < layers:
            save(after, refs.stream.at[layer + 1])

    near = load(last)
    top = refs.near_stream.at[layers]
    norm_rows(top, refs.gains.at[pl.ds(4 * layers, 1)], refs.gains.at[pl.ds(4 * layers + 1, 1)], refs.final)
    local = near.shape[-1]
    for spot in range(spots):
        held = square_block(near[spot // sizes[1], spot % sizes[1]])
        refs.logits[:, spot * local : (spot + 1) * local] = matmul(refs.final[...], held)

    def loss_step(at, loss):
        rows = pl.ds(pl.multiple_of(at * 16, 16), 16)
        logits = refs.logits[rows, :]
        columns = refs.columns[rows, :]
        wanted = columns[:, 2:3] == lax.broadcasted_iota(jnp.int32, logits.shape, 1)
        weight = columns[:, 3:4].astype(full)
        peak = jnp.max(logits, axis=-1, keepdims=True)
        raised = jnp.exp(logits - peak)
        raised_sum = jnp.sum(raised, axis=-1, keepdims=True)
        log_total = peak + jnp.log(raised_sum)
        picked = jnp.sum(jnp.where(wanted, logits, 0.0), axis=-1, keepdims=True)
        share_here = jnp.exp(logits - log_total) - wanted.astype(full)
        refs.grad_logits[rows, :] = (share_here * (weight / count)).astype(low)
        return loss + (log_total - picked) * weight

    loss = lax.fori_loop(0, TOKENS // 16, loss_step, jnp.zeros((16, 1), full))
    loss = jnp.sum(loss, axis=0, keepdims=True)
    corner = (lax.broadcasted_iota(jnp.int32, (8, 128), 0) + lax.broadcasted_iota(jnp.int32, (8, 128), 1)) == 0
    refs.loss[...] = jnp.where(corner, jnp.broadcast_to(loss, (8, 128)), 0.0)
    total[...] = jnp.zeros_like(total)
    for spot in range(spots):
        held = square_block(near[spot // sizes[1], spot % sizes[1]])
        total[...] += matmul_right(refs.grad_logits[:, spot * local : (spot + 1) * local], held)
    refs.grad_top[...] = jnp.zeros_like(refs.grad_top)
    norm_back_rows(refs.grad_top, total, top, refs.gains.at[pl.ds(4 * layers, 1)], refs.final_grads, 0)
    for copy in saves:
        copy.wait()
    gatherer.finish()


def forward_all(dims, layers, share, norms, pieces, columns):
    sizes = tuple(size for axis, size, stride in dims)
    spots = sizes[0] * sizes[1]
    shapes = [piece.shape for piece in pieces]
    depth, square = shapes[1]
    model = depth * sizes[2] * sizes[3]
    part = square // 4
    gatherer = Gatherer(dims, shapes)
    parts = Parts()
    gatherer.declare(parts, pieces)
    parts.put(True, columns=columns)
    wide = dict(stream=(layers, TOKENS, model), middle=(layers, TOKENS, model), slope=(layers, spots, TOKENS, square))
    slim = dict(
        normed=(layers, TOKENS, model),
        normed_two=(layers, TOKENS, model),
        joined=(layers, spots, TOKENS, 3 * part),
        blended=(layers, spots, TOKENS, part),
        active=(layers, spots, TOKENS, square),
    )
    parts.out(full, **wide)
    parts.out(low, **slim)
    parts.out(full, True, gains=(16, model), grad_top=(TOKENS, model), final_grads=(2, model), loss=(8, 128), count=(8, 128))
    parts.out(low, True, final=(TOKENS, model), grad_logits=(TOKENS, spots * shapes[-1][1]))
    dma = pltpu.SemaphoreType.DMA
    for name, shape in wide.items():
        more = (layers + 1, *shape[1:]) if shape[1] == TOKENS else shape
        parts.keep(**{"near_" + name: pltpu.VMEM(more, full)})
    for name, shape in slim.items():
        parts.keep(**{"near_" + name: pltpu.VMEM(shape, low)})
    parts.keep(
        slots=pltpu.VMEM((3, *sizes, depth, square), low),
        near_head=pltpu.VMEM((*sizes, *shapes[-1]), low),
        load_sem=dma((len(pieces),)),
        save_sem=dma((8 * layers,)),
        running=pltpu.VMEM((TOKENS, model), full),
        logits=pltpu.VMEM((TOKENS, spots * shapes[-1][1]), full),
    )
    body = functools.partial(forward_kernel, dims, gatherer, layers, share, HEADS // spots, model // HEADS, norms)
    return parts.call(body, 0)


def body(dp, tensor, *args):
    (image_codes, labels, mask_flags), state = args[:3], args[3:]
    params, moments_one, moments_two = state[0::3], state[1::3], state[2::3]
    attend_in, attend_out, expand, contract, embed_table, logit_table, norm_params = params
    dims = factors(dp, tensor)
    sizes = tuple(size for axis, size, stride in dims)
    spots = list(range(tensor))
    own = lax.axis_index("tensor")
    depth = attend_in.shape[1]
    model = depth * dp
    part = attend_in.shape[3]
    norms = norm_params.shape[0]

    share = embed_table.shape[0] // tensor
    lines = -(-(share + norms + 1) // 16) * 16
    embed_own = lax.dynamic_slice_in_dim(embed_table, own * share, share, 0).astype(low)
    norm_lines = jnp.pad(norm_params, ((0, 0), (0, 0), (0, 128 - depth))).reshape(norms, 256)
    count_own = jnp.sum(mask_flags)
    count_line = jnp.stack([count_own // 64, count_own % 64]).astype(full)[None]
    embed_piece = jnp.concatenate(
        [
            embed_own,
            jnp.pad(norm_lines, ((0, 0), (0, model - 256))).astype(low),
            jnp.pad(count_line, ((0, lines - share - norms - 1), (0, model - 2))).astype(low),
        ],
        0,
    )
    pieces = [embed_piece]
    for layer in range(LAYERS):
        planes = attend_in[layer].astype(low)
        pieces += [
            jnp.concatenate([planes[:, 0], planes[:, 1], planes[:, 2], attend_out[layer].astype(low).T], 1),
            expand[layer].astype(low),
            contract[layer].astype(low).T,
        ]
    pieces.append(logit_table.astype(low))

    codes_own = lax.dynamic_slice_in_dim(image_codes, own, 1, 0)[0]
    flags_own = lax.dynamic_slice_in_dim(mask_flags, own, 1, 0)[0]
    label_own = lax.dynamic_slice_in_dim(labels, own, 1, 0)
    padding = TOKENS - SEQ
    row_index = jnp.concatenate([CODES + 1 + label_own, jnp.where(flags_own == 1, CODES, codes_own)])
    place_rows = CODES + 1 + CLASSES + jnp.arange(SEQ, dtype=jnp.int32)
    targets = jnp.pad(codes_own, (1, padding))
    flags = jnp.pad(flags_own, (1, padding))

    def spot_of(rows):
        block, inside = rows // (share * tensor), rows % (share * tensor)
        return (inside // share) * (lines * dp) + block * lines + inside % share

    rows = jnp.pad(jnp.stack([spot_of(row_index), spot_of(place_rows)]), ((0, 0), (0, padding)), constant_values=-1)
    columns = jnp.concatenate([rows, targets[None], flags[None]]).T
    ahead = forward_all(dims, LAYERS, share, norms, pieces, columns)
    kinds = [(kind, layer) for layer in range(LAYERS) for kind in (ATTEND, EXPAND, CONTRACT)]
    found = backward_all(
        dims,
        LAYERS,
        share,
        lines,
        norms,
        {name: ahead.whole[at + 1] for at, name in enumerate(kinds)},
        dict(
            slope=ahead.slope,
            active=ahead.active,
            normed_two=ahead.normed_two,
            middle=ahead.middle,
            joined=ahead.joined,
            blended=ahead.blended,
            normed=ahead.normed,
            stream=ahead.stream,
        ),
        dict(
            rows=rows,
            gains=ahead.gains,
            grad_top=ahead.grad_top,
            final=ahead.final,
            grad_logits=ahead.grad_logits,
            final_grads=ahead.final_grads,
            loss=ahead.loss,
        ),
        logit_table.shape[1],
    )

    def turn(values):
        return [
            values[0].transpose(0, 2, 1, 3),
            values[1],
            values[2],
            values[3].transpose(0, 2, 1),
            *values[4:],
        ]

    new = adam_all(LAYERS, share, norms, found, turn(params), turn(moments_one), turn(moments_two))
    results = []
    for index in range(7):
        for group in (new.new_weight, new.new_one, new.new_two):
            value = group[index]
            results.append(
                value.transpose(0, 2, 1, 3) if index == 0 else value.transpose(0, 2, 1) if index == 3 else value
            )
    return (*results, new.results[8, 0], ahead.count[0, 0], new.results[0, 0])


def solution(mesh):
    dp, tensor = mesh.shape["dp"], mesh.shape["tensor"]
    in_specs = (
        (P("dp", None), P("dp"), P("dp", None))
        + (P(None, "dp", None, "tensor"),) * 3
        + (P(None, "tensor", "dp"),) * 3
        + (P(None, "dp", "tensor"),) * 3
        + (P(None, "tensor", "dp"),) * 3
        + (P("dp", None),) * 3
        + (P("dp", "tensor"),) * 3
        + (P(None, None, "dp"),) * 3
    )

    def either(*args):
        whole_tiles = args[3].shape[1] % 16 == 0 and args[1].shape[0] == tensor
        return body(dp, tensor, *args) if whole_tiles else plain_body(*args)

    return jax.shard_map(
        either,
        mesh=mesh,
        in_specs=in_specs,
        out_specs=in_specs[3:] + (P(), P(), P()),
        check_vma=False,
    )
```

```python
import functools

import jax
import jax.numpy as jnp
from jax import lax
from jax.experimental import pallas as pl
from jax.experimental.pallas import tpu as pltpu
from jax.sharding import PartitionSpec as P

HEADS = 16
CODES = 1024
CLASSES = 1000
LAYERS = 2
STEP = 10
SEQ = 257
ROWS_UP = 16

beta_one = 0.9
beta_two = 0.96
matrix_rate = 0.02
embed_rate = 0.5
vector_rate = 0.25
weight_decay = 0.045
epsilon = 1e-10
clip_limit = 0.02
norm_epsilon = 1e-06
low = jnp.bfloat16
full = jnp.float32


def matmul(left, right):
    return jnp.dot(left, right, preferred_element_type=full)


def matmul_left(left, right):
    return lax.dot_general(left, right, (((0,), (0,)), ((), ())), preferred_element_type=full)


def matmul_right(left, right):
    return lax.dot_general(left, right, (((1,), (1,)), ((), ())), preferred_element_type=full)


def layer_norm(stream, scaling, offset):
    average = jnp.mean(stream, axis=-1, keepdims=True)
    centred = stream - average
    variance = jnp.mean(centred * centred, axis=-1, keepdims=True)
    return centred * lax.rsqrt(variance + norm_epsilon) * scaling + offset


def norm_back(stream, scaling, offset, gradient):
    normed_out, pull = jax.vjp(layer_norm, stream, scaling, offset)
    return pull(gradient)


def gelu_exact(values):
    return jax.nn.gelu(values, approximate=False)


def branch_total(piece_sum):
    return lax.psum(piece_sum.astype(jnp.bfloat16), "tensor").astype(jnp.float32)


def input_total(piece_sum):
    return lax.psum(piece_sum.astype(jnp.bfloat16), "tensor").astype(jnp.float32)


def split_heads(joined, images, head_count):
    head_width = joined.shape[1] // (3 * head_count)
    sections = joined.reshape(images, SEQ, 3, head_count, head_width)
    return (sections[:, :, 0], sections[:, :, 1], sections[:, :, 2], head_width ** (-0.5))


def attend_forward(joined, images, head_count):
    queries, key_rows, values, score_scale = split_heads(joined, images, head_count)
    scores = (
        jnp.einsum("bqhd,bkhd->bhqk", queries, key_rows, preferred_element_type=jnp.float32)
        * score_scale
    )
    peak_value = jnp.max(scores, axis=-1, keepdims=True)
    log_total = peak_value + jnp.log(jnp.sum(jnp.exp(scores - peak_value), axis=-1, keepdims=True))
    attention = jnp.exp(scores - log_total).astype(jnp.bfloat16)
    blended = jnp.einsum("bhqk,bkhd->bqhd", attention, values, preferred_element_type=jnp.float32)
    return (blended.astype(jnp.bfloat16).reshape(joined.shape[0], -1), log_total)


def attend_backward(joined, log_total, grad_blended, images, head_count):
    queries, key_rows, values, score_scale = split_heads(joined, images, head_count)
    scores = (
        jnp.einsum("bqhd,bkhd->bhqk", queries, key_rows, preferred_element_type=jnp.float32)
        * score_scale
    )
    attention = jnp.exp(scores - log_total)
    grad_out = grad_blended.reshape(queries.shape)
    grad_attention = jnp.einsum(
        "bqhd,bkhd->bhqk", grad_out, values, preferred_element_type=jnp.float32
    )
    row_total = jnp.sum(attention * grad_attention, axis=-1, keepdims=True)
    grad_scores = (attention * (grad_attention - row_total)).astype(jnp.bfloat16)
    grad_queries = (
        jnp.einsum("bhqk,bkhd->bqhd", grad_scores, key_rows, preferred_element_type=jnp.float32)
        * score_scale
    )
    grad_keys = (
        jnp.einsum("bhqk,bqhd->bkhd", grad_scores, queries, preferred_element_type=jnp.float32)
        * score_scale
    )
    grad_values = jnp.einsum(
        "bhqk,bqhd->bkhd",
        attention.astype(jnp.bfloat16),
        grad_out,
        preferred_element_type=jnp.float32,
    )
    stacked = jnp.stack([grad_queries, grad_keys, grad_values], axis=2).astype(jnp.bfloat16)
    return stacked.reshape(joined.shape)


def layer_forward(stream, weights, gains, images, head_count):
    w_in, w_out, w_expand, w_contract = weights
    normed = layer_norm(stream, gains[0, 0], gains[0, 1]).astype(jnp.bfloat16)
    joined = matmul(normed, w_in.reshape(w_in.shape[0], -1)).astype(jnp.bfloat16)
    blended, log_total = attend_forward(joined, images, head_count)
    middle = stream + branch_total(matmul(blended, w_out))
    normed_two = layer_norm(middle, gains[1, 0], gains[1, 1]).astype(jnp.bfloat16)
    hidden = matmul(normed_two, w_expand)
    active = gelu_exact(hidden).astype(jnp.bfloat16)
    result = middle + branch_total(matmul(active, w_contract))
    return (
        result,
        (stream, normed, joined, blended, log_total, middle, normed_two, hidden, active),
    )


def layer_backward(gradient, saved, weights, gains, images, head_count):
    w_in, w_out, w_expand, w_contract = weights
    stream, normed, joined, blended, log_total, middle, normed_two, hidden, active = saved
    grad_low = gradient.astype(jnp.bfloat16)
    g_contract = matmul_left(active, grad_low)
    grad_active = matmul_right(grad_low, w_contract)
    gelu_out, gelu_pull = jax.vjp(gelu_exact, hidden)
    grad_hidden = gelu_pull(grad_active)[0].astype(jnp.bfloat16)
    g_expand = matmul_left(normed_two, grad_hidden)
    grad_normed = input_total(matmul_right(grad_hidden, w_expand))
    grad_mid, scale_two, offset_two = norm_back(middle, gains[1, 0], gains[1, 1], grad_normed)
    gradient = gradient + grad_mid
    grad_low = gradient.astype(jnp.bfloat16)
    g_out = matmul_left(blended, grad_low)
    grad_blended = matmul_right(grad_low, w_out).astype(jnp.bfloat16)
    grad_joined = attend_backward(joined, log_total, grad_blended, images, head_count)
    g_in = matmul_left(normed, grad_joined).reshape(w_in.shape)
    grad_normed = input_total(matmul_right(grad_joined, w_in.reshape(w_in.shape[0], -1)))
    grad_first, scale_one, offset_one = norm_back(stream, gains[0, 0], gains[0, 1], grad_normed)
    norm_grads = jnp.stack([jnp.stack([scale_one, offset_one]), jnp.stack([scale_two, offset_two])])
    return (gradient + grad_first, (g_in, g_out, g_expand, g_contract), norm_grads)


def plain_body(
    image_codes,
    labels,
    mask_flags,
    attend_in,
    attend_in_one,
    attend_in_two,
    attend_out,
    attend_out_one,
    attend_out_two,
    expand,
    expand_one,
    expand_two,
    contract,
    contract_one,
    contract_two,
    embed_table,
    embed_one,
    embed_two,
    logit_table,
    logit_one,
    logit_two,
    norm_params,
    norm_one,
    norm_two,
):
    w_in, w_out, w_expand, w_contract, embed_rows, head_table, gains_low = (
        lax.all_gather(attend_in.astype(jnp.bfloat16), "dp", axis=1, tiled=True),
        lax.all_gather(attend_out.astype(jnp.bfloat16), "dp", axis=2, tiled=True),
        lax.all_gather(expand.astype(jnp.bfloat16), "dp", axis=1, tiled=True),
        lax.all_gather(contract.astype(jnp.bfloat16), "dp", axis=2, tiled=True),
        lax.all_gather(embed_table.astype(jnp.bfloat16), "dp", axis=0, tiled=True),
        lax.all_gather(logit_table.astype(jnp.bfloat16), "dp", axis=0, tiled=True),
        lax.all_gather(norm_params.astype(jnp.bfloat16), "dp", axis=2, tiled=True),
    )
    gains = gains_low.astype(jnp.float32)
    images = labels.shape[0]
    head_count = HEADS // lax.axis_size("tensor")
    code_rows = jnp.where(mask_flags == 1, CODES, image_codes)
    row_index = jnp.concatenate([(CODES + 1 + labels)[:, None], code_rows], axis=1).reshape(-1)
    place_rows = jnp.tile(CODES + 1 + CLASSES + jnp.arange(SEQ), images)
    targets = jnp.concatenate([jnp.zeros((images, 1), jnp.int32), image_codes], axis=1).reshape(-1)
    weights_loss = jnp.concatenate(
        [jnp.zeros((images, 1), jnp.float32), mask_flags.astype(jnp.float32)], axis=1
    ).reshape(-1)
    stream = embed_rows[row_index].astype(jnp.float32) + embed_rows[place_rows].astype(jnp.float32)
    saved_all = []
    for layer_index in range(LAYERS):
        weights = (
            w_in[layer_index],
            w_out[layer_index],
            w_expand[layer_index],
            w_contract[layer_index],
        )
        stream, saved = layer_forward(
            stream, weights, gains[2 * layer_index : 2 * layer_index + 2], images, head_count
        )
        saved_all.append(saved)
    final_gain = gains[2 * LAYERS]
    final = layer_norm(stream, final_gain[0], final_gain[1]).astype(jnp.bfloat16)
    logits = matmul(final, head_table)
    local_codes = logits.shape[1]
    col_start = lax.axis_index("tensor") * local_codes
    is_target = (
        targets[:, None] == col_start + jnp.arange(local_codes, dtype=jnp.int32)[None, :]
    ).astype(jnp.float32)
    peak_value = jnp.max(logits, axis=1)
    exp_total = jnp.sum(jnp.exp(logits - peak_value[:, None]), axis=1)
    picked = jnp.sum(is_target * logits, axis=1)
    peak_all = lax.pmax(peak_value, "tensor")
    exp_all, picked_all = lax.psum((exp_total * jnp.exp(peak_value - peak_all), picked), "tensor")
    log_total = peak_all + jnp.log(exp_all)
    loss_terms = (log_total - picked_all) * weights_loss
    loss_sum, token_count = lax.psum((jnp.sum(loss_terms), jnp.sum(weights_loss)), "dp")
    grad_logits = (
        (jnp.exp(logits - log_total[:, None]) - is_target) * (weights_loss / token_count)[:, None]
    ).astype(jnp.bfloat16)
    g_head = matmul_left(final, grad_logits)
    grad_final = input_total(matmul_right(grad_logits, head_table))
    gradient, final_scale, final_offset = norm_back(
        stream, final_gain[0], final_gain[1], grad_final
    )
    layer_grads = [None] * LAYERS
    norm_grads = [None] * LAYERS
    for layer_index in reversed(range(LAYERS)):
        weights = (
            w_in[layer_index],
            w_out[layer_index],
            w_expand[layer_index],
            w_contract[layer_index],
        )
        gradient, found, gain_grads = layer_backward(
            gradient,
            saved_all[layer_index],
            weights,
            gains[2 * layer_index : 2 * layer_index + 2],
            images,
            head_count,
        )
        layer_grads[layer_index] = found
        norm_grads[layer_index] = gain_grads
    g_norms = jnp.concatenate(
        [
            jnp.stack(norm_grads).reshape(2 * LAYERS, 2, -1),
            jnp.stack([final_scale, final_offset])[None],
        ],
        axis=0,
    )
    g_table = jax.ops.segment_sum(
        jnp.concatenate([gradient, gradient], axis=0),
        jnp.concatenate([row_index, place_rows]),
        num_segments=embed_rows.shape[0],
    )
    g_in_all = jnp.stack([found[0] for found in layer_grads])
    g_out_all = jnp.stack([found[1] for found in layer_grads])
    g_expand_all = jnp.stack([found[2] for found in layer_grads])
    g_contract_all = jnp.stack([found[3] for found in layer_grads])
    g_in_all, g_out_all, g_expand_all, g_contract_all, g_table, g_head, g_norms = (
        lax.psum_scatter(g_in_all, "dp", scatter_dimension=1, tiled=True),
        lax.psum_scatter(g_out_all, "dp", scatter_dimension=2, tiled=True),
        lax.psum_scatter(g_expand_all, "dp", scatter_dimension=1, tiled=True),
        lax.psum_scatter(g_contract_all, "dp", scatter_dimension=2, tiled=True),
        lax.psum_scatter(g_table, "dp", scatter_dimension=0, tiled=True),
        lax.psum_scatter(g_head, "dp", scatter_dimension=0, tiled=True),
        lax.psum_scatter(g_norms, "dp", scatter_dimension=2, tiled=True),
    )
    gradients = (g_in_all, g_out_all, g_expand_all, g_contract_all, g_table, g_head, g_norms)
    first_rank = (lax.axis_index("tensor") == 0).astype(jnp.float32)
    split_squares = (
        jnp.sum(g_in_all * g_in_all)
        + jnp.sum(g_out_all * g_out_all)
        + jnp.sum(g_expand_all * g_expand_all)
        + jnp.sum(g_contract_all * g_contract_all)
        + jnp.sum(g_head * g_head)
    )
    shared_squares = jnp.sum(g_table * g_table) + jnp.sum(g_norms * g_norms)
    grad_norm = jnp.sqrt(lax.psum(split_squares + first_rank * shared_squares, ("dp", "tensor")))
    factor = clip_limit / jnp.maximum(grad_norm, clip_limit)
    params = (attend_in, attend_out, expand, contract, embed_table, logit_table, norm_params)
    moments_one = (
        attend_in_one,
        attend_out_one,
        expand_one,
        contract_one,
        embed_one,
        logit_one,
        norm_one,
    )
    moments_two = (
        attend_in_two,
        attend_out_two,
        expand_two,
        contract_two,
        embed_two,
        logit_two,
        norm_two,
    )
    results = []
    for index in range(7):
        rate_here = vector_rate if index == 6 else embed_rate if index == 4 else matrix_rate
        decay_here = 0.0 if index == 6 else weight_decay
        results.extend(
            adam_step(
                params[index],
                moments_one[index],
                moments_two[index],
                gradients[index],
                factor,
                rate_here,
                decay_here,
            )
        )
    return (
        results[0],
        results[1],
        results[2],
        results[3],
        results[4],
        results[5],
        results[6],
        results[7],
        results[8],
        results[9],
        results[10],
        results[11],
        results[12],
        results[13],
        results[14],
        results[15],
        results[16],
        results[17],
        results[18],
        results[19],
        results[20],
        loss_sum,
        token_count,
        grad_norm,
    )


def adam_step(weight, moment_one, moment_two, gradient, factor, rate_here, decay_here):
    gradient = gradient * factor
    moment_one = beta_one * moment_one + (1.0 - beta_one) * gradient
    moment_two = beta_two * moment_two + (1.0 - beta_two) * gradient * gradient
    correct_one = 1.0 - beta_one**STEP
    correct_two = 1.0 - beta_two**STEP
    weight = weight - rate_here * (
        moment_one / correct_one / (jnp.sqrt(moment_two / correct_two) + epsilon)
        + decay_here * weight
    )
    return [weight, moment_one, moment_two]


MESH = pl.DeviceIdType.MESH


def factors(dp, tensor):
    return [("tensor", tensor // 2, 2), ("tensor", 2, 1), ("dp", dp // 2, 2), ("dp", 2, 1)]


OUTER, PAIR, LONG, NEAR = range(4)
ORDERS = {
    "a": (LONG, NEAR, OUTER, PAIR),
    "b": (LONG, OUTER, NEAR, PAIR),
    "d": (OUTER, LONG, NEAR, PAIR),
    "e": (NEAR, LONG, OUTER, PAIR),
}


def place_of(dims):
    return [(lax.axis_index(axis) // stride) % size for axis, size, stride in dims]


def peer_of(dims, here, moved, moves):
    there = list(here)
    for dim, move in zip(moved, moves):
        there[dim] = lax.rem(here[dim] + move, dims[dim][1])
    found = {"dp": 0, "tensor": 0}
    for (axis, size, stride), at in zip(dims, there):
        found[axis] = found[axis] + at * stride
    return (found["dp"], found["tensor"])


def greet(dims, here, planes=False):
    barrier = pltpu.get_barrier_semaphore()
    moves = [((dim,), (move,)) for dim, (axis, size, stride) in enumerate(dims) for move in range(1, size)]
    if planes:
        for pair in ((OUTER, PAIR), (LONG, NEAR)):
            for one in range(1, dims[pair[0]][1]):
                for two in range(1, dims[pair[1]][1]):
                    moves.append((pair, (one, two)))
    for moved, move in moves:
        pl.semaphore_signal(barrier, inc=1, device_id=peer_of(dims, here, moved, move), device_id_type=MESH)
    pl.semaphore_wait(barrier, len(moves))


def gather_units(rows):
    tiles = rows // 16
    if rows % 16 or tiles < 4:
        return [[(0, rows, "a")]]
    if tiles == 6:
        cuts = [[("a", 1), ("b", 1), ("d", 1)], [("a", 1), ("b", 1), ("e", 1)]]
    else:
        cuts = [[("a", 1), ("b", 1)], [("a", 1), ("b", 1), ("d", tiles - 4)]]
    units, row = [], 0
    for cut in cuts:
        unit = []
        for order, count in cut:
            unit.append((row, 16 * count, order))
            row += 16 * count
        units.append(unit)
    return units


TOKENS = -(-SEQ // 16) * 16


class Refs:
    pass


class Parts:
    def __init__(self):
        self.ins, self.outs, self.scratch = [], [], []

    def put(self, near=False, key=None, **named):
        for name, value in named.items():
            space = pltpu.VMEM if near else pl.ANY
            self.ins.append(((name, key), value, pl.BlockSpec(memory_space=space)))

    def out(self, kind, near=False, key=None, **named):
        for name, shape in named.items():
            space = pltpu.VMEM if near else pl.ANY
            self.outs.append(
                ((name, key), jax.ShapeDtypeStruct(shape, kind), pl.BlockSpec(memory_space=space))
            )

    def keep(self, key=None, **named):
        for name, scratch in named.items():
            self.scratch.append(((name, key), scratch))

    def refs(self, refs):
        found = Refs()
        for ((name, key), *rest), ref in zip(self.ins + self.outs + self.scratch, refs):
            if key is None:
                setattr(found, name, ref)
            else:
                found.__dict__.setdefault(name, {})[key] = ref
        return found

    def call(self, body, barrier=None):
        found = pl.pallas_call(
            lambda *refs: body(self.refs(refs)),
            out_shape=[shape for name, shape, spec in self.outs],
            in_specs=[spec for name, value, spec in self.ins],
            out_specs=[spec for name, shape, spec in self.outs],
            scratch_shapes=[scratch for name, scratch in self.scratch],
            compiler_params=pltpu.CompilerParams(
                collective_id=barrier,
                has_side_effects=barrier is not None,
                vmem_limit_bytes=63 * 1024 * 1024,
            ),
        )(*[value for name, value, spec in self.ins])
        return self.refs([None] * len(self.ins) + list(found))


class Reducer:
    def __init__(self, dims, chunks, cuts):
        self.dims, self.chunks = dims, chunks
        self.sizes = [size for axis, size, stride in dims]
        self.units, self.sides, counts = [], set(), {}
        self.slots = 0
        for chunk, (name, rows, width, wide) in enumerate(chunks):
            for unit in cuts(rows, width, wide):
                found = []
                for row, size, order in unit:
                    stages = []
                    for stage in range(4):
                        dim = ORDERS[order][3 - stage]
                        key = (order, stage, size, width, wide)
                        stages.append((dim, key, counts.get(key, 0), self.slots))
                        self.sides.add((key, len(self.units) % 2))
                        counts[key] = counts.get(key, 0) + 1
                        self.slots += self.sizes[dim] - 1
                    found.append((row, size, order, stages, len(self.units) % 2))
                self.units.append((chunk, found))
        self.counts = counts
        self.started, self.busy = {}, {}

    def room(self, key):
        order, stage, size, width, wide = key
        gone = [ORDERS[order][3 - at] for at in range(stage + 1)]
        rest = tuple(self.sizes[dim] for dim in range(4) if dim not in gone)
        return (self.sizes[gone[-1]] - 1, *rest, size, width)

    def declare(self, parts):
        for key, count in self.counts.items():
            order, stage, size, width, wide = key
            kind = full if wide and stage == 3 else low
            parts.out(kind, key=key, came=(count, *self.room(key)))
            parts.keep(key=key, staged=pltpu.VMEM(self.room(key), kind), staged_sem=pltpu.SemaphoreType.DMA)
            for side in range(2):
                if stage == 2 and wide and (key, side) in self.sides:
                    parts.keep(key=(key, side), exact=pltpu.VMEM(self.room(key)[1:], full))
        parts.keep(
            send=pltpu.SemaphoreType.DMA((self.slots,)),
            recv=pltpu.SemaphoreType.DMA((self.slots,)),
            squares=pltpu.VMEM((8, 128), full),
        )

    def bind(self, refs, here, blocks, results):
        self.refs, self.here, self.blocks, self.results = refs, here, blocks, results
        refs.squares[...] = jnp.zeros_like(refs.squares)

    def turn(self, dim, move):
        return lax.rem(self.here[dim] + move, self.sizes[dim]) if move else self.here[dim]

    def block(self, chunk, part, stage, move):
        row, size, order, stages, side = part
        gone = [ORDERS[order][3 - at] for at in range(stage)]
        dim = ORDERS[order][3 - stage]
        spot = [
            self.turn(at, move) if at == dim else (self.here[at] if at in gone else slice(None))
            for at in range(4)
        ]
        return self.blocks[chunk].at[(*spot, pl.ds(row, size))]

    def exact(self, part, stage, move):
        row, size, order, stages, side = part
        left = sorted(ORDERS[order][: 4 - stage])
        dim = ORDERS[order][3 - stage]
        spot = [self.turn(at, move) if at == dim else slice(None) for at in left]
        return self.refs.exact[(stages[stage - 1][1], side)].at[tuple(spot)]

    def copies(self, chunk, part, stage):
        dim, key, count, slot = part[3][stage]
        wide = key[4] and stage == 3
        return [
            pltpu.make_async_remote_copy(
                src_ref=self.exact(part, stage, move) if wide else self.block(chunk, part, stage, move),
                dst_ref=self.refs.came[key].at[count, move - 1],
                send_sem=self.refs.send.at[slot + move - 1],
                recv_sem=self.refs.recv.at[slot + move - 1],
                device_id=peer_of(self.dims, self.here, (dim,), (move,)),
                device_id_type=MESH,
            )
            for move in range(1, self.sizes[dim])
        ]

    def staged(self, part, stage):
        dim, key, count, slot = part[3][stage]
        return pltpu.make_async_copy(
            self.refs.came[key].at[count], self.refs.staged[key], self.refs.staged_sem[key]
        )

    def add(self, chunk, part, stage):
        row, size, order, stages, side = part
        dim, key, count, slot = stages[stage]
        held, came = self.block(chunk, part, stage, 0), self.refs.staged[key]
        if stage == 0:
            total = held[...]
            for move in range(self.sizes[dim] - 1):
                total = total + came[move]
            held[...] = total
            return
        exact = stage == 3 and key[4]
        total = (self.exact(part, stage, 0) if exact else held)[...].astype(full)
        for move in range(self.sizes[dim] - 1):
            total = total + came[move].astype(full)
        if stage < 3 and not (stage == 2 and key[4]):
            held[...] = total.astype(low)
            return
        if stage == 2:
            for copy in self.busy.pop((key, side), []):
                copy.wait_send()
            self.refs.exact[(key, side)][...] = total
            return
        self.results[chunk][pl.ds(row, size), :] = total
        square = total * total
        square = sum(square[at : at + 8] for at in range(0, size, 8))
        self.refs.squares[...] += sum(square[:, at : at + 128] for at in range(0, square.shape[1], 128))

    def tick(self, now):
        work = [
            (at, (now - at) // 2)
            for at in range(len(self.units))
            if (now - at) % 2 == 0 and 0 <= now - at <= 8
        ]
        for at, stage in work:
            chunk, found = self.units[at]
            if stage:
                for part in found:
                    for copy in self.copies(chunk, part, stage - 1):
                        copy.wait_recv()
                    self.staged(part, stage - 1).start()
        for at, stage in work:
            chunk, found = self.units[at]
            for part in found:
                if stage:
                    self.staged(part, stage - 1).wait()
                    self.add(chunk, part, stage - 1)
                if stage < 4:
                    dim, key, count, slot = part[3][stage]
                    copies = self.copies(chunk, part, stage)
                    for copy in copies:
                        copy.start()
                    if key[4] and stage == 3:
                        self.busy[(part[3][2][1], part[4])] = copies
                    else:
                        self.started.setdefault(chunk, []).extend(copies)

    def ticks(self):
        return len(self.units) + 8

    def finish(self):
        for chunk in list(self.started):
            self.release(chunk)
        for copy in sum(self.busy.values(), []):
            copy.wait_send()

    def release(self, chunk):
        for copy in self.started.pop(chunk):
            copy.wait_send()


def reduce_cuts(rows, width, wide):
    tiles = rows // 16
    if width <= 256:
        cuts = [[("a", tiles // 2), ("b", tiles - tiles // 2)]]
    elif wide and tiles == 6:
        cuts = [[("d", 1), ("e", 1), ("a", 1)], [("d", 1), ("e", 1), ("b", 1)]]
    elif tiles == 6:
        cuts = [[("a", 2), ("b", 1)], [("a", 1), ("b", 2)]]
    else:
        cuts = [[("a", 1), ("b", 1)], [("a", 1), ("b", tiles - 3)]]
    units, row = [], 0
    for cut in cuts:
        unit = []
        for order, count in cut:
            unit.append((row, 16 * count, order))
            row += 16 * count
        units.append(unit)
    return units


def norm_back_rows(grad, grad_normed, source, gain, found, row):
    value, up = source[...], grad_normed[...]
    centred = value - jnp.mean(value, axis=-1, keepdims=True)
    spread = lax.rsqrt(jnp.mean(centred * centred, axis=-1, keepdims=True) + norm_epsilon)
    unit = centred * spread
    inner = up * gain[...]
    pulled = spread * (
        inner - jnp.mean(inner, axis=-1, keepdims=True) - unit * jnp.mean(inner * unit, axis=-1, keepdims=True)
    )
    grad[...] = grad[...] + pulled
    found[pl.ds(row, 1), :] = jnp.sum(up * unit, axis=0, keepdims=True)
    found[pl.ds(row + 1, 1), :] = jnp.sum(up, axis=0, keepdims=True)


def square_block(value):
    return value.reshape(-1, value.shape[-1])


HEAD, ATTEND, EXPAND, CONTRACT, TABLE = range(5)


def backward_kernel(dims, reducer, layers, heads, width, refs):
    here = place_of(dims)
    sizes = reducer.sizes
    sides = (sizes[2], sizes[3])
    names = [name for name, rows, across, wide in reducer.chunks]
    spots = sizes[0] * sizes[1]
    part = heads * width

    weights = {
        name: pltpu.make_async_copy(refs.weight[name], refs.slots.at[at], refs.weight_sem.at[at])
        for at, name in enumerate(names[1:-1])
    }
    mlp = (refs.slope, refs.active, refs.normed_two, refs.middle)
    mlp_near = (refs.near_slope, refs.near_active, refs.near_normed_two, refs.near_middle)
    attend = (refs.joined, refs.blended, refs.normed, refs.stream)
    attend_near = (refs.near_joined, refs.near_blended, refs.near_normed, refs.near_stream)

    def fetches(far, near, sem, layer):
        return [
            pltpu.make_async_copy(source.at[layer], target, sem.at[at])
            for at, (source, target) in enumerate(zip(far, near))
        ]

    def mlp_fetches(layer):
        return fetches(mlp, mlp_near, refs.mlp_sem, layer)

    def attend_fetches(layer):
        return fetches(attend, attend_near, refs.attend_sem, layer)

    order = names[1:-1]
    for copy in mlp_fetches(layers - 1):
        copy.start()
    for name in order[:2]:
        weights[name].start()
    for copy in attend_fetches(layers - 1):
        copy.start()
    for name in order[2:]:
        weights[name].start()
    greet(dims, here, True)

    lines = refs.total[(TABLE, 0)].shape[0]
    table_blocks = refs.slots.at[0, :, :, :, :, pl.ds(0, lines)]
    blocks = [refs.head_blocks] + [refs.slots.at[at] for at in range(len(order))] + [table_blocks]
    reducer.bind(refs, here, blocks, [refs.total[name] for name in names])
    clock = [0]

    made = [0]

    def run(count):
        for _ in range(count):
            reducer.tick(clock[0])
            clock[0] += 1

    def done(chunk):
        made[0] += sum(1 for at, found in reducer.units if at == chunk)

    def step(count=1):
        run(min(count, made[0] - clock[0]))

    grad, grad_normed, norm_grads = refs.grad, refs.grad_normed, refs.norm_grads
    gains = refs.gains

    norm_grads[...] = jnp.zeros_like(norm_grads)
    norm_grads[pl.ds(4 * layers, 2), :] = refs.final_grads[...]
    grad[...] = refs.grad_top[...]
    turned = refs.final[...].T
    for spot in range(spots):
        across = refs.grad_logits.shape[1] // spots
        found = matmul(turned, refs.grad_logits[:, spot * across : (spot + 1) * across])
        refs.head_blocks[spot // sizes[1], spot % sizes[1]] = found.astype(low).reshape(*sides, -1, across)
    done(0)
    step()

    for layer in reversed(range(layers)):
        at_contract, at_expand, at_attend = [names.index((kind, layer)) for kind in (CONTRACT, EXPAND, ATTEND)]
        slot_contract, slot_expand, slot_attend = [
            refs.slots.at[at - 1] for at in (at_contract, at_expand, at_attend)
        ]

        for copy in mlp_fetches(layer):
            copy.wait()
        weights[(CONTRACT, layer)].wait()
        refs.grad_low[...] = grad[...].astype(low)
        refs.turned[...] = grad[...].astype(low).T

        def contract_step(spot, carry):
            outer, pair = spot // sizes[1], spot % sizes[1]
            held = square_block(slot_contract[outer, pair])
            pulled = matmul(refs.grad_low[...], held) * refs.near_slope[spot]
            refs.grad_hidden[spot] = pulled.astype(low)
            found = matmul(refs.turned[...], refs.near_active[spot]).astype(low)
            slot_contract[outer, pair] = found.reshape(*sides, -1, found.shape[-1])
            return carry

        lax.fori_loop(0, spots, contract_step, 0)
        done(at_contract)
        step()

        weights[(EXPAND, layer)].wait()
        refs.turned[...] = refs.near_normed_two[...].T
        grad_normed[...] = jnp.zeros_like(grad_normed)

        def expand_step(spot, carry):
            outer, pair = spot // sizes[1], spot % sizes[1]
            held = square_block(slot_expand[outer, pair])
            pulled = refs.grad_hidden[spot]
            grad_normed[...] += matmul_right(pulled, held)
            found = matmul(refs.turned[...], pulled).astype(low)
            slot_expand[outer, pair] = found.reshape(*sides, -1, found.shape[-1])
            return carry

        lax.fori_loop(0, spots, expand_step, 0)
        done(at_expand)
        step()
        norm_back_rows(
            grad, grad_normed, refs.near_middle, gains.at[pl.ds(4 * layer + 2, 1)], norm_grads, 4 * layer + 2
        )
        if layer:
            for copy in mlp_fetches(layer - 1):
                copy.start()

        for copy in attend_fetches(layer):
            copy.wait()
        weights[(ATTEND, layer)].wait()
        refs.grad_low[...] = grad[...].astype(low)
        refs.turned[...] = grad[...].astype(low).T
        refs.turned_two[...] = refs.near_normed[...].T
        grad_normed[...] = jnp.zeros_like(grad_normed)
        known = lax.broadcasted_iota(jnp.int32, (1, TOKENS), 1) < SEQ
        scale = width ** (-0.5)

        def attend_step(spot, carry):
            outer, pair = spot // sizes[1], spot % sizes[1]
            held = square_block(slot_attend[outer, pair])
            up_all = matmul(refs.grad_low[...], held[:, 3 * part :]).astype(low)
            pulled_all = []
            joined = refs.near_joined[spot]
            parts = [[], [], []]
            for head in range(heads):
                query, key, value = [
                    joined[:, (at * heads + head) * width : (at * heads + head + 1) * width] for at in range(3)
                ]
                up = up_all[:, head * width : (head + 1) * width]
                scores = jnp.where(known, matmul_right(query, key) * scale, -1e30)
                top = jnp.max(scores, axis=-1, keepdims=True)
                probs = jnp.exp(scores - top)
                probs = probs * (1.0 / jnp.sum(probs, axis=-1, keepdims=True))
                pulled = matmul_right(up, value)
                total = jnp.sum(probs * pulled, axis=-1, keepdims=True)
                moved = (probs * (pulled - total)).astype(low)
                parts[0].append((matmul(moved, key) * scale).astype(low))
                parts[1].append((matmul_left(moved, query) * scale).astype(low))
                parts[2].append(matmul_left(probs.astype(low), up).astype(low))
            pulled = jnp.concatenate(parts[0] + parts[1] + parts[2], axis=1)
            grad_normed[...] += matmul_right(pulled, held[:, : 3 * part])
            found = jnp.concatenate(
                [
                    matmul(refs.turned_two[...], pulled).astype(low),
                    matmul(refs.turned[...], refs.near_blended[spot]).astype(low),
                ],
                axis=1,
            )
            slot_attend[outer, pair] = found.reshape(*sides, -1, found.shape[-1])
            return carry

        step()
        lax.fori_loop(0, spots // 2, attend_step, 0)
        step()
        lax.fori_loop(spots // 2, spots, attend_step, 0)
        done(at_attend)
        step()
        norm_back_rows(grad, grad_normed, refs.near_stream, gains.at[pl.ds(4 * layer, 1)], norm_grads, 4 * layer)
        if layer:
            for copy in attend_fetches(layer - 1):
                copy.start()

    upper = grad[...].astype(low)
    lower = (grad[...] - upper.astype(full)).astype(low)
    model = grad.shape[1]
    depth = refs.slots.shape[5]
    reducer.release(1)

    def table_step(block, carry):
        outer, pair = block // (sizes[1] * sizes[2] * sizes[3]), (block // (sizes[2] * sizes[3])) % sizes[1]
        far, near = (block // sizes[3]) % sizes[2], block % sizes[3]
        row = block * lines + lax.broadcasted_iota(jnp.int32, (lines, TOKENS), 0)
        picks = (row == refs.rows[0:1, :]).astype(full) + (row == refs.rows[1:2, :]).astype(full)
        picks = picks.astype(low)
        found = matmul(picks, upper) + matmul(picks, lower)
        table_blocks[outer, pair, far, near] = found.astype(low)
        return carry

    lax.fori_loop(0, spots * sizes[2] * sizes[3], table_step, 0)
    run(reducer.ticks() - clock[0])
    finish_sums(dims, here, reducer, refs)
    reducer.finish()


def finish_sums(dims, here, reducer, refs):
    sizes = reducer.sizes
    total = refs.total[(TABLE, 0)]
    own = pltpu.make_async_copy(total, refs.spread.at[here[0], here[1]], refs.spread_own)
    own.start()
    model = total.shape[1]
    refs.shared[0, :8] = refs.squares[...]
    refs.shared[0, 8:16] = refs.loss[...]
    for at in range(model // 128):
        refs.shared[0, 16 * at + 16 : 16 * at + 32] = refs.norm_grads[:, at * 128 : (at + 1) * 128]
    waits = []
    for hop, dims_here in enumerate(((OUTER, PAIR), (LONG, NEAR))):
        copies = []
        for move in range(1, sizes[dims_here[0]] * sizes[dims_here[1]]):
            moves = (move // sizes[dims_here[1]], move % sizes[dims_here[1]])
            sems = (refs.shared_send.at[hop, move - 1], refs.shared_recv.at[hop, move - 1])
            copies.append(
                pltpu.make_async_remote_copy(
                    src_ref=refs.shared.at[hop],
                    dst_ref=refs.shared_came.at[hop, move - 1],
                    send_sem=sems[0],
                    recv_sem=sems[1],
                    device_id=peer_of(dims, here, dims_here, moves),
                    device_id_type=MESH,
                )
            )
        for copy in copies:
            copy.start()
        table = []
        if hop == 0:
            pairs = [(OUTER, move, total, refs.spread.at[here[0], here[1]]) for move in range(1, sizes[OUTER])]
        else:
            beside = refs.spread.at[:, here[1]]
            pairs = [(PAIR, move, beside, beside) for move in range(1, sizes[PAIR])]
        for dim, move, source, target in pairs:
            table.append(
                pltpu.make_async_remote_copy(
                    src_ref=source,
                    dst_ref=target,
                    send_sem=refs.spread_send.at[hop, move - 1],
                    recv_sem=refs.spread_recv.at[hop, move - 1],
                    device_id=peer_of(dims, here, (dim,), (move,)),
                    device_id_type=MESH,
                )
            )
        if hop:
            own.wait()
            for copy in last:
                copy.wait_recv()
        for copy in table:
            copy.start()
        last = table
        value = refs.shared[hop]
        for move, copy in enumerate(copies):
            copy.wait_recv()
            value = value + refs.shared_came[hop, move]
        if hop:
            refs.sums[...] = value
        else:
            refs.shared[1] = value
        waits += copies + table
    for copy in last:
        copy.wait_recv()
    for copy in waits:
        copy.wait_send()


def backward_all(dims, layers, lines, weights, saved, near, logit_width):
    sizes = tuple(size for axis, size, stride in dims)
    spots = sizes[0] * sizes[1]
    order = [(kind, layer) for layer in reversed(range(layers)) for kind in (CONTRACT, EXPAND, ATTEND)]
    depth, square = weights[order[0]].shape[-2:]
    model = depth * sizes[2] * sizes[3]
    chunks = [((HEAD, 0), depth, logit_width, False)]
    chunks += [(name, depth, square, name[0] == ATTEND) for name in order]
    chunks += [((TABLE, 0), lines, model, False)]
    reducer = Reducer(dims, chunks, reduce_cuts)
    parts = Parts()
    parts.put(True, **near)
    for name in order:
        parts.put(key=name, weight=weights[name])
    parts.put(**saved)
    for name, height, across, wide in chunks:
        parts.out(full, True, key=name, total=(height, across))
    tall = 16 * (model // 128 + 1)
    parts.out(full, True, spread=(sizes[0], sizes[1], lines, model), sums=(tall, 128))
    reducer.declare(parts)
    largest = max(sizes[0] * sizes[1], sizes[2] * sizes[3])
    dma = pltpu.SemaphoreType.DMA
    parts.keep(
        slots=pltpu.VMEM((len(order), *sizes, depth, square), low),
        head_blocks=pltpu.VMEM((*sizes, depth, logit_width), low),
        weight_sem=dma((len(order),)),
        mlp_sem=dma((4,)),
        attend_sem=dma((4,)),
        grad=pltpu.VMEM((TOKENS, model), full),
        grad_normed=pltpu.VMEM((TOKENS, model), full),
        grad_low=pltpu.VMEM((TOKENS, model), low),
        turned=pltpu.VMEM((model, TOKENS), low),
        turned_two=pltpu.VMEM((model, TOKENS), low),
        grad_hidden=pltpu.VMEM((spots, TOKENS, square), low),
        norm_grads=pltpu.VMEM((16, model), full),
        shared=pltpu.VMEM((2, tall, 128), full),
        shared_came=pltpu.VMEM((2, largest, tall, 128), full),
        shared_send=dma((2, largest)),
        shared_recv=dma((2, largest)),
        spread_send=dma((2, largest)),
        spread_recv=dma((2, largest)),
        spread_own=dma,
    )
    for name, value in saved.items():
        parts.keep(**{"near_" + name: pltpu.VMEM(value.shape[1:], value.dtype)})
    body = functools.partial(
        backward_kernel, dims, reducer, layers, HEADS // spots, model // HEADS
    )
    return parts.call(body, 1)


def adam_kernel(layers, share, norms, part, refs):
    norm = jnp.sqrt(jnp.sum(refs.sums[:8]) + jnp.sum(refs.sums[16:] * refs.sums[16:]))
    factor = clip_limit / jnp.maximum(norm, clip_limit)
    refs.results[...] = jnp.concatenate(
        [jnp.full((8, 128), norm), jnp.full((8, 128), jnp.sum(refs.sums[8:16])), refs.count[...]], axis=0
    )

    def update(name, spot, gradient, rate_here, decay_here):
        found = adam_step(
            refs.weight[name][spot],
            refs.one[name][spot],
            refs.two[name][spot],
            gradient,
            factor,
            rate_here,
            decay_here,
        )
        for target, value in zip((refs.new_weight, refs.new_one, refs.new_two), found):
            target[name][spot] = value

    for layer in range(layers):
        attend = refs.total[(ATTEND, layer)]
        for at in range(3):
            update(0, (layer, at), attend[:, at * part : (at + 1) * part], matrix_rate, weight_decay)
        update(1, layer, attend[:, 3 * part :].T, matrix_rate, weight_decay)
        update(2, layer, refs.total[(EXPAND, layer)][...], matrix_rate, weight_decay)
        update(3, layer, refs.total[(CONTRACT, layer)][...], matrix_rate, weight_decay)
    for spot in range(refs.spread.shape[0]):
        update(4, pl.ds(spot * share, share), refs.spread[spot, :share], embed_rate, weight_decay)
    update(5, slice(None), refs.total[(HEAD, 0)][...], matrix_rate, weight_decay)
    across = refs.weight[6].shape[2]
    start = lax.axis_index("dp") * across
    lanes = lax.broadcasted_iota(jnp.int32, (refs.spread.shape[2], across), 0)
    own = (lanes == start + lax.broadcasted_iota(jnp.int32, lanes.shape, 1)).astype(full)
    lines = jnp.concatenate([refs.sums[at : at + 16] for at in range(16, refs.sums.shape[0], 16)], axis=1)
    lines = jnp.dot(lines, own, precision=lax.Precision.HIGHEST, preferred_element_type=full)
    for at in range(norms):
        for kind in range(2):
            update(6, (at, pl.ds(kind, 1)), lines[2 * at + kind : 2 * at + kind + 1], vector_rate, 0.0)


def adam_all(layers, share, norms, found, count, params, moments_one, moments_two):
    parts = Parts()
    parts.put(True, count=count, sums=found.sums, spread=found.spread.reshape(-1, *found.spread.shape[2:]))
    for name, value in found.total.items():
        parts.put(True, key=name, total=value)
    for at in range(7):
        parts.put(True, key=at, weight=params[at], one=moments_one[at], two=moments_two[at])
        shape = params[at].shape
        parts.out(full, True, key=at, new_weight=shape, new_one=shape, new_two=shape)
    parts.out(full, True, results=(24, 128))
    return parts.call(functools.partial(adam_kernel, layers, share, norms, params[0].shape[3]))


class Gatherer:
    def __init__(self, dims, shapes):
        self.dims, self.shapes = dims, shapes
        self.sizes = [size for axis, size, stride in dims]
        self.units, self.slots = [], 0
        for chunk, (rows, width) in enumerate(shapes):
            for unit in gather_units(rows):
                found = []
                for row, size, order in unit:
                    found.append((row, size, order, self.slots))
                    self.slots += sum(size - 1 for size in self.sizes)
                self.units.append((chunk, found))

    def declare(self, parts):
        for at, shape in enumerate(self.shapes):
            parts.keep(key=at, piece=pltpu.VMEM(shape, low))
            parts.out(low, key=at, whole=(*self.sizes, *shape))
        parts.keep(
            send=pltpu.SemaphoreType.DMA((self.slots,)),
            recv=pltpu.SemaphoreType.DMA((self.slots,)),
            own=pltpu.SemaphoreType.DMA((len(self.shapes),)),
        )

    def bind(self, refs, here, prepare):
        self.refs, self.here, self.started, self.prepare = refs, here, [], prepare
        self.copies_own = {}
        self.ready = set()

    def copies(self, chunk, part, stage):
        row, size, order, slot = part
        dim, done = ORDERS[order][stage], ORDERS[order][:stage]
        slot += sum(self.sizes[at] - 1 for at in done)
        block = self.refs.whole[chunk].at[
            (*[slice(None) if at in done else self.here[at] for at in range(4)], pl.ds(row, size))
        ]
        source = block if stage else self.refs.piece[chunk].at[pl.ds(row, size)]
        return [
            pltpu.make_async_remote_copy(
                src_ref=source,
                dst_ref=block,
                send_sem=self.refs.send.at[slot + move - 1],
                recv_sem=self.refs.recv.at[slot + move - 1],
                device_id=peer_of(self.dims, self.here, (dim,), (move,)),
                device_id_type=MESH,
            )
            for move in range(1, self.sizes[dim])
        ]

    def tick(self, now):
        for at, (chunk, found) in enumerate(self.units):
            if (now - at) % 2 or not 0 <= now - at <= 8:
                continue
            stage = (now - at) // 2
            for part in found:
                if stage:
                    for copy in self.copies(chunk, part, stage - 1):
                        copy.wait_recv()
            if stage == 0 and chunk not in self.copies_own:
                self.prepare(chunk)
                copy = pltpu.make_async_copy(
                    self.refs.piece[chunk], self.refs.whole[chunk].at[tuple(self.here)], self.refs.own.at[chunk]
                )
                copy.start()
                self.copies_own[chunk] = copy
            if stage == 1 and chunk not in self.ready:
                self.copies_own[chunk].wait()
                self.ready.add(chunk)
            for part in found:
                if stage < 4:
                    for copy in self.copies(chunk, part, stage):
                        copy.start()
                        self.started.append(copy)

    def complete(self, chunk):
        return max(at for at, (other, found) in enumerate(self.units) if other == chunk) + 8

    def finish(self):
        for copy in self.started:
            copy.wait_send()


def norm_rows(source, gain, offset, target):
    value = source[...]
    centred = value - jnp.mean(value, axis=-1, keepdims=True)
    spread = lax.rsqrt(jnp.mean(centred * centred, axis=-1, keepdims=True) + norm_epsilon)
    target[...] = (centred * spread * gain[...] + offset[...]).astype(low)


def heads_forward(joined, heads, width):
    scale = width ** (-0.5)
    known = lax.broadcasted_iota(jnp.int32, (1, TOKENS), 1) < SEQ
    real = lax.broadcasted_iota(jnp.int32, (TOKENS, 1), 0) < SEQ
    found = []
    for head in range(heads):
        query, key, value = [
            joined[:, (at * heads + head) * width : (at * heads + head + 1) * width] for at in range(3)
        ]
        scores = jnp.where(known, matmul_right(query, key) * scale, -1e30)
        top = jnp.max(scores, axis=-1, keepdims=True)
        probs = jnp.exp(scores - top)
        probs = probs * (1.0 / jnp.sum(probs, axis=-1, keepdims=True))
        found.append(jnp.where(real, matmul(probs.astype(low), value), 0.0).astype(low))
    return jnp.concatenate(found, axis=1)


def as_column(row):
    shape = (row.shape[1], row.shape[1])
    same = lax.broadcasted_iota(jnp.int32, shape, 0) == lax.broadcasted_iota(jnp.int32, shape, 1)
    return jnp.sum(jnp.where(same, row, 0.0), axis=1, keepdims=True)


def index_rows(refs, own, share, tensor, dp, lines):
    codes = refs.codes[pl.ds(own, 1), :].astype(full)
    flags = refs.flags[pl.ds(own, 1), :].astype(full)
    lanes = lax.broadcasted_iota(jnp.int32, refs.labels.shape, 1)
    label = jnp.sum(jnp.where(lanes == own, refs.labels[...].astype(full), 0.0), axis=1, keepdims=True)
    padding = jnp.zeros((1, TOKENS - SEQ), full)
    first = jnp.zeros((1, 1), full)
    token = lax.broadcasted_iota(jnp.int32, (1, TOKENS), 1)
    index = jnp.concatenate([label + (CODES + 1.0), jnp.where(flags == 1.0, float(CODES), codes), padding], axis=1)
    places = token.astype(full) + float(CODES + 1 + CLASSES)
    for at, values in enumerate((index, places)):
        block = jnp.floor((values + 0.5) * (1.0 / (share * tensor)))
        inside = values - block * (share * tensor)
        part = jnp.floor((inside + 0.5) * (1.0 / share))
        spot = part * (lines * dp) + block * lines + (inside - part * share)
        spot = jnp.where(token < SEQ, spot, -1.0)
        refs.rows[at : at + 1, :] = spot.astype(jnp.int32)
        refs.columns[:, at : at + 1] = as_column(spot).astype(jnp.int32)
    refs.columns[:, 2:3] = as_column(jnp.concatenate([first, codes, padding], axis=1)).astype(jnp.int32)
    refs.columns[:, 3:4] = as_column(jnp.concatenate([first, flags, padding], axis=1)).astype(jnp.int32)


def table_piece(refs, share, lines):
    norms, kinds, across = refs.norms.shape
    model = refs.table_own.shape[1]
    rows = []
    for norm in range(norms):
        both = refs.norms[norm]
        line = [both[0:1], jnp.zeros((1, 128 - across), full), both[1:2], jnp.zeros((1, model - 128 - across), full)]
        rows.append(jnp.concatenate(line, axis=1))
    masked = jnp.sum(refs.flags[...].astype(full), axis=1, keepdims=True)
    masked = jnp.sum(masked, axis=0, keepdims=True)
    high = jnp.floor(masked * (1.0 / 64.0))
    rows.append(jnp.concatenate([high, masked - high * 64.0, jnp.zeros((1, model - 2), full)], axis=1))
    rows.append(jnp.zeros((lines - share - norms - 1, model), full))
    refs.piece[0][...] = jnp.concatenate([refs.table_own[...]] + rows, axis=0).astype(low)


def forward_kernel(dims, gatherer, layers, share, heads, width, norms, refs):
    here = place_of(dims)
    sizes = gatherer.sizes
    spots = sizes[0] * sizes[1]
    part = heads * width
    last = len(gatherer.shapes) - 1
    lines = gatherer.shapes[0][0]
    own = here[0] * sizes[1] + here[1]
    fetch = pltpu.make_async_copy(
        refs.table.at[pl.ds(pl.multiple_of(own * share, 8), share)], refs.table_own, refs.table_sem
    )
    fetch.start()

    def prepare(chunk):
        piece = refs.piece[chunk]
        layer, kind = (chunk - 1) // 3, (chunk - 1) % 3
        if chunk == 0:
            fetch.wait()
            table_piece(refs, share, lines)
        elif chunk == last:
            piece[...] = refs.logit[...].astype(low)
        elif kind == 0:
            planes = [refs.attend_in[layer, at] for at in range(3)]
            piece[...] = jnp.concatenate(planes + [refs.attend_out[layer].T], axis=1).astype(low)
        else:
            piece[...] = (refs.expand, refs.contract)[kind - 1][layer].astype(low)

    gatherer.bind(refs, here, prepare)
    greet(dims, here)
    clock = [0]

    def run(until):
        while clock[0] <= until:
            gatherer.tick(clock[0])
            clock[0] += 1

    def load(chunk):
        run(gatherer.complete(chunk))
        near = refs.near_head if chunk == last else refs.slots.at[chunk % 3]
        if chunk == 0:
            near = near.at[:, :, :, :, pl.ds(0, gatherer.shapes[0][0])]
        copy = pltpu.make_async_copy(refs.whole[chunk], near, refs.load_sem.at[chunk])
        copy.start()
        copy.wait()
        return near

    def halves(near, step):
        def one(spot, carry):
            outer, pair = spot // sizes[1], spot % sizes[1]
            step(spot, square_block(near[outer, pair]))
            return carry

        lax.fori_loop(0, spots // 2, one, 0)
        run(min(clock[0], gatherer.complete(last)))
        lax.fori_loop(spots // 2, spots, one, 0)

    saves = []

    def save(near, far):
        copy = pltpu.make_async_copy(near, far, refs.save_sem.at[len(saves)])
        copy.start()
        saves.append(copy)

    run(1)
    index_rows(refs, own, share, spots, sizes[2] * sizes[3], lines)
    near = load(0)
    block_rows = sizes[2] * sizes[3] * lines
    stream = refs.near_stream.at[0]
    stream[...] = jnp.zeros_like(stream)

    def table_step(spot, carry):
        column = spot * block_rows + lax.broadcasted_iota(jnp.int32, (TOKENS, block_rows), 1)
        picks = (column == refs.columns[:, 0:1]).astype(full) + (column == refs.columns[:, 1:2]).astype(full)
        stream[...] += matmul(picks.astype(low), square_block(near[spot // sizes[1], spot % sizes[1]]))
        return carry

    lax.fori_loop(0, spots, table_step, 0)
    save(stream, refs.stream.at[0])
    base = share // 16 * 16
    depth = gatherer.shapes[1][0]
    refs.gains[...] = jnp.zeros_like(refs.gains)
    count = jnp.zeros((1, 1), full)
    for far in range(sizes[2]):
        for close in range(sizes[3]):
            at = (far * sizes[3] + close) * depth
            rows = near[0, 0, far, close, base:lines, :256].astype(full)[share - base :]
            for norm in range(norms):
                for kind in range(2):
                    refs.gains[2 * norm + kind : 2 * norm + kind + 1, at : at + depth] = rows[
                        norm : norm + 1, kind * 128 : kind * 128 + depth
                    ]
            count = count + rows[norms : norms + 1, 0:1] * 64.0 + rows[norms : norms + 1, 1:2]
    refs.count[...] = jnp.broadcast_to(count, (8, 128))

    total = refs.running
    for layer in range(layers):
        stream, middle = refs.near_stream.at[layer], refs.near_middle.at[layer]
        gains = [refs.gains.at[pl.ds(4 * layer + at, 1)] for at in range(4)]

        normed = refs.near_normed.at[layer]
        norm_rows(stream, gains[0], gains[1], normed)
        save(normed, refs.normed.at[layer])
        middle[...] = stream[...]

        def attend_step(spot, held):
            joined = matmul(normed[...], held[:, : 3 * part]).astype(low)
            refs.near_joined[layer, spot] = joined
            blended = heads_forward(joined, heads, width)
            refs.near_blended[layer, spot] = blended
            middle[...] += matmul_right(blended, held[:, 3 * part :])

        halves(load(1 + 3 * layer), attend_step)
        save(refs.near_joined.at[layer], refs.joined.at[layer])
        save(refs.near_blended.at[layer], refs.blended.at[layer])
        save(middle, refs.middle.at[layer])
        normed_two = refs.near_normed_two.at[layer]
        norm_rows(middle, gains[2], gains[3], normed_two)
        save(normed_two, refs.normed_two.at[layer])

        def expand_step(spot, held):
            hidden = matmul(normed_two[...], held)
            side = 0.5 * (1.0 + lax.erf(hidden * (0.5**0.5)))
            refs.near_active[layer, spot] = (hidden * side).astype(low)
            refs.near_slope[layer, spot] = side + hidden * jnp.exp(-0.5 * hidden * hidden) * (0.5 / jnp.pi) ** 0.5

        halves(load(2 + 3 * layer), expand_step)
        save(refs.near_active.at[layer], refs.active.at[layer])
        save(refs.near_slope.at[layer], refs.slope.at[layer])
        after = refs.near_stream.at[layer + 1]
        after[...] = middle[...]

        def contract_step(spot, held):
            after[...] += matmul_right(refs.near_active[layer, spot], held)

        halves(load(3 + 3 * layer), contract_step)
        if layer + 1 < layers:
            save(after, refs.stream.at[layer + 1])

    near = load(last)
    top = refs.near_stream.at[layers]
    norm_rows(top, refs.gains.at[pl.ds(4 * layers, 1)], refs.gains.at[pl.ds(4 * layers + 1, 1)], refs.final)
    local = near.shape[-1]
    for spot in range(spots):
        held = square_block(near[spot // sizes[1], spot % sizes[1]])
        refs.logits[:, spot * local : (spot + 1) * local] = matmul(refs.final[...], held)

    def loss_step(at, loss):
        rows = pl.ds(pl.multiple_of(at * 16, 16), 16)
        logits = refs.logits[rows, :]
        columns = refs.columns[rows, :]
        wanted = columns[:, 2:3] == lax.broadcasted_iota(jnp.int32, logits.shape, 1)
        weight = columns[:, 3:4].astype(full)
        peak = jnp.max(logits, axis=-1, keepdims=True)
        raised = jnp.exp(logits - peak)
        raised_sum = jnp.sum(raised, axis=-1, keepdims=True)
        log_total = peak + jnp.log(raised_sum)
        picked = jnp.sum(jnp.where(wanted, logits, 0.0), axis=-1, keepdims=True)
        share_here = jnp.exp(logits - log_total) - wanted.astype(full)
        refs.grad_logits[rows, :] = (share_here * (weight / count)).astype(low)
        return loss + (log_total - picked) * weight

    loss = lax.fori_loop(0, TOKENS // 16, loss_step, jnp.zeros((16, 1), full))
    loss = jnp.sum(loss, axis=0, keepdims=True)
    corner = (lax.broadcasted_iota(jnp.int32, (8, 128), 0) + lax.broadcasted_iota(jnp.int32, (8, 128), 1)) == 0
    refs.loss[...] = jnp.where(corner, jnp.broadcast_to(loss, (8, 128)), 0.0)
    total[...] = jnp.zeros_like(total)
    for spot in range(spots):
        held = square_block(near[spot // sizes[1], spot % sizes[1]])
        total[...] += matmul_right(refs.grad_logits[:, spot * local : (spot + 1) * local], held)
    refs.grad_top[...] = jnp.zeros_like(refs.grad_top)
    norm_back_rows(refs.grad_top, total, top, refs.gains.at[pl.ds(4 * layers, 1)], refs.final_grads, 0)
    for copy in saves:
        copy.wait()
    gatherer.finish()


def forward_all(dims, layers, share, lines, norms, params, codes, labels, flags):
    attend_in, attend_out, expand, contract, table, logit, norm_params = params
    sizes = tuple(size for axis, size, stride in dims)
    spots = sizes[0] * sizes[1]
    depth, square = expand.shape[1:]
    model = depth * sizes[2] * sizes[3]
    part = attend_in.shape[3]
    shapes = [(lines, model)] + [(depth, square)] * (3 * layers) + [logit.shape]
    gatherer = Gatherer(dims, shapes)
    parts = Parts()
    gatherer.declare(parts)
    parts.put(table=table)
    parts.put(True, attend_in=attend_in, attend_out=attend_out, expand=expand, contract=contract)
    parts.put(True, logit=logit, norms=norm_params, codes=codes, labels=labels, flags=flags)
    wide = dict(stream=(layers, TOKENS, model), middle=(layers, TOKENS, model), slope=(layers, spots, TOKENS, square))
    slim = dict(
        normed=(layers, TOKENS, model),
        normed_two=(layers, TOKENS, model),
        joined=(layers, spots, TOKENS, 3 * part),
        blended=(layers, spots, TOKENS, part),
        active=(layers, spots, TOKENS, square),
    )
    parts.out(full, **wide)
    parts.out(low, **slim)
    parts.out(full, True, gains=(16, model), grad_top=(TOKENS, model), final_grads=(2, model), loss=(8, 128), count=(8, 128))
    parts.out(jnp.int32, True, rows=(2, TOKENS))
    parts.out(low, True, final=(TOKENS, model), grad_logits=(TOKENS, spots * shapes[-1][1]))
    dma = pltpu.SemaphoreType.DMA
    for name, shape in wide.items():
        more = (layers + 1, *shape[1:]) if shape[1] == TOKENS else shape
        parts.keep(**{"near_" + name: pltpu.VMEM(more, full)})
    for name, shape in slim.items():
        parts.keep(**{"near_" + name: pltpu.VMEM(shape, low)})
    parts.keep(
        slots=pltpu.VMEM((3, *sizes, depth, square), low),
        near_head=pltpu.VMEM((*sizes, *shapes[-1]), low),
        columns=pltpu.VMEM((TOKENS, 4), jnp.int32),
        table_own=pltpu.VMEM((share, model), full),
        table_sem=dma,
        load_sem=dma((len(shapes),)),
        save_sem=dma((8 * layers,)),
        running=pltpu.VMEM((TOKENS, model), full),
        logits=pltpu.VMEM((TOKENS, spots * shapes[-1][1]), full),
    )
    body = functools.partial(forward_kernel, dims, gatherer, layers, share, HEADS // spots, model // HEADS, norms)
    return parts.call(body, 0)


def body(dp, tensor, *args):
    (image_codes, labels, mask_flags), state = args[:3], args[3:]
    params, moments_one, moments_two = state[0::3], state[1::3], state[2::3]
    attend_in, attend_out, expand, contract, embed_table, logit_table, norm_params = params
    dims = factors(dp, tensor)
    sizes = tuple(size for axis, size, stride in dims)
    spots = list(range(tensor))
    own = lax.axis_index("tensor")
    depth = attend_in.shape[1]
    model = depth * dp
    part = attend_in.shape[3]
    norms = norm_params.shape[0]

    share = embed_table.shape[0] // tensor
    lines = -(-(share + norms + 1) // 16) * 16

    def turn(values):
        return [
            values[0].transpose(0, 2, 1, 3),
            values[1],
            values[2],
            values[3].transpose(0, 2, 1),
            *values[4:],
        ]

    params = turn(params)
    ahead = forward_all(
        dims, LAYERS, share, lines, norms, params, image_codes, labels.reshape(1, -1), mask_flags
    )
    kinds = [(kind, layer) for layer in range(LAYERS) for kind in (ATTEND, EXPAND, CONTRACT)]
    found = backward_all(
        dims,
        LAYERS,
        lines,
        {name: ahead.whole[at + 1] for at, name in enumerate(kinds)},
        dict(
            slope=ahead.slope,
            active=ahead.active,
            normed_two=ahead.normed_two,
            middle=ahead.middle,
            joined=ahead.joined,
            blended=ahead.blended,
            normed=ahead.normed,
            stream=ahead.stream,
        ),
        dict(
            rows=ahead.rows,
            gains=ahead.gains,
            grad_top=ahead.grad_top,
            final=ahead.final,
            grad_logits=ahead.grad_logits,
            final_grads=ahead.final_grads,
            loss=ahead.loss,
        ),
        logit_table.shape[1],
    )

    new = adam_all(LAYERS, share, norms, found, ahead.count, params, turn(moments_one), turn(moments_two))
    results = []
    for index in range(7):
        for group in (new.new_weight, new.new_one, new.new_two):
            value = group[index]
            results.append(
                value.transpose(0, 2, 1, 3) if index == 0 else value.transpose(0, 2, 1) if index == 3 else value
            )
    return (*results, new.results[8, 0], new.results[16, 0], new.results[0, 0])


def solution(mesh):
    dp, tensor = mesh.shape["dp"], mesh.shape["tensor"]
    in_specs = (
        (P("dp", None), P("dp"), P("dp", None))
        + (P(None, "dp", None, "tensor"),) * 3
        + (P(None, "tensor", "dp"),) * 3
        + (P(None, "dp", "tensor"),) * 3
        + (P(None, "tensor", "dp"),) * 3
        + (P("dp", None),) * 3
        + (P("dp", "tensor"),) * 3
        + (P(None, None, "dp"),) * 3
    )

    def either(*args):
        whole_tiles = args[3].shape[1] % 16 == 0 and args[1].shape[0] == tensor
        return body(dp, tensor, *args) if whole_tiles else plain_body(*args)

    return jax.shard_map(
        either,
        mesh=mesh,
        in_specs=in_specs,
        out_specs=in_specs[3:] + (P(), P(), P()),
        check_vma=False,
    )
```

```python
import functools

import jax
import jax.numpy as jnp
from jax import lax
from jax.experimental import pallas as pl
from jax.experimental.pallas import tpu as pltpu
from jax.sharding import PartitionSpec as P

HEADS = 16
CODES = 1024
CLASSES = 1000
LAYERS = 2
STEP = 10
SEQ = 257
ROWS_UP = 16

beta_one = 0.9
beta_two = 0.96
matrix_rate = 0.02
embed_rate = 0.5
vector_rate = 0.25
weight_decay = 0.045
epsilon = 1e-10
clip_limit = 0.02
norm_epsilon = 1e-06
low = jnp.bfloat16
full = jnp.float32


def matmul(left, right):
    return jnp.dot(left, right, preferred_element_type=full)


def matmul_left(left, right):
    return lax.dot_general(left, right, (((0,), (0,)), ((), ())), preferred_element_type=full)


def matmul_right(left, right):
    return lax.dot_general(left, right, (((1,), (1,)), ((), ())), preferred_element_type=full)


def layer_norm(stream, scaling, offset):
    average = jnp.mean(stream, axis=-1, keepdims=True)
    centred = stream - average
    variance = jnp.mean(centred * centred, axis=-1, keepdims=True)
    return centred * lax.rsqrt(variance + norm_epsilon) * scaling + offset


def norm_back(stream, scaling, offset, gradient):
    normed_out, pull = jax.vjp(layer_norm, stream, scaling, offset)
    return pull(gradient)


def gelu_exact(values):
    return jax.nn.gelu(values, approximate=False)


def branch_total(piece_sum):
    return lax.psum(piece_sum.astype(jnp.bfloat16), "tensor").astype(jnp.float32)


def input_total(piece_sum):
    return lax.psum(piece_sum.astype(jnp.bfloat16), "tensor").astype(jnp.float32)


def split_heads(joined, images, head_count):
    head_width = joined.shape[1] // (3 * head_count)
    sections = joined.reshape(images, SEQ, 3, head_count, head_width)
    return (sections[:, :, 0], sections[:, :, 1], sections[:, :, 2], head_width ** (-0.5))


def attend_forward(joined, images, head_count):
    queries, key_rows, values, score_scale = split_heads(joined, images, head_count)
    scores = (
        jnp.einsum("bqhd,bkhd->bhqk", queries, key_rows, preferred_element_type=jnp.float32)
        * score_scale
    )
    peak_value = jnp.max(scores, axis=-1, keepdims=True)
    log_total = peak_value + jnp.log(jnp.sum(jnp.exp(scores - peak_value), axis=-1, keepdims=True))
    attention = jnp.exp(scores - log_total).astype(jnp.bfloat16)
    blended = jnp.einsum("bhqk,bkhd->bqhd", attention, values, preferred_element_type=jnp.float32)
    return (blended.astype(jnp.bfloat16).reshape(joined.shape[0], -1), log_total)


def attend_backward(joined, log_total, grad_blended, images, head_count):
    queries, key_rows, values, score_scale = split_heads(joined, images, head_count)
    scores = (
        jnp.einsum("bqhd,bkhd->bhqk", queries, key_rows, preferred_element_type=jnp.float32)
        * score_scale
    )
    attention = jnp.exp(scores - log_total)
    grad_out = grad_blended.reshape(queries.shape)
    grad_attention = jnp.einsum(
        "bqhd,bkhd->bhqk", grad_out, values, preferred_element_type=jnp.float32
    )
    row_total = jnp.sum(attention * grad_attention, axis=-1, keepdims=True)
    grad_scores = (attention * (grad_attention - row_total)).astype(jnp.bfloat16)
    grad_queries = (
        jnp.einsum("bhqk,bkhd->bqhd", grad_scores, key_rows, preferred_element_type=jnp.float32)
        * score_scale
    )
    grad_keys = (
        jnp.einsum("bhqk,bqhd->bkhd", grad_scores, queries, preferred_element_type=jnp.float32)
        * score_scale
    )
    grad_values = jnp.einsum(
        "bhqk,bqhd->bkhd",
        attention.astype(jnp.bfloat16),
        grad_out,
        preferred_element_type=jnp.float32,
    )
    stacked = jnp.stack([grad_queries, grad_keys, grad_values], axis=2).astype(jnp.bfloat16)
    return stacked.reshape(joined.shape)


def layer_forward(stream, weights, gains, images, head_count):
    w_in, w_out, w_expand, w_contract = weights
    normed = layer_norm(stream, gains[0, 0], gains[0, 1]).astype(jnp.bfloat16)
    joined = matmul(normed, w_in.reshape(w_in.shape[0], -1)).astype(jnp.bfloat16)
    blended, log_total = attend_forward(joined, images, head_count)
    middle = stream + branch_total(matmul(blended, w_out))
    normed_two = layer_norm(middle, gains[1, 0], gains[1, 1]).astype(jnp.bfloat16)
    hidden = matmul(normed_two, w_expand)
    active = gelu_exact(hidden).astype(jnp.bfloat16)
    result = middle + branch_total(matmul(active, w_contract))
    return (
        result,
        (stream, normed, joined, blended, log_total, middle, normed_two, hidden, active),
    )


def layer_backward(gradient, saved, weights, gains, images, head_count):
    w_in, w_out, w_expand, w_contract = weights
    stream, normed, joined, blended, log_total, middle, normed_two, hidden, active = saved
    grad_low = gradient.astype(jnp.bfloat16)
    g_contract = matmul_left(active, grad_low)
    grad_active = matmul_right(grad_low, w_contract)
    gelu_out, gelu_pull = jax.vjp(gelu_exact, hidden)
    grad_hidden = gelu_pull(grad_active)[0].astype(jnp.bfloat16)
    g_expand = matmul_left(normed_two, grad_hidden)
    grad_normed = input_total(matmul_right(grad_hidden, w_expand))
    grad_mid, scale_two, offset_two = norm_back(middle, gains[1, 0], gains[1, 1], grad_normed)
    gradient = gradient + grad_mid
    grad_low = gradient.astype(jnp.bfloat16)
    g_out = matmul_left(blended, grad_low)
    grad_blended = matmul_right(grad_low, w_out).astype(jnp.bfloat16)
    grad_joined = attend_backward(joined, log_total, grad_blended, images, head_count)
    g_in = matmul_left(normed, grad_joined).reshape(w_in.shape)
    grad_normed = input_total(matmul_right(grad_joined, w_in.reshape(w_in.shape[0], -1)))
    grad_first, scale_one, offset_one = norm_back(stream, gains[0, 0], gains[0, 1], grad_normed)
    norm_grads = jnp.stack([jnp.stack([scale_one, offset_one]), jnp.stack([scale_two, offset_two])])
    return (gradient + grad_first, (g_in, g_out, g_expand, g_contract), norm_grads)


def plain_body(
    image_codes,
    labels,
    mask_flags,
    attend_in,
    attend_in_one,
    attend_in_two,
    attend_out,
    attend_out_one,
    attend_out_two,
    expand,
    expand_one,
    expand_two,
    contract,
    contract_one,
    contract_two,
    embed_table,
    embed_one,
    embed_two,
    logit_table,
    logit_one,
    logit_two,
    norm_params,
    norm_one,
    norm_two,
):
    w_in, w_out, w_expand, w_contract, embed_rows, head_table, gains_low = (
        lax.all_gather(attend_in.astype(jnp.bfloat16), "dp", axis=1, tiled=True),
        lax.all_gather(attend_out.astype(jnp.bfloat16), "dp", axis=2, tiled=True),
        lax.all_gather(expand.astype(jnp.bfloat16), "dp", axis=1, tiled=True),
        lax.all_gather(contract.astype(jnp.bfloat16), "dp", axis=2, tiled=True),
        lax.all_gather(embed_table.astype(jnp.bfloat16), "dp", axis=0, tiled=True),
        lax.all_gather(logit_table.astype(jnp.bfloat16), "dp", axis=0, tiled=True),
        lax.all_gather(norm_params.astype(jnp.bfloat16), "dp", axis=2, tiled=True),
    )
    gains = gains_low.astype(jnp.float32)
    images = labels.shape[0]
    head_count = HEADS // lax.axis_size("tensor")
    code_rows = jnp.where(mask_flags == 1, CODES, image_codes)
    row_index = jnp.concatenate([(CODES + 1 + labels)[:, None], code_rows], axis=1).reshape(-1)
    place_rows = jnp.tile(CODES + 1 + CLASSES + jnp.arange(SEQ), images)
    targets = jnp.concatenate([jnp.zeros((images, 1), jnp.int32), image_codes], axis=1).reshape(-1)
    weights_loss = jnp.concatenate(
        [jnp.zeros((images, 1), jnp.float32), mask_flags.astype(jnp.float32)], axis=1
    ).reshape(-1)
    stream = embed_rows[row_index].astype(jnp.float32) + embed_rows[place_rows].astype(jnp.float32)
    saved_all = []
    for layer_index in range(LAYERS):
        weights = (
            w_in[layer_index],
            w_out[layer_index],
            w_expand[layer_index],
            w_contract[layer_index],
        )
        stream, saved = layer_forward(
            stream, weights, gains[2 * layer_index : 2 * layer_index + 2], images, head_count
        )
        saved_all.append(saved)
    final_gain = gains[2 * LAYERS]
    final = layer_norm(stream, final_gain[0], final_gain[1]).astype(jnp.bfloat16)
    logits = matmul(final, head_table)
    local_codes = logits.shape[1]
    col_start = lax.axis_index("tensor") * local_codes
    is_target = (
        targets[:, None] == col_start + jnp.arange(local_codes, dtype=jnp.int32)[None, :]
    ).astype(jnp.float32)
    peak_value = jnp.max(logits, axis=1)
    exp_total = jnp.sum(jnp.exp(logits - peak_value[:, None]), axis=1)
    picked = jnp.sum(is_target * logits, axis=1)
    peak_all = lax.pmax(peak_value, "tensor")
    exp_all, picked_all = lax.psum((exp_total * jnp.exp(peak_value - peak_all), picked), "tensor")
    log_total = peak_all + jnp.log(exp_all)
    loss_terms = (log_total - picked_all) * weights_loss
    loss_sum, token_count = lax.psum((jnp.sum(loss_terms), jnp.sum(weights_loss)), "dp")
    grad_logits = (
        (jnp.exp(logits - log_total[:, None]) - is_target) * (weights_loss / token_count)[:, None]
    ).astype(jnp.bfloat16)
    g_head = matmul_left(final, grad_logits)
    grad_final = input_total(matmul_right(grad_logits, head_table))
    gradient, final_scale, final_offset = norm_back(
        stream, final_gain[0], final_gain[1], grad_final
    )
    layer_grads = [None] * LAYERS
    norm_grads = [None] * LAYERS
    for layer_index in reversed(range(LAYERS)):
        weights = (
            w_in[layer_index],
            w_out[layer_index],
            w_expand[layer_index],
            w_contract[layer_index],
        )
        gradient, found, gain_grads = layer_backward(
            gradient,
            saved_all[layer_index],
            weights,
            gains[2 * layer_index : 2 * layer_index + 2],
            images,
            head_count,
        )
        layer_grads[layer_index] = found
        norm_grads[layer_index] = gain_grads
    g_norms = jnp.concatenate(
        [
            jnp.stack(norm_grads).reshape(2 * LAYERS, 2, -1),
            jnp.stack([final_scale, final_offset])[None],
        ],
        axis=0,
    )
    g_table = jax.ops.segment_sum(
        jnp.concatenate([gradient, gradient], axis=0),
        jnp.concatenate([row_index, place_rows]),
        num_segments=embed_rows.shape[0],
    )
    g_in_all = jnp.stack([found[0] for found in layer_grads])
    g_out_all = jnp.stack([found[1] for found in layer_grads])
    g_expand_all = jnp.stack([found[2] for found in layer_grads])
    g_contract_all = jnp.stack([found[3] for found in layer_grads])
    g_in_all, g_out_all, g_expand_all, g_contract_all, g_table, g_head, g_norms = (
        lax.psum_scatter(g_in_all, "dp", scatter_dimension=1, tiled=True),
        lax.psum_scatter(g_out_all, "dp", scatter_dimension=2, tiled=True),
        lax.psum_scatter(g_expand_all, "dp", scatter_dimension=1, tiled=True),
        lax.psum_scatter(g_contract_all, "dp", scatter_dimension=2, tiled=True),
        lax.psum_scatter(g_table, "dp", scatter_dimension=0, tiled=True),
        lax.psum_scatter(g_head, "dp", scatter_dimension=0, tiled=True),
        lax.psum_scatter(g_norms, "dp", scatter_dimension=2, tiled=True),
    )
    gradients = (g_in_all, g_out_all, g_expand_all, g_contract_all, g_table, g_head, g_norms)
    first_rank = (lax.axis_index("tensor") == 0).astype(jnp.float32)
    split_squares = (
        jnp.sum(g_in_all * g_in_all)
        + jnp.sum(g_out_all * g_out_all)
        + jnp.sum(g_expand_all * g_expand_all)
        + jnp.sum(g_contract_all * g_contract_all)
        + jnp.sum(g_head * g_head)
    )
    shared_squares = jnp.sum(g_table * g_table) + jnp.sum(g_norms * g_norms)
    grad_norm = jnp.sqrt(lax.psum(split_squares + first_rank * shared_squares, ("dp", "tensor")))
    factor = clip_limit / jnp.maximum(grad_norm, clip_limit)
    params = (attend_in, attend_out, expand, contract, embed_table, logit_table, norm_params)
    moments_one = (
        attend_in_one,
        attend_out_one,
        expand_one,
        contract_one,
        embed_one,
        logit_one,
        norm_one,
    )
    moments_two = (
        attend_in_two,
        attend_out_two,
        expand_two,
        contract_two,
        embed_two,
        logit_two,
        norm_two,
    )
    results = []
    for index in range(7):
        rate_here = vector_rate if index == 6 else embed_rate if index == 4 else matrix_rate
        decay_here = 0.0 if index == 6 else weight_decay
        results.extend(
            adam_step(
                params[index],
                moments_one[index],
                moments_two[index],
                gradients[index],
                factor,
                rate_here,
                decay_here,
            )
        )
    return (
        results[0],
        results[1],
        results[2],
        results[3],
        results[4],
        results[5],
        results[6],
        results[7],
        results[8],
        results[9],
        results[10],
        results[11],
        results[12],
        results[13],
        results[14],
        results[15],
        results[16],
        results[17],
        results[18],
        results[19],
        results[20],
        loss_sum,
        token_count,
        grad_norm,
    )


def adam_step(weight, moment_one, moment_two, gradient, factor, rate_here, decay_here):
    gradient = gradient * factor
    moment_one = beta_one * moment_one + (1.0 - beta_one) * gradient
    moment_two = beta_two * moment_two + (1.0 - beta_two) * gradient * gradient
    correct_one = 1.0 - beta_one**STEP
    correct_two = 1.0 - beta_two**STEP
    weight = weight - rate_here * (
        moment_one * (1.0 / correct_one) / (jnp.sqrt(moment_two * (1.0 / correct_two)) + epsilon)
        + decay_here * weight
    )
    return [weight, moment_one, moment_two]


MESH = pl.DeviceIdType.MESH


def factors(dp, tensor):
    return [("tensor", tensor // 2, 2), ("tensor", 2, 1), ("dp", dp // 2, 2), ("dp", 2, 1)]


OUTER, PAIR, LONG, NEAR = range(4)
ORDERS = {
    "a": (LONG, NEAR, OUTER, PAIR),
    "b": (LONG, OUTER, NEAR, PAIR),
    "d": (OUTER, LONG, NEAR, PAIR),
    "e": (NEAR, LONG, OUTER, PAIR),
}


def place_of(dims):
    return [(lax.axis_index(axis) // stride) % size for axis, size, stride in dims]


def peer_of(dims, here, moved, moves):
    there = list(here)
    for dim, move in zip(moved, moves):
        there[dim] = lax.rem(here[dim] + move, dims[dim][1])
    found = {"dp": 0, "tensor": 0}
    for (axis, size, stride), at in zip(dims, there):
        found[axis] = found[axis] + at * stride
    return (found["dp"], found["tensor"])


def greet(dims, here, planes=False):
    barrier = pltpu.get_barrier_semaphore()
    moves = [((dim,), (move,)) for dim, (axis, size, stride) in enumerate(dims) for move in range(1, size)]
    if planes:
        for pair in ((OUTER, PAIR), (LONG, NEAR)):
            for one in range(1, dims[pair[0]][1]):
                for two in range(1, dims[pair[1]][1]):
                    moves.append((pair, (one, two)))
    for moved, move in moves:
        pl.semaphore_signal(barrier, inc=1, device_id=peer_of(dims, here, moved, move), device_id_type=MESH)
    pl.semaphore_wait(barrier, len(moves))


def gather_units(rows):
    tiles = rows // 16
    if rows % 16 or tiles < 4:
        return [[(0, rows, "a")]]
    if tiles == 6:
        cuts = [[("a", 2), ("b", 1), ("d", 1)], [("b", 1), ("e", 1)]]
    else:
        cuts = [[("a", 1), ("b", 1)], [("a", 1), ("b", 1), ("d", tiles - 4)]]
    units, row = [], 0
    for cut in cuts:
        unit = []
        for order, count in cut:
            unit.append((row, 16 * count, order))
            row += 16 * count
        units.append(unit)
    return units


TOKENS = -(-SEQ // 16) * 16


class Refs:
    pass


class Parts:
    def __init__(self):
        self.ins, self.outs, self.scratch = [], [], []

    def put(self, near=False, key=None, **named):
        for name, value in named.items():
            space = pltpu.VMEM if near else pl.ANY
            self.ins.append(((name, key), value, pl.BlockSpec(memory_space=space)))

    def out(self, kind, near=False, key=None, **named):
        for name, shape in named.items():
            space = pltpu.VMEM if near else pl.ANY
            self.outs.append(
                ((name, key), jax.ShapeDtypeStruct(shape, kind), pl.BlockSpec(memory_space=space))
            )

    def keep(self, key=None, **named):
        for name, scratch in named.items():
            self.scratch.append(((name, key), scratch))

    def refs(self, refs):
        found = Refs()
        for ((name, key), *rest), ref in zip(self.ins + self.outs + self.scratch, refs):
            if key is None:
                setattr(found, name, ref)
            else:
                found.__dict__.setdefault(name, {})[key] = ref
        return found

    def call(self, body, barrier=None):
        found = pl.pallas_call(
            lambda *refs: body(self.refs(refs)),
            out_shape=[shape for name, shape, spec in self.outs],
            in_specs=[spec for name, value, spec in self.ins],
            out_specs=[spec for name, shape, spec in self.outs],
            scratch_shapes=[scratch for name, scratch in self.scratch],
            compiler_params=pltpu.CompilerParams(
                collective_id=barrier,
                has_side_effects=barrier is not None,
                vmem_limit_bytes=63 * 1024 * 1024,
            ),
        )(*[value for name, value, spec in self.ins])
        return self.refs([None] * len(self.ins) + list(found))


class Reducer:
    def __init__(self, dims, chunks, cuts):
        self.dims, self.chunks = dims, chunks
        self.sizes = [size for axis, size, stride in dims]
        self.units, self.sides, counts = [], set(), {}
        self.slots = 0
        for chunk, (name, rows, width, wide) in enumerate(chunks):
            for unit in cuts(rows, width, wide):
                found = []
                for row, size, order in unit:
                    stages = []
                    for stage in range(4):
                        dim = ORDERS[order][3 - stage]
                        key = (order, stage, size, width, wide)
                        stages.append((dim, key, counts.get(key, 0), self.slots))
                        self.sides.add((key, len(self.units) % 2))
                        counts[key] = counts.get(key, 0) + 1
                        self.slots += self.sizes[dim] - 1
                    found.append((row, size, order, stages, len(self.units) % 2))
                self.units.append((chunk, found))
        self.counts = counts
        self.started, self.busy = {}, {}

    def room(self, key):
        order, stage, size, width, wide = key
        gone = [ORDERS[order][3 - at] for at in range(stage + 1)]
        rest = tuple(self.sizes[dim] for dim in range(4) if dim not in gone)
        return (self.sizes[gone[-1]] - 1, *rest, size, width)

    def declare(self, parts):
        for key, count in self.counts.items():
            order, stage, size, width, wide = key
            kind = full if wide and stage == 3 else low
            parts.out(kind, key=key, came=(count, *self.room(key)))
            parts.keep(key=key, staged=pltpu.VMEM(self.room(key), kind), staged_sem=pltpu.SemaphoreType.DMA)
            for side in range(2):
                if stage == 2 and wide and (key, side) in self.sides:
                    parts.keep(key=(key, side), exact=pltpu.VMEM(self.room(key)[1:], full))
        parts.keep(
            send=pltpu.SemaphoreType.DMA((self.slots,)),
            recv=pltpu.SemaphoreType.DMA((self.slots,)),
            squares=pltpu.VMEM((8, 128), full),
        )

    def bind(self, refs, here, blocks, results):
        self.refs, self.here, self.blocks, self.results = refs, here, blocks, results
        refs.squares[...] = jnp.zeros_like(refs.squares)

    def turn(self, dim, move):
        return lax.rem(self.here[dim] + move, self.sizes[dim]) if move else self.here[dim]

    def block(self, chunk, part, stage, move):
        row, size, order, stages, side = part
        gone = [ORDERS[order][3 - at] for at in range(stage)]
        dim = ORDERS[order][3 - stage]
        spot = [
            self.turn(at, move) if at == dim else (self.here[at] if at in gone else slice(None))
            for at in range(4)
        ]
        return self.blocks[chunk].at[(*spot, pl.ds(row, size))]

    def exact(self, part, stage, move):
        row, size, order, stages, side = part
        left = sorted(ORDERS[order][: 4 - stage])
        dim = ORDERS[order][3 - stage]
        spot = [self.turn(at, move) if at == dim else slice(None) for at in left]
        return self.refs.exact[(stages[stage - 1][1], side)].at[tuple(spot)]

    def copies(self, chunk, part, stage):
        dim, key, count, slot = part[3][stage]
        wide = key[4] and stage == 3
        return [
            pltpu.make_async_remote_copy(
                src_ref=self.exact(part, stage, move) if wide else self.block(chunk, part, stage, move),
                dst_ref=self.refs.came[key].at[count, move - 1],
                send_sem=self.refs.send.at[slot + move - 1],
                recv_sem=self.refs.recv.at[slot + move - 1],
                device_id=peer_of(self.dims, self.here, (dim,), (move,)),
                device_id_type=MESH,
            )
            for move in range(1, self.sizes[dim])
        ]

    def staged(self, part, stage):
        dim, key, count, slot = part[3][stage]
        return pltpu.make_async_copy(
            self.refs.came[key].at[count], self.refs.staged[key], self.refs.staged_sem[key]
        )

    def add(self, chunk, part, stage):
        row, size, order, stages, side = part
        dim, key, count, slot = stages[stage]
        held, came = self.block(chunk, part, stage, 0), self.refs.staged[key]
        if stage == 0:
            total = held[...]
            for move in range(self.sizes[dim] - 1):
                total = total + came[move]
            held[...] = total
            return
        exact = stage == 3 and key[4]
        total = (self.exact(part, stage, 0) if exact else held)[...].astype(full)
        for move in range(self.sizes[dim] - 1):
            total = total + came[move].astype(full)
        if stage < 3 and not (stage == 2 and key[4]):
            held[...] = total.astype(low)
            return
        if stage == 2:
            for copy in self.busy.pop((key, side), []):
                copy.wait_send()
            self.refs.exact[(key, side)][...] = total
            return
        self.results[chunk][pl.ds(row, size), :] = total
        square = total * total
        square = sum(square[at : at + 8] for at in range(0, size, 8))
        self.refs.squares[...] += sum(square[:, at : at + 128] for at in range(0, square.shape[1], 128))

    def tick(self, now):
        work = [
            (at, (now - at) // 2)
            for at in range(len(self.units))
            if (now - at) % 2 == 0 and 0 <= now - at <= 8
        ]
        for at, stage in work:
            if stage == 0:
                self.send_on(at, stage)
        behind = None
        for at, stage in work:
            if stage:
                chunk, found = self.units[at]
                for part in found:
                    for copy in self.copies(chunk, part, stage - 1):
                        copy.wait_recv()
                    self.staged(part, stage - 1).start()
                if behind:
                    self.send_on(*behind)
                behind = (at, stage)
        if behind:
            self.send_on(*behind)

    def send_on(self, at, stage):
        chunk, found = self.units[at]
        for part in found:
            if stage:
                self.staged(part, stage - 1).wait()
                self.add(chunk, part, stage - 1)
            if stage < 4:
                dim, key, count, slot = part[3][stage]
                copies = self.copies(chunk, part, stage)
                for copy in copies:
                    copy.start()
                if key[4] and stage == 3:
                    self.busy[(part[3][2][1], part[4])] = copies
                else:
                    self.started.setdefault(chunk, []).extend(copies)

    def ticks(self):
        return len(self.units) + 8

    def finish(self):
        for chunk in list(self.started):
            self.release(chunk)
        for copy in sum(self.busy.values(), []):
            copy.wait_send()

    def release(self, chunk):
        for copy in self.started.pop(chunk):
            copy.wait_send()


def reduce_cuts(rows, width, wide):
    tiles = rows // 16
    if width <= 256:
        cuts = [[("a", tiles // 2), ("b", tiles - tiles // 2)]]
    elif wide and tiles == 6:
        cuts = [[("a", 1), ("d", 1), ("e", 1)], [("b", 1), ("d", 1), ("e", 1)]]
    elif tiles == 6:
        cuts = [[("a", 2), ("b", 1)], [("a", 1), ("b", 2)]]
    else:
        cuts = [[("a", 1), ("b", 1), ("e", 1)], [("a", 1), ("b", tiles - 4)]]
    units, row = [], 0
    for cut in cuts:
        unit = []
        for order, count in cut:
            unit.append((row, 16 * count, order))
            row += 16 * count
        units.append(unit)
    return units


def norm_back_rows(grad, grad_normed, source, gain, found, row):
    value, up = source[...], grad_normed[...]
    centred = value - jnp.mean(value, axis=-1, keepdims=True)
    spread = lax.rsqrt(jnp.mean(centred * centred, axis=-1, keepdims=True) + norm_epsilon)
    unit = centred * spread
    inner = up * gain[...]
    pulled = spread * (
        inner - jnp.mean(inner, axis=-1, keepdims=True) - unit * jnp.mean(inner * unit, axis=-1, keepdims=True)
    )
    grad[...] = grad[...] + pulled
    found[pl.ds(row, 1), :] = jnp.sum(up * unit, axis=0, keepdims=True)
    found[pl.ds(row + 1, 1), :] = jnp.sum(up, axis=0, keepdims=True)


def square_block(value):
    return value.reshape(-1, value.shape[-1])


HEAD, ATTEND, EXPAND, CONTRACT, TABLE = range(5)


def backward_kernel(dims, reducer, layers, heads, width, refs):
    here = place_of(dims)
    sizes = reducer.sizes
    sides = (sizes[2], sizes[3])
    names = [name for name, rows, across, wide in reducer.chunks]
    spots = sizes[0] * sizes[1]
    part = heads * width

    weights = {
        name: pltpu.make_async_copy(refs.weight[name], refs.slots.at[at], refs.weight_sem.at[at])
        for at, name in enumerate(names[1:-1])
    }
    mlp = (refs.slope, refs.active, refs.normed_two, refs.middle)
    mlp_near = (refs.near_slope, refs.near_active, refs.near_normed_two, refs.near_middle)
    attend = (refs.joined, refs.blended, refs.normed, refs.stream)
    attend_near = (refs.near_joined, refs.near_blended, refs.near_normed, refs.near_stream)

    def fetches(far, near, sem, layer):
        return [
            pltpu.make_async_copy(source.at[layer], target, sem.at[at])
            for at, (source, target) in enumerate(zip(far, near))
        ]

    def mlp_fetches(layer):
        return fetches(mlp, mlp_near, refs.mlp_sem, layer)

    def attend_fetches(layer):
        return fetches(attend, attend_near, refs.attend_sem, layer)

    order = names[1:-1]
    for copy in mlp_fetches(layers - 1):
        copy.start()
    for name in order[:2]:
        weights[name].start()
    for copy in attend_fetches(layers - 1):
        copy.start()
    for name in order[2:]:
        weights[name].start()
    greet(dims, here, True)

    lines = refs.total[(TABLE, 0)].shape[0]
    table_blocks = refs.slots.at[0, :, :, :, :, pl.ds(0, lines)]
    blocks = [refs.head_blocks] + [refs.slots.at[at] for at in range(len(order))] + [table_blocks]
    reducer.bind(refs, here, blocks, [refs.total[name] for name in names])
    clock = [0]

    made = [0]

    def run(count):
        for _ in range(count):
            reducer.tick(clock[0])
            clock[0] += 1

    def done(chunk):
        made[0] += sum(1 for at, found in reducer.units if at == chunk)

    def step(count=1):
        run(min(count, made[0] - clock[0]))

    grad, grad_normed, norm_grads = refs.grad, refs.grad_normed, refs.norm_grads
    gains = refs.gains

    norm_grads[...] = jnp.zeros_like(norm_grads)
    norm_grads[pl.ds(4 * layers, 2), :] = refs.final_grads[...]
    grad[...] = refs.grad_top[...]
    turned = refs.final[...].T
    for spot in range(spots):
        across = refs.grad_logits.shape[1] // spots
        found = matmul(turned, refs.grad_logits[:, spot * across : (spot + 1) * across])
        refs.head_blocks[spot // sizes[1], spot % sizes[1]] = found.astype(low).reshape(*sides, -1, across)
    done(0)
    step()

    for layer in reversed(range(layers)):
        at_contract, at_expand, at_attend = [names.index((kind, layer)) for kind in (CONTRACT, EXPAND, ATTEND)]
        slot_contract, slot_expand, slot_attend = [
            refs.slots.at[at - 1] for at in (at_contract, at_expand, at_attend)
        ]

        for copy in mlp_fetches(layer):
            copy.wait()
        weights[(CONTRACT, layer)].wait()
        refs.grad_low[...] = grad[...].astype(low)
        refs.turned[...] = grad[...].astype(low).T

        def contract_step(spot, carry):
            outer, pair = spot // sizes[1], spot % sizes[1]
            held = square_block(slot_contract[outer, pair])
            pulled = matmul(refs.grad_low[...], held) * refs.near_slope[spot]
            refs.grad_hidden[spot] = pulled.astype(low)
            found = matmul(refs.turned[...], refs.near_active[spot]).astype(low)
            slot_contract[outer, pair] = found.reshape(*sides, -1, found.shape[-1])
            return carry

        lax.fori_loop(0, spots, contract_step, 0)
        done(at_contract)
        step()

        weights[(EXPAND, layer)].wait()
        refs.turned[...] = refs.near_normed_two[...].T
        grad_normed[...] = jnp.zeros_like(grad_normed)

        def expand_step(spot, carry):
            outer, pair = spot // sizes[1], spot % sizes[1]
            held = square_block(slot_expand[outer, pair])
            pulled = refs.grad_hidden[spot]
            grad_normed[...] += matmul_right(pulled, held)
            found = matmul(refs.turned[...], pulled).astype(low)
            slot_expand[outer, pair] = found.reshape(*sides, -1, found.shape[-1])
            return carry

        lax.fori_loop(0, spots, expand_step, 0)
        done(at_expand)
        step()
        norm_back_rows(
            grad, grad_normed, refs.near_middle, gains.at[pl.ds(4 * layer + 2, 1)], norm_grads, 4 * layer + 2
        )
        if layer:
            for copy in mlp_fetches(layer - 1):
                copy.start()

        for copy in attend_fetches(layer):
            copy.wait()
        weights[(ATTEND, layer)].wait()
        refs.grad_low[...] = grad[...].astype(low)
        refs.turned[...] = grad[...].astype(low).T
        refs.turned_two[...] = refs.near_normed[...].T
        grad_normed[...] = jnp.zeros_like(grad_normed)
        known = lax.broadcasted_iota(jnp.int32, (TOKENS, 1), 0) < SEQ
        scale = width ** (-0.5)

        def attend_step(spot, carry):
            outer, pair = spot // sizes[1], spot % sizes[1]
            held = square_block(slot_attend[outer, pair])
            up_all = matmul(refs.grad_low[...], held[:, 3 * part :]).astype(low)
            pulled_all = []
            joined = refs.near_joined[spot]
            parts = [[], [], []]
            for head in range(heads):
                query, key, value = [
                    joined[:, (at * heads + head) * width : (at * heads + head + 1) * width] for at in range(3)
                ]
                up = up_all[:, head * width : (head + 1) * width]
                scores = jnp.where(known, matmul_right(key, query) * scale, -1e30)
                probs = jnp.exp(scores - jnp.max(scores, axis=0, keepdims=True))
                probs = probs * (1.0 / jnp.sum(probs, axis=0, keepdims=True))
                pulled = matmul_right(value, up)
                total = jnp.sum(probs * pulled, axis=0, keepdims=True)
                moved = (probs * (pulled - total)).astype(low)
                parts[0].append((matmul_left(moved, key) * scale).astype(low))
                parts[1].append((matmul(moved, query) * scale).astype(low))
                parts[2].append(matmul(probs.astype(low), up).astype(low))
            pulled = jnp.concatenate(parts[0] + parts[1] + parts[2], axis=1)
            grad_normed[...] += matmul_right(pulled, held[:, : 3 * part])
            found = jnp.concatenate(
                [
                    matmul(refs.turned_two[...], pulled).astype(low),
                    matmul(refs.turned[...], refs.near_blended[spot]).astype(low),
                ],
                axis=1,
            )
            slot_attend[outer, pair] = found.reshape(*sides, -1, found.shape[-1])
            return carry

        step()
        lax.fori_loop(0, spots // 2, attend_step, 0)
        step()
        lax.fori_loop(spots // 2, spots, attend_step, 0)
        done(at_attend)
        step()
        norm_back_rows(grad, grad_normed, refs.near_stream, gains.at[pl.ds(4 * layer, 1)], norm_grads, 4 * layer)
        if layer:
            for copy in attend_fetches(layer - 1):
                copy.start()

    upper = grad[...].astype(low)
    lower = (grad[...] - upper.astype(full)).astype(low)
    model = grad.shape[1]
    depth = refs.slots.shape[5]
    reducer.release(1)

    def table_step(spot, carry):
        height = sizes[2] * sizes[3] * lines
        row = spot * height + lax.broadcasted_iota(jnp.int32, (height, TOKENS), 0)
        picks = (row == refs.rows[0:1, :]).astype(full) + (row == refs.rows[1:2, :]).astype(full)
        picks = picks.astype(low)
        found = (matmul(picks, upper) + matmul(picks, lower)).astype(low)
        table_blocks[spot // sizes[1], spot % sizes[1]] = found.reshape(*sides, lines, model)
        return carry

    lax.fori_loop(0, spots, table_step, 0)
    done(len(names) - 1)
    run(reducer.ticks() - clock[0])
    finish_sums(dims, here, reducer, refs)
    reducer.finish()


def finish_sums(dims, here, reducer, refs):
    sizes = reducer.sizes
    total = refs.total[(TABLE, 0)]
    refs.total_low[...] = total[...].astype(low)
    own = pltpu.make_async_copy(refs.total_low, refs.spread.at[here[0], here[1]], refs.spread_own)
    own.start()
    model = total.shape[1]
    refs.shared[0, :8] = refs.squares[...]
    refs.shared[0, 8:16] = refs.loss[...]
    for at in range(model // 128):
        refs.shared[0, 16 * at + 16 : 16 * at + 32] = refs.norm_grads[:, at * 128 : (at + 1) * 128]
    waits = []
    for hop, dims_here in enumerate(((OUTER, PAIR), (LONG, NEAR))):
        copies = []
        for move in range(1, sizes[dims_here[0]] * sizes[dims_here[1]]):
            moves = (move // sizes[dims_here[1]], move % sizes[dims_here[1]])
            sems = (refs.shared_send.at[hop, move - 1], refs.shared_recv.at[hop, move - 1])
            copies.append(
                pltpu.make_async_remote_copy(
                    src_ref=refs.shared.at[hop],
                    dst_ref=refs.shared_came.at[hop, move - 1],
                    send_sem=sems[0],
                    recv_sem=sems[1],
                    device_id=peer_of(dims, here, dims_here, moves),
                    device_id_type=MESH,
                )
            )
        for copy in copies:
            copy.start()
        table = []
        if hop == 0:
            pairs = [(OUTER, move, refs.total_low, refs.spread.at[here[0], here[1]]) for move in range(1, sizes[OUTER])]
        else:
            beside = refs.spread.at[:, here[1]]
            pairs = [(PAIR, move, beside, beside) for move in range(1, sizes[PAIR])]
        for dim, move, source, target in pairs:
            table.append(
                pltpu.make_async_remote_copy(
                    src_ref=source,
                    dst_ref=target,
                    send_sem=refs.spread_send.at[hop, move - 1],
                    recv_sem=refs.spread_recv.at[hop, move - 1],
                    device_id=peer_of(dims, here, (dim,), (move,)),
                    device_id_type=MESH,
                )
            )
        if hop:
            own.wait()
            for copy in last:
                copy.wait_recv()
        for copy in table:
            copy.start()
        last = table
        value = refs.shared[hop]
        for move, copy in enumerate(copies):
            copy.wait_recv()
            value = value + refs.shared_came[hop, move]
        if hop:
            refs.sums[...] = value
        else:
            refs.shared[1] = value
        waits += copies + table
    for copy in last:
        copy.wait_recv()
    for copy in waits:
        copy.wait_send()


def backward_all(dims, layers, lines, weights, saved, near, logit_width):
    sizes = tuple(size for axis, size, stride in dims)
    spots = sizes[0] * sizes[1]
    order = [(kind, layer) for layer in reversed(range(layers)) for kind in (CONTRACT, EXPAND, ATTEND)]
    depth, square = weights[order[0]].shape[-2:]
    model = depth * sizes[2] * sizes[3]
    chunks = [((HEAD, 0), depth, logit_width, False)]
    chunks += [(name, depth, square, name[0] == ATTEND) for name in order]
    chunks += [((TABLE, 0), lines, model, False)]
    reducer = Reducer(dims, chunks, reduce_cuts)
    parts = Parts()
    parts.put(True, **near)
    for name in order:
        parts.put(key=name, weight=weights[name])
    parts.put(**saved)
    for name, height, across, wide in chunks:
        parts.out(full, True, key=name, total=(height, across))
    tall = 16 * (model // 128 + 1)
    parts.out(low, True, spread=(sizes[0], sizes[1], lines, model))
    parts.out(full, True, sums=(tall, 128))
    parts.keep(total_low=pltpu.VMEM((lines, model), low))
    reducer.declare(parts)
    largest = max(sizes[0] * sizes[1], sizes[2] * sizes[3])
    dma = pltpu.SemaphoreType.DMA
    parts.keep(
        slots=pltpu.VMEM((len(order), *sizes, depth, square), low),
        head_blocks=pltpu.VMEM((*sizes, depth, logit_width), low),
        weight_sem=dma((len(order),)),
        mlp_sem=dma((4,)),
        attend_sem=dma((4,)),
        grad=pltpu.VMEM((TOKENS, model), full),
        grad_normed=pltpu.VMEM((TOKENS, model), full),
        grad_low=pltpu.VMEM((TOKENS, model), low),
        turned=pltpu.VMEM((model, TOKENS), low),
        turned_two=pltpu.VMEM((model, TOKENS), low),
        grad_hidden=pltpu.VMEM((spots, TOKENS, square), low),
        norm_grads=pltpu.VMEM((16, model), full),
        shared=pltpu.VMEM((2, tall, 128), full),
        shared_came=pltpu.VMEM((2, largest, tall, 128), full),
        shared_send=dma((2, largest)),
        shared_recv=dma((2, largest)),
        spread_send=dma((2, largest)),
        spread_recv=dma((2, largest)),
        spread_own=dma,
    )
    for name, value in saved.items():
        parts.keep(**{"near_" + name: pltpu.VMEM(value.shape[1:], value.dtype)})
    body = functools.partial(
        backward_kernel, dims, reducer, layers, HEADS // spots, model // HEADS
    )
    return parts.call(body, 1)


def adam_kernel(layers, share, norms, part, refs):
    groups = ((refs.weight, refs.new_weight), (refs.one, refs.new_one), (refs.two, refs.new_two))
    order = (2, 3, 0, 1, 4, 5, 6)

    def moves(at, back):
        found = []
        for group, (source, target) in enumerate(groups):
            near, sem = refs.near[(at, group)], refs.sems.at[int(back), at, group]
            ends = (near, target[at]) if back else (source[at], near)
            found.append(pltpu.make_async_copy(*ends, sem))
        return found

    for at in order:
        for copy in moves(at, False):
            copy.start()

    norm = jnp.sqrt(jnp.sum(refs.sums[:8]) + jnp.sum(refs.sums[16:] * refs.sums[16:]))
    factor = clip_limit / jnp.maximum(norm, clip_limit)
    refs.norm[...] = jnp.full((1, 1), norm)
    refs.loss[...] = jnp.full((1, 1), jnp.sum(refs.sums[8:16]))
    refs.masked[...] = refs.count[:1, :1]

    def update(name, spot, gradient, rate_here, decay_here):
        near = [refs.near[(name, group)] for group in range(3)]
        found = adam_step(*[ref[spot] for ref in near], gradient, factor, rate_here, decay_here)
        for target, value in zip(near, found):
            target[spot] = value

    def arrived(name):
        for copy in moves(name, False):
            copy.wait()

    def leave(name):
        for copy in moves(name, True):
            copy.start()

    for name, kind in ((2, EXPAND), (3, CONTRACT)):
        arrived(name)
        for layer in range(layers):
            update(name, layer, refs.total[(kind, layer)][...], matrix_rate, weight_decay)
        leave(name)
    arrived(0)
    for layer in range(layers):
        attend = refs.total[(ATTEND, layer)]
        for at in range(3):
            update(0, (layer, at), attend[:, at * part : (at + 1) * part], matrix_rate, weight_decay)
    leave(0)
    arrived(1)
    for layer in range(layers):
        update(1, layer, refs.total[(ATTEND, layer)][:, 3 * part :].T, matrix_rate, weight_decay)
    leave(1)
    arrived(4)
    for spot in range(refs.spread.shape[0]):
        update(4, pl.ds(spot * share, share), refs.spread[spot].astype(full)[:share], embed_rate, weight_decay)
    leave(4)
    arrived(5)
    update(5, slice(None), refs.total[(HEAD, 0)][...], matrix_rate, weight_decay)
    leave(5)
    arrived(6)
    across = refs.weight[6].shape[2]
    start = lax.axis_index("dp") * across
    lanes = lax.broadcasted_iota(jnp.int32, (refs.spread.shape[2], across), 0)
    own = (lanes == start + lax.broadcasted_iota(jnp.int32, lanes.shape, 1)).astype(full)
    lines = jnp.concatenate([refs.sums[at : at + 16] for at in range(16, refs.sums.shape[0], 16)], axis=1)
    lines = jnp.dot(lines, own, precision=lax.Precision.HIGHEST, preferred_element_type=full)
    for at in range(norms):
        for kind in range(2):
            update(6, (at, pl.ds(kind, 1)), lines[2 * at + kind : 2 * at + kind + 1], vector_rate, 0.0)
    leave(6)
    for at in order:
        for copy in moves(at, True):
            copy.wait()


def adam_all(layers, share, norms, found, count, params, moments_one, moments_two):
    parts = Parts()
    parts.put(True, count=count, sums=found.sums, spread=found.spread.reshape(-1, *found.spread.shape[2:]))
    for name, value in found.total.items():
        parts.put(True, key=name, total=value)
    for at in range(7):
        parts.put(key=at, weight=params[at], one=moments_one[at], two=moments_two[at])
        shape = params[at].shape
        parts.out(full, key=at, new_weight=shape, new_one=shape, new_two=shape)
        for group in range(3):
            parts.keep(key=(at, group), near=pltpu.VMEM(shape, full))
    parts.keep(sems=pltpu.SemaphoreType.DMA((2, 7, 3)))
    parts.out(full, True, norm=(1, 1), loss=(1, 1), masked=(1, 1))
    return parts.call(functools.partial(adam_kernel, layers, share, norms, params[0].shape[3]))


class Gatherer:
    def __init__(self, dims, shapes):
        self.dims, self.shapes = dims, shapes
        self.sizes = [size for axis, size, stride in dims]
        self.units, self.slots = [], 0
        for chunk, (rows, width) in enumerate(shapes):
            for unit in gather_units(rows):
                found = []
                for row, size, order in unit:
                    found.append((row, size, order, self.slots))
                    self.slots += sum(size - 1 for size in self.sizes)
                self.units.append((chunk, found))

    def declare(self, parts):
        for at, shape in enumerate(self.shapes):
            parts.keep(key=at, piece=pltpu.VMEM(shape, low))
            parts.out(low, key=at, whole=(*self.sizes, *shape))
        parts.keep(
            send=pltpu.SemaphoreType.DMA((self.slots,)),
            recv=pltpu.SemaphoreType.DMA((self.slots,)),
            own=pltpu.SemaphoreType.DMA((len(self.shapes),)),
        )

    def bind(self, refs, here, prepare):
        self.refs, self.here, self.started, self.prepare = refs, here, [], prepare
        self.copies_own = {}
        self.ready = set()

    def copies(self, chunk, part, stage):
        row, size, order, slot = part
        dim, done = ORDERS[order][stage], ORDERS[order][:stage]
        slot += sum(self.sizes[at] - 1 for at in done)
        block = self.refs.whole[chunk].at[
            (*[slice(None) if at in done else self.here[at] for at in range(4)], pl.ds(row, size))
        ]
        source = block if stage else self.refs.piece[chunk].at[pl.ds(row, size)]
        return [
            pltpu.make_async_remote_copy(
                src_ref=source,
                dst_ref=block,
                send_sem=self.refs.send.at[slot + move - 1],
                recv_sem=self.refs.recv.at[slot + move - 1],
                device_id=peer_of(self.dims, self.here, (dim,), (move,)),
                device_id_type=MESH,
            )
            for move in range(1, self.sizes[dim])
        ]

    def tick(self, now):
        for at, (chunk, found) in enumerate(self.units):
            if (now - at) % 2 or not 0 <= now - at <= 8:
                continue
            stage = (now - at) // 2
            for part in found:
                if stage:
                    for copy in self.copies(chunk, part, stage - 1):
                        copy.wait_recv()
            if stage == 0 and chunk not in self.copies_own:
                self.prepare(chunk)
                copy = pltpu.make_async_copy(
                    self.refs.piece[chunk], self.refs.whole[chunk].at[tuple(self.here)], self.refs.own.at[chunk]
                )
                copy.start()
                self.copies_own[chunk] = copy
            if stage == 1 and chunk not in self.ready:
                self.copies_own[chunk].wait()
                self.ready.add(chunk)
            for part in found:
                if stage < 4:
                    for copy in self.copies(chunk, part, stage):
                        copy.start()
                        self.started.append(copy)

    def complete(self, chunk):
        return max(at for at, (other, found) in enumerate(self.units) if other == chunk) + 8

    def finish(self):
        for copy in self.started:
            copy.wait_send()


def norm_rows(source, gain, offset, target):
    value = source[...]
    centred = value - jnp.mean(value, axis=-1, keepdims=True)
    spread = lax.rsqrt(jnp.mean(centred * centred, axis=-1, keepdims=True) + norm_epsilon)
    target[...] = (centred * spread * gain[...] + offset[...]).astype(low)


def heads_forward(joined, heads, width):
    scale = width ** (-0.5)
    known = lax.broadcasted_iota(jnp.int32, (TOKENS, 1), 0) < SEQ
    real = lax.broadcasted_iota(jnp.int32, (TOKENS, 1), 0) < SEQ
    found = []
    for head in range(heads):
        query, key, value = [
            joined[:, (at * heads + head) * width : (at * heads + head + 1) * width] for at in range(3)
        ]
        scores = jnp.where(known, matmul_right(key, query) * scale, -1e30)
        probs = jnp.exp(scores - jnp.max(scores, axis=0, keepdims=True))
        probs = probs * (1.0 / jnp.sum(probs, axis=0, keepdims=True))
        found.append(jnp.where(real, matmul_left(probs.astype(low), value), 0.0).astype(low))
    return jnp.concatenate(found, axis=1)


def as_column(row):
    shape = (row.shape[1], row.shape[1])
    same = lax.broadcasted_iota(jnp.int32, shape, 0) == lax.broadcasted_iota(jnp.int32, shape, 1)
    return jnp.sum(jnp.where(same, row, 0.0), axis=1, keepdims=True)


def index_rows(refs, own, share, tensor, dp, lines):
    codes = refs.codes[pl.ds(own, 1), :].astype(full)
    flags = refs.flags[pl.ds(own, 1), :].astype(full)
    lanes = lax.broadcasted_iota(jnp.int32, refs.labels.shape, 1)
    label = jnp.sum(jnp.where(lanes == own, refs.labels[...].astype(full), 0.0), axis=1, keepdims=True)
    padding = jnp.zeros((1, TOKENS - SEQ), full)
    first = jnp.zeros((1, 1), full)
    token = lax.broadcasted_iota(jnp.int32, (1, TOKENS), 1)
    index = jnp.concatenate([label + (CODES + 1.0), jnp.where(flags == 1.0, float(CODES), codes), padding], axis=1)
    places = token.astype(full) + float(CODES + 1 + CLASSES)
    for at, values in enumerate((index, places)):
        block = jnp.floor((values + 0.5) * (1.0 / (share * tensor)))
        inside = values - block * (share * tensor)
        part = jnp.floor((inside + 0.5) * (1.0 / share))
        spot = part * (lines * dp) + block * lines + (inside - part * share)
        spot = jnp.where(token < SEQ, spot, -1.0)
        refs.rows[at : at + 1, :] = spot.astype(jnp.int32)
        refs.columns[:, at : at + 1] = as_column(spot).astype(jnp.int32)
    refs.columns[:, 2:3] = as_column(jnp.concatenate([first, codes, padding], axis=1)).astype(jnp.int32)
    refs.columns[:, 3:4] = as_column(jnp.concatenate([first, flags, padding], axis=1)).astype(jnp.int32)


def table_piece(refs, share, lines):
    norms, kinds, across = refs.norms.shape
    model = refs.table_own.shape[1]
    rows = []
    for norm in range(norms):
        both = refs.norms[norm]
        line = [both[0:1], jnp.zeros((1, 128 - across), full), both[1:2], jnp.zeros((1, model - 128 - across), full)]
        rows.append(jnp.concatenate(line, axis=1))
    masked = jnp.sum(refs.flags[...].astype(full), axis=1, keepdims=True)
    masked = jnp.sum(masked, axis=0, keepdims=True)
    high = jnp.floor(masked * (1.0 / 64.0))
    rows.append(jnp.concatenate([high, masked - high * 64.0, jnp.zeros((1, model - 2), full)], axis=1))
    rows.append(jnp.zeros((lines - share - norms - 1, model), full))
    refs.piece[0][...] = jnp.concatenate([refs.table_own[...]] + rows, axis=0).astype(low)


def forward_kernel(dims, gatherer, layers, share, heads, width, norms, refs):
    here = place_of(dims)
    sizes = gatherer.sizes
    spots = sizes[0] * sizes[1]
    part = heads * width
    last = len(gatherer.shapes) - 1
    lines = gatherer.shapes[0][0]
    own = here[0] * sizes[1] + here[1]
    fetch = pltpu.make_async_copy(
        refs.table.at[pl.ds(pl.multiple_of(own * share, 8), share)], refs.table_own, refs.table_sem
    )
    fetch.start()

    def prepare(chunk):
        piece = refs.piece[chunk]
        layer, kind = (chunk - 1) // 3, (chunk - 1) % 3
        if chunk == 0:
            fetch.wait()
            table_piece(refs, share, lines)
        elif chunk == last:
            piece[...] = refs.logit[...].astype(low)
        elif kind == 0:
            planes = [refs.attend_in[layer, at] for at in range(3)]
            piece[...] = jnp.concatenate(planes + [refs.attend_out[layer].T], axis=1).astype(low)
        else:
            piece[...] = (refs.expand, refs.contract)[kind - 1][layer].astype(low)

    gatherer.bind(refs, here, prepare)
    greet(dims, here)
    clock = [0]

    def run(until):
        while clock[0] <= until:
            gatherer.tick(clock[0])
            clock[0] += 1

    def load(chunk):
        run(gatherer.complete(chunk))
        near = refs.near_head if chunk == last else refs.slots.at[chunk % 3]
        if chunk == 0:
            near = near.at[:, :, :, :, pl.ds(0, gatherer.shapes[0][0])]
        copy = pltpu.make_async_copy(refs.whole[chunk], near, refs.load_sem.at[chunk])
        copy.start()
        copy.wait()
        return near

    def halves(near, step):
        def one(spot, carry):
            outer, pair = spot // sizes[1], spot % sizes[1]
            step(spot, square_block(near[outer, pair]))
            return carry

        lax.fori_loop(0, spots // 2, one, 0)
        run(min(clock[0], gatherer.complete(last)))
        lax.fori_loop(spots // 2, spots, one, 0)

    saves = []

    def save(near, far):
        copy = pltpu.make_async_copy(near, far, refs.save_sem.at[len(saves)])
        copy.start()
        saves.append(copy)

    run(1)
    index_rows(refs, own, share, spots, sizes[2] * sizes[3], lines)
    near = load(0)
    block_rows = sizes[2] * sizes[3] * lines
    stream = refs.near_stream.at[0]
    stream[...] = jnp.zeros_like(stream)

    def table_step(spot, carry):
        column = spot * block_rows + lax.broadcasted_iota(jnp.int32, (TOKENS, block_rows), 1)
        picks = (column == refs.columns[:, 0:1]).astype(full) + (column == refs.columns[:, 1:2]).astype(full)
        stream[...] += matmul(picks.astype(low), square_block(near[spot // sizes[1], spot % sizes[1]]))
        return carry

    lax.fori_loop(0, spots, table_step, 0)
    save(stream, refs.stream.at[0])
    base = share // 16 * 16
    depth = gatherer.shapes[1][0]
    refs.gains[...] = jnp.zeros_like(refs.gains)
    count = jnp.zeros((1, 1), full)
    for far in range(sizes[2]):
        for close in range(sizes[3]):
            at = (far * sizes[3] + close) * depth
            rows = near[0, 0, far, close, base:lines, :256].astype(full)[share - base :]
            for norm in range(norms):
                for kind in range(2):
                    refs.gains[2 * norm + kind : 2 * norm + kind + 1, at : at + depth] = rows[
                        norm : norm + 1, kind * 128 : kind * 128 + depth
                    ]
            count = count + rows[norms : norms + 1, 0:1] * 64.0 + rows[norms : norms + 1, 1:2]
    refs.count[...] = jnp.broadcast_to(count, (8, 128))

    total = refs.running
    for layer in range(layers):
        stream, middle = refs.near_stream.at[layer], refs.near_middle.at[layer]
        gains = [refs.gains.at[pl.ds(4 * layer + at, 1)] for at in range(4)]

        normed = refs.near_normed.at[layer]
        norm_rows(stream, gains[0], gains[1], normed)
        save(normed, refs.normed.at[layer])
        middle[...] = stream[...]

        def attend_step(spot, held):
            joined = matmul(normed[...], held[:, : 3 * part]).astype(low)
            refs.near_joined[layer, spot] = joined
            blended = heads_forward(joined, heads, width)
            refs.near_blended[layer, spot] = blended
            middle[...] += matmul_right(blended, held[:, 3 * part :])

        halves(load(1 + 3 * layer), attend_step)
        save(refs.near_joined.at[layer], refs.joined.at[layer])
        save(refs.near_blended.at[layer], refs.blended.at[layer])
        save(middle, refs.middle.at[layer])
        normed_two = refs.near_normed_two.at[layer]
        norm_rows(middle, gains[2], gains[3], normed_two)
        save(normed_two, refs.normed_two.at[layer])

        def expand_step(spot, held):
            hidden = matmul(normed_two[...], held)
            side = 0.5 * (1.0 + lax.erf(hidden * (0.5**0.5)))
            refs.near_active[layer, spot] = (hidden * side).astype(low)
            refs.near_slope[layer, spot] = side + hidden * jnp.exp(-0.5 * hidden * hidden) * (0.5 / jnp.pi) ** 0.5

        halves(load(2 + 3 * layer), expand_step)
        save(refs.near_active.at[layer], refs.active.at[layer])
        save(refs.near_slope.at[layer], refs.slope.at[layer])
        after = refs.near_stream.at[layer + 1]
        after[...] = middle[...]

        def contract_step(spot, held):
            after[...] += matmul_right(refs.near_active[layer, spot], held)

        halves(load(3 + 3 * layer), contract_step)
        if layer + 1 < layers:
            save(after, refs.stream.at[layer + 1])

    near = load(last)
    top = refs.near_stream.at[layers]
    norm_rows(top, refs.gains.at[pl.ds(4 * layers, 1)], refs.gains.at[pl.ds(4 * layers + 1, 1)], refs.final)
    local = near.shape[-1]
    for spot in range(spots):
        held = square_block(near[spot // sizes[1], spot % sizes[1]])
        refs.logits[:, spot * local : (spot + 1) * local] = matmul(refs.final[...], held)

    logits = refs.logits[...]
    wanted = refs.columns[:, 2:3] == lax.broadcasted_iota(jnp.int32, logits.shape, 1)
    weight = refs.columns[:, 3:4].astype(full)
    peak = jnp.max(logits, axis=-1, keepdims=True)
    log_total = peak + jnp.log(jnp.sum(jnp.exp(logits - peak), axis=-1, keepdims=True))
    picked = jnp.sum(jnp.where(wanted, logits, 0.0), axis=-1, keepdims=True)
    share_here = jnp.exp(logits - log_total) - wanted.astype(full)
    refs.grad_logits[...] = (share_here * (weight / count)).astype(low)
    loss = jnp.sum((log_total - picked) * weight, axis=0, keepdims=True)
    corner = (lax.broadcasted_iota(jnp.int32, (8, 128), 0) + lax.broadcasted_iota(jnp.int32, (8, 128), 1)) == 0
    refs.loss[...] = jnp.where(corner, jnp.broadcast_to(loss, (8, 128)), 0.0)
    total[...] = jnp.zeros_like(total)
    for spot in range(spots):
        held = square_block(near[spot // sizes[1], spot % sizes[1]])
        total[...] += matmul_right(refs.grad_logits[:, spot * local : (spot + 1) * local], held)
    refs.grad_top[...] = jnp.zeros_like(refs.grad_top)
    norm_back_rows(refs.grad_top, total, top, refs.gains.at[pl.ds(4 * layers, 1)], refs.final_grads, 0)
    for copy in saves:
        copy.wait()
    gatherer.finish()


def forward_all(dims, layers, share, lines, norms, params, codes, labels, flags):
    attend_in, attend_out, expand, contract, table, logit, norm_params = params
    sizes = tuple(size for axis, size, stride in dims)
    spots = sizes[0] * sizes[1]
    depth, square = expand.shape[1:]
    model = depth * sizes[2] * sizes[3]
    part = attend_in.shape[3]
    shapes = [(lines, model)] + [(depth, square)] * (3 * layers) + [logit.shape]
    gatherer = Gatherer(dims, shapes)
    parts = Parts()
    gatherer.declare(parts)
    parts.put(table=table)
    parts.put(True, attend_in=attend_in, attend_out=attend_out, expand=expand, contract=contract)
    parts.put(True, logit=logit, norms=norm_params, codes=codes, labels=labels, flags=flags)
    wide = dict(stream=(layers, TOKENS, model), middle=(layers, TOKENS, model), slope=(layers, spots, TOKENS, square))
    slim = dict(
        normed=(layers, TOKENS, model),
        normed_two=(layers, TOKENS, model),
        joined=(layers, spots, TOKENS, 3 * part),
        blended=(layers, spots, TOKENS, part),
        active=(layers, spots, TOKENS, square),
    )
    parts.out(full, **wide)
    parts.out(low, **slim)
    parts.out(full, True, gains=(16, model), grad_top=(TOKENS, model), final_grads=(2, model), loss=(8, 128), count=(8, 128))
    parts.out(jnp.int32, True, rows=(2, TOKENS))
    parts.out(low, True, final=(TOKENS, model), grad_logits=(TOKENS, spots * shapes[-1][1]))
    dma = pltpu.SemaphoreType.DMA
    for name, shape in wide.items():
        more = (layers + 1, *shape[1:]) if shape[1] == TOKENS else shape
        parts.keep(**{"near_" + name: pltpu.VMEM(more, full)})
    for name, shape in slim.items():
        parts.keep(**{"near_" + name: pltpu.VMEM(shape, low)})
    parts.keep(
        slots=pltpu.VMEM((3, *sizes, depth, square), low),
        near_head=pltpu.VMEM((*sizes, *shapes[-1]), low),
        columns=pltpu.VMEM((TOKENS, 4), jnp.int32),
        table_own=pltpu.VMEM((share, model), full),
        table_sem=dma,
        load_sem=dma((len(shapes),)),
        save_sem=dma((8 * layers,)),
        running=pltpu.VMEM((TOKENS, model), full),
        logits=pltpu.VMEM((TOKENS, spots * shapes[-1][1]), full),
    )
    body = functools.partial(forward_kernel, dims, gatherer, layers, share, HEADS // spots, model // HEADS, norms)
    return parts.call(body, 0)


def body(dp, tensor, *args):
    (image_codes, labels, mask_flags), state = args[:3], args[3:]
    params, moments_one, moments_two = state[0::3], state[1::3], state[2::3]
    attend_in, attend_out, expand, contract, embed_table, logit_table, norm_params = params
    dims = factors(dp, tensor)
    sizes = tuple(size for axis, size, stride in dims)
    spots = list(range(tensor))
    own = lax.axis_index("tensor")
    depth = attend_in.shape[1]
    model = depth * dp
    part = attend_in.shape[3]
    norms = norm_params.shape[0]

    share = embed_table.shape[0] // tensor
    lines = -(-(share + norms + 1) // 16) * 16

    def turn(values):
        return [
            values[0].transpose(0, 2, 1, 3),
            values[1],
            values[2],
            values[3].transpose(0, 2, 1),
            *values[4:],
        ]

    params = turn(params)
    ahead = forward_all(
        dims, LAYERS, share, lines, norms, params, image_codes, labels.reshape(1, -1), mask_flags
    )
    kinds = [(kind, layer) for layer in range(LAYERS) for kind in (ATTEND, EXPAND, CONTRACT)]
    found = backward_all(
        dims,
        LAYERS,
        lines,
        {name: ahead.whole[at + 1] for at, name in enumerate(kinds)},
        dict(
            slope=ahead.slope,
            active=ahead.active,
            normed_two=ahead.normed_two,
            middle=ahead.middle,
            joined=ahead.joined,
            blended=ahead.blended,
            normed=ahead.normed,
            stream=ahead.stream,
        ),
        dict(
            rows=ahead.rows,
            gains=ahead.gains,
            grad_top=ahead.grad_top,
            final=ahead.final,
            grad_logits=ahead.grad_logits,
            final_grads=ahead.final_grads,
            loss=ahead.loss,
        ),
        logit_table.shape[1],
    )

    new = adam_all(LAYERS, share, norms, found, ahead.count, params, turn(moments_one), turn(moments_two))
    results = []
    for index in range(7):
        for group in (new.new_weight, new.new_one, new.new_two):
            value = group[index]
            results.append(
                value.transpose(0, 2, 1, 3) if index == 0 else value.transpose(0, 2, 1) if index == 3 else value
            )
    return (*results, new.loss.reshape(()), new.masked.reshape(()), new.norm.reshape(()))


def solution(mesh):
    dp, tensor = mesh.shape["dp"], mesh.shape["tensor"]
    in_specs = (
        (P("dp", None), P("dp"), P("dp", None))
        + (P(None, "dp", None, "tensor"),) * 3
        + (P(None, "tensor", "dp"),) * 3
        + (P(None, "dp", "tensor"),) * 3
        + (P(None, "tensor", "dp"),) * 3
        + (P("dp", None),) * 3
        + (P("dp", "tensor"),) * 3
        + (P(None, None, "dp"),) * 3
    )

    def either(*args):
        whole_tiles = args[3].shape[1] % 16 == 0 and args[1].shape[0] == tensor
        return body(dp, tensor, *args) if whole_tiles else plain_body(*args)

    return jax.shard_map(
        either,
        mesh=mesh,
        in_specs=in_specs,
        out_specs=in_specs[3:] + (P(), P(), P()),
        check_vma=False,
    )
```

```python
import functools

import jax
import jax.numpy as jnp
from jax import lax
from jax.experimental import pallas as pl
from jax.experimental.pallas import tpu as pltpu
from jax.sharding import PartitionSpec as P

HEADS = 16
CODES = 1024
CLASSES = 1000
LAYERS = 2
STEP = 10
SEQ = 257
ROWS_UP = 16

beta_one = 0.9
beta_two = 0.96
matrix_rate = 0.02
embed_rate = 0.5
vector_rate = 0.25
weight_decay = 0.045
epsilon = 1e-10
clip_limit = 0.02
norm_epsilon = 1e-06
low = jnp.bfloat16
full = jnp.float32


def matmul(left, right):
    return jnp.dot(left, right, preferred_element_type=full)


def matmul_left(left, right):
    return lax.dot_general(left, right, (((0,), (0,)), ((), ())), preferred_element_type=full)


def matmul_right(left, right):
    return lax.dot_general(left, right, (((1,), (1,)), ((), ())), preferred_element_type=full)


def layer_norm(stream, scaling, offset):
    average = jnp.mean(stream, axis=-1, keepdims=True)
    centred = stream - average
    variance = jnp.mean(centred * centred, axis=-1, keepdims=True)
    return centred * lax.rsqrt(variance + norm_epsilon) * scaling + offset


def norm_back(stream, scaling, offset, gradient):
    normed_out, pull = jax.vjp(layer_norm, stream, scaling, offset)
    return pull(gradient)


def gelu_exact(values):
    return jax.nn.gelu(values, approximate=False)


def branch_total(piece_sum):
    return lax.psum(piece_sum.astype(jnp.bfloat16), "tensor").astype(jnp.float32)


def input_total(piece_sum):
    return lax.psum(piece_sum.astype(jnp.bfloat16), "tensor").astype(jnp.float32)


def split_heads(joined, images, head_count):
    head_width = joined.shape[1] // (3 * head_count)
    sections = joined.reshape(images, SEQ, 3, head_count, head_width)
    return (sections[:, :, 0], sections[:, :, 1], sections[:, :, 2], head_width ** (-0.5))


def attend_forward(joined, images, head_count):
    queries, key_rows, values, score_scale = split_heads(joined, images, head_count)
    scores = (
        jnp.einsum("bqhd,bkhd->bhqk", queries, key_rows, preferred_element_type=jnp.float32)
        * score_scale
    )
    peak_value = jnp.max(scores, axis=-1, keepdims=True)
    log_total = peak_value + jnp.log(jnp.sum(jnp.exp(scores - peak_value), axis=-1, keepdims=True))
    attention = jnp.exp(scores - log_total).astype(jnp.bfloat16)
    blended = jnp.einsum("bhqk,bkhd->bqhd", attention, values, preferred_element_type=jnp.float32)
    return (blended.astype(jnp.bfloat16).reshape(joined.shape[0], -1), log_total)


def attend_backward(joined, log_total, grad_blended, images, head_count):
    queries, key_rows, values, score_scale = split_heads(joined, images, head_count)
    scores = (
        jnp.einsum("bqhd,bkhd->bhqk", queries, key_rows, preferred_element_type=jnp.float32)
        * score_scale
    )
    attention = jnp.exp(scores - log_total)
    grad_out = grad_blended.reshape(queries.shape)
    grad_attention = jnp.einsum(
        "bqhd,bkhd->bhqk", grad_out, values, preferred_element_type=jnp.float32
    )
    row_total = jnp.sum(attention * grad_attention, axis=-1, keepdims=True)
    grad_scores = (attention * (grad_attention - row_total)).astype(jnp.bfloat16)
    grad_queries = (
        jnp.einsum("bhqk,bkhd->bqhd", grad_scores, key_rows, preferred_element_type=jnp.float32)
        * score_scale
    )
    grad_keys = (
        jnp.einsum("bhqk,bqhd->bkhd", grad_scores, queries, preferred_element_type=jnp.float32)
        * score_scale
    )
    grad_values = jnp.einsum(
        "bhqk,bqhd->bkhd",
        attention.astype(jnp.bfloat16),
        grad_out,
        preferred_element_type=jnp.float32,
    )
    stacked = jnp.stack([grad_queries, grad_keys, grad_values], axis=2).astype(jnp.bfloat16)
    return stacked.reshape(joined.shape)


def layer_forward(stream, weights, gains, images, head_count):
    w_in, w_out, w_expand, w_contract = weights
    normed = layer_norm(stream, gains[0, 0], gains[0, 1]).astype(jnp.bfloat16)
    joined = matmul(normed, w_in.reshape(w_in.shape[0], -1)).astype(jnp.bfloat16)
    blended, log_total = attend_forward(joined, images, head_count)
    middle = stream + branch_total(matmul(blended, w_out))
    normed_two = layer_norm(middle, gains[1, 0], gains[1, 1]).astype(jnp.bfloat16)
    hidden = matmul(normed_two, w_expand)
    active = gelu_exact(hidden).astype(jnp.bfloat16)
    result = middle + branch_total(matmul(active, w_contract))
    return (
        result,
        (stream, normed, joined, blended, log_total, middle, normed_two, hidden, active),
    )


def layer_backward(gradient, saved, weights, gains, images, head_count):
    w_in, w_out, w_expand, w_contract = weights
    stream, normed, joined, blended, log_total, middle, normed_two, hidden, active = saved
    grad_low = gradient.astype(jnp.bfloat16)
    g_contract = matmul_left(active, grad_low)
    grad_active = matmul_right(grad_low, w_contract)
    gelu_out, gelu_pull = jax.vjp(gelu_exact, hidden)
    grad_hidden = gelu_pull(grad_active)[0].astype(jnp.bfloat16)
    g_expand = matmul_left(normed_two, grad_hidden)
    grad_normed = input_total(matmul_right(grad_hidden, w_expand))
    grad_mid, scale_two, offset_two = norm_back(middle, gains[1, 0], gains[1, 1], grad_normed)
    gradient = gradient + grad_mid
    grad_low = gradient.astype(jnp.bfloat16)
    g_out = matmul_left(blended, grad_low)
    grad_blended = matmul_right(grad_low, w_out).astype(jnp.bfloat16)
    grad_joined = attend_backward(joined, log_total, grad_blended, images, head_count)
    g_in = matmul_left(normed, grad_joined).reshape(w_in.shape)
    grad_normed = input_total(matmul_right(grad_joined, w_in.reshape(w_in.shape[0], -1)))
    grad_first, scale_one, offset_one = norm_back(stream, gains[0, 0], gains[0, 1], grad_normed)
    norm_grads = jnp.stack([jnp.stack([scale_one, offset_one]), jnp.stack([scale_two, offset_two])])
    return (gradient + grad_first, (g_in, g_out, g_expand, g_contract), norm_grads)


def plain_body(
    image_codes,
    labels,
    mask_flags,
    attend_in,
    attend_in_one,
    attend_in_two,
    attend_out,
    attend_out_one,
    attend_out_two,
    expand,
    expand_one,
    expand_two,
    contract,
    contract_one,
    contract_two,
    embed_table,
    embed_one,
    embed_two,
    logit_table,
    logit_one,
    logit_two,
    norm_params,
    norm_one,
    norm_two,
):
    w_in, w_out, w_expand, w_contract, embed_rows, head_table, gains_low = (
        lax.all_gather(attend_in.astype(jnp.bfloat16), "dp", axis=1, tiled=True),
        lax.all_gather(attend_out.astype(jnp.bfloat16), "dp", axis=2, tiled=True),
        lax.all_gather(expand.astype(jnp.bfloat16), "dp", axis=1, tiled=True),
        lax.all_gather(contract.astype(jnp.bfloat16), "dp", axis=2, tiled=True),
        lax.all_gather(embed_table.astype(jnp.bfloat16), "dp", axis=0, tiled=True),
        lax.all_gather(logit_table.astype(jnp.bfloat16), "dp", axis=0, tiled=True),
        lax.all_gather(norm_params.astype(jnp.bfloat16), "dp", axis=2, tiled=True),
    )
    gains = gains_low.astype(jnp.float32)
    images = labels.shape[0]
    head_count = HEADS // lax.axis_size("tensor")
    code_rows = jnp.where(mask_flags == 1, CODES, image_codes)
    row_index = jnp.concatenate([(CODES + 1 + labels)[:, None], code_rows], axis=1).reshape(-1)
    place_rows = jnp.tile(CODES + 1 + CLASSES + jnp.arange(SEQ), images)
    targets = jnp.concatenate([jnp.zeros((images, 1), jnp.int32), image_codes], axis=1).reshape(-1)
    weights_loss = jnp.concatenate(
        [jnp.zeros((images, 1), jnp.float32), mask_flags.astype(jnp.float32)], axis=1
    ).reshape(-1)
    stream = embed_rows[row_index].astype(jnp.float32) + embed_rows[place_rows].astype(jnp.float32)
    saved_all = []
    for layer_index in range(LAYERS):
        weights = (
            w_in[layer_index],
            w_out[layer_index],
            w_expand[layer_index],
            w_contract[layer_index],
        )
        stream, saved = layer_forward(
            stream, weights, gains[2 * layer_index : 2 * layer_index + 2], images, head_count
        )
        saved_all.append(saved)
    final_gain = gains[2 * LAYERS]
    final = layer_norm(stream, final_gain[0], final_gain[1]).astype(jnp.bfloat16)
    logits = matmul(final, head_table)
    local_codes = logits.shape[1]
    col_start = lax.axis_index("tensor") * local_codes
    is_target = (
        targets[:, None] == col_start + jnp.arange(local_codes, dtype=jnp.int32)[None, :]
    ).astype(jnp.float32)
    peak_value = jnp.max(logits, axis=1)
    exp_total = jnp.sum(jnp.exp(logits - peak_value[:, None]), axis=1)
    picked = jnp.sum(is_target * logits, axis=1)
    peak_all = lax.pmax(peak_value, "tensor")
    exp_all, picked_all = lax.psum((exp_total * jnp.exp(peak_value - peak_all), picked), "tensor")
    log_total = peak_all + jnp.log(exp_all)
    loss_terms = (log_total - picked_all) * weights_loss
    loss_sum, token_count = lax.psum((jnp.sum(loss_terms), jnp.sum(weights_loss)), "dp")
    grad_logits = (
        (jnp.exp(logits - log_total[:, None]) - is_target) * (weights_loss / token_count)[:, None]
    ).astype(jnp.bfloat16)
    g_head = matmul_left(final, grad_logits)
    grad_final = input_total(matmul_right(grad_logits, head_table))
    gradient, final_scale, final_offset = norm_back(
        stream, final_gain[0], final_gain[1], grad_final
    )
    layer_grads = [None] * LAYERS
    norm_grads = [None] * LAYERS
    for layer_index in reversed(range(LAYERS)):
        weights = (
            w_in[layer_index],
            w_out[layer_index],
            w_expand[layer_index],
            w_contract[layer_index],
        )
        gradient, found, gain_grads = layer_backward(
            gradient,
            saved_all[layer_index],
            weights,
            gains[2 * layer_index : 2 * layer_index + 2],
            images,
            head_count,
        )
        layer_grads[layer_index] = found
        norm_grads[layer_index] = gain_grads
    g_norms = jnp.concatenate(
        [
            jnp.stack(norm_grads).reshape(2 * LAYERS, 2, -1),
            jnp.stack([final_scale, final_offset])[None],
        ],
        axis=0,
    )
    g_table = jax.ops.segment_sum(
        jnp.concatenate([gradient, gradient], axis=0),
        jnp.concatenate([row_index, place_rows]),
        num_segments=embed_rows.shape[0],
    )
    g_in_all = jnp.stack([found[0] for found in layer_grads])
    g_out_all = jnp.stack([found[1] for found in layer_grads])
    g_expand_all = jnp.stack([found[2] for found in layer_grads])
    g_contract_all = jnp.stack([found[3] for found in layer_grads])
    g_in_all, g_out_all, g_expand_all, g_contract_all, g_table, g_head, g_norms = (
        lax.psum_scatter(g_in_all, "dp", scatter_dimension=1, tiled=True),
        lax.psum_scatter(g_out_all, "dp", scatter_dimension=2, tiled=True),
        lax.psum_scatter(g_expand_all, "dp", scatter_dimension=1, tiled=True),
        lax.psum_scatter(g_contract_all, "dp", scatter_dimension=2, tiled=True),
        lax.psum_scatter(g_table, "dp", scatter_dimension=0, tiled=True),
        lax.psum_scatter(g_head, "dp", scatter_dimension=0, tiled=True),
        lax.psum_scatter(g_norms, "dp", scatter_dimension=2, tiled=True),
    )
    gradients = (g_in_all, g_out_all, g_expand_all, g_contract_all, g_table, g_head, g_norms)
    first_rank = (lax.axis_index("tensor") == 0).astype(jnp.float32)
    split_squares = (
        jnp.sum(g_in_all * g_in_all)
        + jnp.sum(g_out_all * g_out_all)
        + jnp.sum(g_expand_all * g_expand_all)
        + jnp.sum(g_contract_all * g_contract_all)
        + jnp.sum(g_head * g_head)
    )
    shared_squares = jnp.sum(g_table * g_table) + jnp.sum(g_norms * g_norms)
    grad_norm = jnp.sqrt(lax.psum(split_squares + first_rank * shared_squares, ("dp", "tensor")))
    factor = clip_limit / jnp.maximum(grad_norm, clip_limit)
    params = (attend_in, attend_out, expand, contract, embed_table, logit_table, norm_params)
    moments_one = (
        attend_in_one,
        attend_out_one,
        expand_one,
        contract_one,
        embed_one,
        logit_one,
        norm_one,
    )
    moments_two = (
        attend_in_two,
        attend_out_two,
        expand_two,
        contract_two,
        embed_two,
        logit_two,
        norm_two,
    )
    results = []
    for index in range(7):
        rate_here = vector_rate if index == 6 else embed_rate if index == 4 else matrix_rate
        decay_here = 0.0 if index == 6 else weight_decay
        results.extend(
            adam_step(
                params[index],
                moments_one[index],
                moments_two[index],
                gradients[index],
                factor,
                rate_here,
                decay_here,
            )
        )
    return (
        results[0],
        results[1],
        results[2],
        results[3],
        results[4],
        results[5],
        results[6],
        results[7],
        results[8],
        results[9],
        results[10],
        results[11],
        results[12],
        results[13],
        results[14],
        results[15],
        results[16],
        results[17],
        results[18],
        results[19],
        results[20],
        loss_sum,
        token_count,
        grad_norm,
    )


def adam_step(weight, moment_one, moment_two, gradient, factor, rate_here, decay_here):
    gradient = gradient * factor
    moment_one = beta_one * moment_one + (1.0 - beta_one) * gradient
    moment_two = beta_two * moment_two + (1.0 - beta_two) * gradient * gradient
    correct_one = 1.0 - beta_one**STEP
    correct_two = 1.0 - beta_two**STEP
    weight = weight - rate_here * (
        moment_one * (1.0 / correct_one) / (jnp.sqrt(moment_two * (1.0 / correct_two)) + epsilon)
        + decay_here * weight
    )
    return [weight, moment_one, moment_two]


MESH = pl.DeviceIdType.MESH


def factors(dp, tensor):
    return [("tensor", tensor // 2, 2), ("tensor", 2, 1), ("dp", dp // 2, 2), ("dp", 2, 1)]


OUTER, PAIR, LONG, NEAR = range(4)
ORDERS = {
    "a": (LONG, NEAR, OUTER, PAIR),
    "b": (LONG, OUTER, NEAR, PAIR),
    "d": (OUTER, LONG, NEAR, PAIR),
    "e": (NEAR, LONG, OUTER, PAIR),
}


def place_of(dims):
    return [(lax.axis_index(axis) // stride) % size for axis, size, stride in dims]


def peer_of(dims, here, moved, moves):
    there = list(here)
    for dim, move in zip(moved, moves):
        there[dim] = lax.rem(here[dim] + move, dims[dim][1])
    found = {"dp": 0, "tensor": 0}
    for (axis, size, stride), at in zip(dims, there):
        found[axis] = found[axis] + at * stride
    return (found["dp"], found["tensor"])


def greet(dims, here, planes=False):
    barrier = pltpu.get_barrier_semaphore()
    moves = [((dim,), (move,)) for dim, (axis, size, stride) in enumerate(dims) for move in range(1, size)]
    if planes:
        for pair in ((OUTER, PAIR), (LONG, NEAR)):
            for one in range(1, dims[pair[0]][1]):
                for two in range(1, dims[pair[1]][1]):
                    moves.append((pair, (one, two)))
    for moved, move in moves:
        pl.semaphore_signal(barrier, inc=1, device_id=peer_of(dims, here, moved, move), device_id_type=MESH)
    pl.semaphore_wait(barrier, len(moves))


def gather_units(rows):
    tiles = rows // 16
    if rows % 16 or tiles < 4:
        return [[(0, rows, "a")]]
    if tiles == 6:
        cuts = [[("a", 2), ("b", 1), ("d", 1)], [("b", 1), ("e", 1)]]
    else:
        cuts = [[("a", 1), ("b", 1)], [("a", 1), ("b", 1), ("d", tiles - 4)]]
    units, row = [], 0
    for cut in cuts:
        unit = []
        for order, count in cut:
            unit.append((row, 16 * count, order))
            row += 16 * count
        units.append(unit)
    return units


TOKENS = -(-SEQ // 16) * 16


class Refs:
    pass


class Parts:
    def __init__(self):
        self.ins, self.outs, self.scratch = [], [], []

    def put(self, near=False, key=None, **named):
        for name, value in named.items():
            space = pltpu.VMEM if near else pl.ANY
            self.ins.append(((name, key), value, pl.BlockSpec(memory_space=space)))

    def out(self, kind, near=False, key=None, **named):
        for name, shape in named.items():
            space = pltpu.VMEM if near else pl.ANY
            self.outs.append(
                ((name, key), jax.ShapeDtypeStruct(shape, kind), pl.BlockSpec(memory_space=space))
            )

    def keep(self, key=None, **named):
        for name, scratch in named.items():
            self.scratch.append(((name, key), scratch))

    def refs(self, refs):
        found = Refs()
        for ((name, key), *rest), ref in zip(self.ins + self.outs + self.scratch, refs):
            if key is None:
                setattr(found, name, ref)
            else:
                found.__dict__.setdefault(name, {})[key] = ref
        return found

    def call(self, body, barrier=None):
        found = pl.pallas_call(
            lambda *refs: body(self.refs(refs)),
            out_shape=[shape for name, shape, spec in self.outs],
            in_specs=[spec for name, value, spec in self.ins],
            out_specs=[spec for name, shape, spec in self.outs],
            scratch_shapes=[scratch for name, scratch in self.scratch],
            compiler_params=pltpu.CompilerParams(
                collective_id=barrier,
                has_side_effects=barrier is not None,
                vmem_limit_bytes=63 * 1024 * 1024,
            ),
        )(*[value for name, value, spec in self.ins])
        return self.refs([None] * len(self.ins) + list(found))


class Reducer:
    def __init__(self, dims, chunks, cuts):
        self.dims, self.chunks = dims, chunks
        self.sizes = [size for axis, size, stride in dims]
        self.units, self.sides, counts = [], set(), {}
        self.slots = 0
        for chunk, (name, rows, width, wide) in enumerate(chunks):
            for unit in cuts(rows, width, wide):
                found = []
                for row, size, order in unit:
                    stages = []
                    for stage in range(4):
                        dim = ORDERS[order][3 - stage]
                        key = (order, stage, size, width, wide)
                        stages.append((dim, key, counts.get(key, 0), self.slots))
                        self.sides.add((key, len(self.units) % 2))
                        counts[key] = counts.get(key, 0) + 1
                        self.slots += self.sizes[dim] - 1
                    found.append((row, size, order, stages, len(self.units) % 2))
                self.units.append((chunk, found))
        self.counts = counts
        self.started, self.busy = {}, {}

    def room(self, key):
        order, stage, size, width, wide = key
        gone = [ORDERS[order][3 - at] for at in range(stage + 1)]
        rest = tuple(self.sizes[dim] for dim in range(4) if dim not in gone)
        return (self.sizes[gone[-1]] - 1, *rest, size, width)

    def declare(self, parts):
        for key, count in self.counts.items():
            order, stage, size, width, wide = key
            kind = full if wide and stage == 3 else low
            parts.out(kind, key=key, came=(count, *self.room(key)))
            parts.keep(key=key, staged=pltpu.VMEM(self.room(key), kind), staged_sem=pltpu.SemaphoreType.DMA)
            for side in range(2):
                if stage == 2 and wide and (key, side) in self.sides:
                    parts.keep(key=(key, side), exact=pltpu.VMEM(self.room(key)[1:], full))
        parts.keep(
            send=pltpu.SemaphoreType.DMA((self.slots,)),
            recv=pltpu.SemaphoreType.DMA((self.slots,)),
            squares=pltpu.VMEM((8, 128), full),
        )

    def bind(self, refs, here, blocks, results):
        self.refs, self.here, self.blocks, self.results = refs, here, blocks, results
        refs.squares[...] = jnp.zeros_like(refs.squares)

    def turn(self, dim, move):
        return lax.rem(self.here[dim] + move, self.sizes[dim]) if move else self.here[dim]

    def block(self, chunk, part, stage, move):
        row, size, order, stages, side = part
        gone = [ORDERS[order][3 - at] for at in range(stage)]
        dim = ORDERS[order][3 - stage]
        spot = [
            self.turn(at, move) if at == dim else (self.here[at] if at in gone else slice(None))
            for at in range(4)
        ]
        return self.blocks[chunk].at[(*spot, pl.ds(row, size))]

    def exact(self, part, stage, move):
        row, size, order, stages, side = part
        left = sorted(ORDERS[order][: 4 - stage])
        dim = ORDERS[order][3 - stage]
        spot = [self.turn(at, move) if at == dim else slice(None) for at in left]
        return self.refs.exact[(stages[stage - 1][1], side)].at[tuple(spot)]

    def copies(self, chunk, part, stage):
        dim, key, count, slot = part[3][stage]
        wide = key[4] and stage == 3
        return [
            pltpu.make_async_remote_copy(
                src_ref=self.exact(part, stage, move) if wide else self.block(chunk, part, stage, move),
                dst_ref=self.refs.came[key].at[count, move - 1],
                send_sem=self.refs.send.at[slot + move - 1],
                recv_sem=self.refs.recv.at[slot + move - 1],
                device_id=peer_of(self.dims, self.here, (dim,), (move,)),
                device_id_type=MESH,
            )
            for move in range(1, self.sizes[dim])
        ]

    def staged(self, part, stage):
        dim, key, count, slot = part[3][stage]
        return pltpu.make_async_copy(
            self.refs.came[key].at[count], self.refs.staged[key], self.refs.staged_sem[key]
        )

    def add(self, chunk, part, stage):
        row, size, order, stages, side = part
        dim, key, count, slot = stages[stage]
        held, came = self.block(chunk, part, stage, 0), self.refs.staged[key]
        if stage == 0:
            total = held[...]
            for move in range(self.sizes[dim] - 1):
                total = total + came[move]
            held[...] = total
            return
        exact = stage == 3 and key[4]
        total = (self.exact(part, stage, 0) if exact else held)[...].astype(full)
        for move in range(self.sizes[dim] - 1):
            total = total + came[move].astype(full)
        if stage < 3 and not (stage == 2 and key[4]):
            held[...] = total.astype(low)
            return
        if stage == 2:
            for copy in self.busy.pop((key, side), []):
                copy.wait_send()
            self.refs.exact[(key, side)][...] = total
            return
        self.results[chunk][pl.ds(row, size), :] = total
        square = total * total
        square = sum(square[at : at + 8] for at in range(0, size, 8))
        self.refs.squares[...] += sum(square[:, at : at + 128] for at in range(0, square.shape[1], 128))

    def tick(self, now):
        work = [
            (at, (now - at) // 2)
            for at in range(len(self.units))
            if (now - at) % 2 == 0 and 0 <= now - at <= 8
        ]
        for at, stage in work:
            if stage == 0:
                self.send_on(at, stage)
        behind = None
        for at, stage in work:
            if stage:
                chunk, found = self.units[at]
                for part in found:
                    for copy in self.copies(chunk, part, stage - 1):
                        copy.wait_recv()
                    self.staged(part, stage - 1).start()
                if behind:
                    self.send_on(*behind)
                behind = (at, stage)
        if behind:
            self.send_on(*behind)

    def send_on(self, at, stage):
        chunk, found = self.units[at]
        for part in found:
            if stage:
                self.staged(part, stage - 1).wait()
                self.add(chunk, part, stage - 1)
            if stage < 4:
                dim, key, count, slot = part[3][stage]
                copies = self.copies(chunk, part, stage)
                for copy in copies:
                    copy.start()
                if key[4] and stage == 3:
                    self.busy[(part[3][2][1], part[4])] = copies
                else:
                    self.started.setdefault(chunk, []).extend(copies)

    def ticks(self):
        return len(self.units) + 8

    def finish(self):
        for chunk in list(self.started):
            self.release(chunk)
        for copy in sum(self.busy.values(), []):
            copy.wait_send()

    def release(self, chunk):
        for copy in self.started.pop(chunk):
            copy.wait_send()


def reduce_cuts(rows, width, wide):
    tiles = rows // 16
    if width <= 256:
        cuts = [[("a", tiles // 2), ("b", tiles - tiles // 2)]]
    elif wide and tiles == 6:
        cuts = [[("a", 1), ("d", 1), ("e", 1)], [("b", 1), ("d", 1), ("e", 1)]]
    elif tiles == 6:
        cuts = [[("a", 2), ("b", 1), ("e", 1)], [("b", 2)]]
    else:
        cuts = [[("a", 1), ("b", 1), ("e", 1)], [("a", 1), ("b", tiles - 4)]]
    units, row = [], 0
    for cut in cuts:
        unit = []
        for order, count in cut:
            unit.append((row, 16 * count, order))
            row += 16 * count
        units.append(unit)
    return units


def norm_back_rows(grad, grad_normed, source, gain, found, row):
    value, up = source[...], grad_normed[...]
    centred = value - jnp.mean(value, axis=-1, keepdims=True)
    spread = lax.rsqrt(jnp.mean(centred * centred, axis=-1, keepdims=True) + norm_epsilon)
    unit = centred * spread
    inner = up * gain[...]
    pulled = spread * (
        inner - jnp.mean(inner, axis=-1, keepdims=True) - unit * jnp.mean(inner * unit, axis=-1, keepdims=True)
    )
    grad[...] = grad[...] + pulled
    found[pl.ds(row, 1), :] = jnp.sum(up * unit, axis=0, keepdims=True)
    found[pl.ds(row + 1, 1), :] = jnp.sum(up, axis=0, keepdims=True)


def square_block(value):
    return value.reshape(-1, value.shape[-1])


HEAD, ATTEND, EXPAND, CONTRACT, TABLE = range(5)


def backward_kernel(dims, reducer, layers, heads, width, refs):
    here = place_of(dims)
    sizes = reducer.sizes
    sides = (sizes[2], sizes[3])
    names = [name for name, rows, across, wide in reducer.chunks]
    spots = sizes[0] * sizes[1]
    part = heads * width

    weights = {
        name: pltpu.make_async_copy(refs.weight[name], refs.slots.at[at], refs.weight_sem.at[at])
        for at, name in enumerate(names[1:-1])
    }
    mlp = (refs.slope, refs.active, refs.normed_two, refs.middle)
    mlp_near = (refs.near_slope, refs.near_active, refs.near_normed_two, refs.near_middle)
    attend = (refs.joined, refs.blended, refs.normed, refs.stream)
    attend_near = (refs.near_joined, refs.near_blended, refs.near_normed, refs.near_stream)

    def fetches(far, near, sem, layer):
        return [
            pltpu.make_async_copy(source.at[layer], target, sem.at[at])
            for at, (source, target) in enumerate(zip(far, near))
        ]

    def mlp_fetches(layer):
        return fetches(mlp, mlp_near, refs.mlp_sem, layer)

    def attend_fetches(layer):
        return fetches(attend, attend_near, refs.attend_sem, layer)

    order = names[1:-1]
    for copy in mlp_fetches(layers - 1):
        copy.start()
    for name in order[:2]:
        weights[name].start()
    for copy in attend_fetches(layers - 1):
        copy.start()
    for name in order[2:]:
        weights[name].start()
    greet(dims, here, True)

    lines = refs.total[(TABLE, 0)].shape[0]
    table_blocks = refs.slots.at[0, :, :, :, :, pl.ds(0, lines)]
    blocks = [refs.head_blocks] + [refs.slots.at[at] for at in range(len(order))] + [table_blocks]
    reducer.bind(refs, here, blocks, [refs.total[name] for name in names])
    clock = [0]

    made = [0]

    def run(count):
        for _ in range(count):
            reducer.tick(clock[0])
            clock[0] += 1

    def done(chunk):
        made[0] += sum(1 for at, found in reducer.units if at == chunk)

    def step(count=1):
        run(min(count, made[0] - clock[0]))

    grad, grad_normed, norm_grads = refs.grad, refs.grad_normed, refs.norm_grads
    gains = refs.gains

    norm_grads[...] = jnp.zeros_like(norm_grads)
    norm_grads[pl.ds(4 * layers, 2), :] = refs.final_grads[...]
    grad[...] = refs.grad_top[...]
    turned = refs.final[...].T
    for spot in range(spots):
        across = refs.grad_logits.shape[1] // spots
        found = matmul(turned, refs.grad_logits[:, spot * across : (spot + 1) * across])
        refs.head_blocks[spot // sizes[1], spot % sizes[1]] = found.astype(low).reshape(*sides, -1, across)
    done(0)
    step()

    for layer in reversed(range(layers)):
        at_contract, at_expand, at_attend = [names.index((kind, layer)) for kind in (CONTRACT, EXPAND, ATTEND)]
        slot_contract, slot_expand, slot_attend = [
            refs.slots.at[at - 1] for at in (at_contract, at_expand, at_attend)
        ]

        for copy in mlp_fetches(layer):
            copy.wait()
        weights[(CONTRACT, layer)].wait()
        refs.grad_low[...] = grad[...].astype(low)
        refs.turned[...] = grad[...].astype(low).T

        def contract_step(spot, carry):
            outer, pair = spot // sizes[1], spot % sizes[1]
            held = square_block(slot_contract[outer, pair])
            pulled = matmul(refs.grad_low[...], held) * refs.near_slope[spot]
            refs.grad_hidden[spot] = pulled.astype(low)
            found = matmul(refs.turned[...], refs.near_active[spot]).astype(low)
            slot_contract[outer, pair] = found.reshape(*sides, -1, found.shape[-1])
            return carry

        lax.fori_loop(0, spots, contract_step, 0)
        done(at_contract)
        step()

        weights[(EXPAND, layer)].wait()
        refs.turned[...] = refs.near_normed_two[...].T
        grad_normed[...] = jnp.zeros_like(grad_normed)

        def expand_step(spot, carry):
            outer, pair = spot // sizes[1], spot % sizes[1]
            held = square_block(slot_expand[outer, pair])
            pulled = refs.grad_hidden[spot]
            grad_normed[...] += matmul_right(pulled, held)
            found = matmul(refs.turned[...], pulled).astype(low)
            slot_expand[outer, pair] = found.reshape(*sides, -1, found.shape[-1])
            return carry

        lax.fori_loop(0, spots, expand_step, 0)
        done(at_expand)
        step()
        norm_back_rows(
            grad, grad_normed, refs.near_middle, gains.at[pl.ds(4 * layer + 2, 1)], norm_grads, 4 * layer + 2
        )
        if layer:
            for copy in mlp_fetches(layer - 1):
                copy.start()

        for copy in attend_fetches(layer):
            copy.wait()
        weights[(ATTEND, layer)].wait()
        refs.grad_low[...] = grad[...].astype(low)
        refs.turned[...] = grad[...].astype(low).T
        refs.turned_two[...] = refs.near_normed[...].T
        grad_normed[...] = jnp.zeros_like(grad_normed)
        known = lax.broadcasted_iota(jnp.int32, (TOKENS, 1), 0) < SEQ
        scale = width ** (-0.5)

        def attend_step(spot, carry):
            outer, pair = spot // sizes[1], spot % sizes[1]
            held = square_block(slot_attend[outer, pair])
            up_all = matmul(refs.grad_low[...], held[:, 3 * part :]).astype(low)
            pulled_all = []
            joined = refs.near_joined[spot]
            parts = [[], [], []]
            for head in range(heads):
                query, key, value = [
                    joined[:, (at * heads + head) * width : (at * heads + head + 1) * width] for at in range(3)
                ]
                up = up_all[:, head * width : (head + 1) * width]
                scores = jnp.where(known, matmul_right(key, query) * scale, -1e30)
                probs = jnp.exp(scores - jnp.max(scores, axis=0, keepdims=True))
                probs = probs * (1.0 / jnp.sum(probs, axis=0, keepdims=True))
                pulled = matmul_right(value, up)
                total = jnp.sum(probs * pulled, axis=0, keepdims=True)
                moved = (probs * (pulled - total)).astype(low)
                parts[0].append((matmul_left(moved, key) * scale).astype(low))
                parts[1].append((matmul(moved, query) * scale).astype(low))
                parts[2].append(matmul(probs.astype(low), up).astype(low))
            pulled = jnp.concatenate(parts[0] + parts[1] + parts[2], axis=1)
            grad_normed[...] += matmul_right(pulled, held[:, : 3 * part])
            found = jnp.concatenate(
                [
                    matmul(refs.turned_two[...], pulled).astype(low),
                    matmul(refs.turned[...], refs.near_blended[spot]).astype(low),
                ],
                axis=1,
            )
            slot_attend[outer, pair] = found.reshape(*sides, -1, found.shape[-1])
            return carry

        step()
        lax.fori_loop(0, spots // 2, attend_step, 0)
        step()
        lax.fori_loop(spots // 2, spots, attend_step, 0)
        done(at_attend)
        step()
        norm_back_rows(grad, grad_normed, refs.near_stream, gains.at[pl.ds(4 * layer, 1)], norm_grads, 4 * layer)
        if layer:
            for copy in attend_fetches(layer - 1):
                copy.start()

    upper = grad[...].astype(low)
    lower = (grad[...] - upper.astype(full)).astype(low)
    model = grad.shape[1]
    depth = refs.slots.shape[5]
    reducer.release(1)

    def table_step(spot, carry):
        height = sizes[2] * sizes[3] * lines
        row = spot * height + lax.broadcasted_iota(jnp.int32, (height, TOKENS), 0)
        picks = (row == refs.rows[0:1, :]).astype(full) + (row == refs.rows[1:2, :]).astype(full)
        picks = picks.astype(low)
        found = (matmul(picks, upper) + matmul(picks, lower)).astype(low)
        table_blocks[spot // sizes[1], spot % sizes[1]] = found.reshape(*sides, lines, model)
        return carry

    lax.fori_loop(0, spots, table_step, 0)
    done(len(names) - 1)
    run(reducer.ticks() - clock[0])
    finish_sums(dims, here, reducer, refs)
    reducer.finish()


def finish_sums(dims, here, reducer, refs):
    sizes = reducer.sizes
    total = refs.total[(TABLE, 0)]
    refs.total_low[...] = total[...].astype(low)
    own = pltpu.make_async_copy(refs.total_low, refs.spread.at[here[0], here[1]], refs.spread_own)
    own.start()
    model = total.shape[1]
    refs.shared[0, :8] = refs.squares[...]
    refs.shared[0, 8:16] = refs.loss[...]
    for at in range(model // 128):
        refs.shared[0, 16 * at + 16 : 16 * at + 32] = refs.norm_grads[:, at * 128 : (at + 1) * 128]
    waits = []
    for hop, dims_here in enumerate(((OUTER, PAIR), (LONG, NEAR))):
        copies = []
        for move in range(1, sizes[dims_here[0]] * sizes[dims_here[1]]):
            moves = (move // sizes[dims_here[1]], move % sizes[dims_here[1]])
            sems = (refs.shared_send.at[hop, move - 1], refs.shared_recv.at[hop, move - 1])
            copies.append(
                pltpu.make_async_remote_copy(
                    src_ref=refs.shared.at[hop],
                    dst_ref=refs.shared_came.at[hop, move - 1],
                    send_sem=sems[0],
                    recv_sem=sems[1],
                    device_id=peer_of(dims, here, dims_here, moves),
                    device_id_type=MESH,
                )
            )
        for copy in copies:
            copy.start()
        table = []
        if hop == 0:
            pairs = [(OUTER, move, refs.total_low, refs.spread.at[here[0], here[1]]) for move in range(1, sizes[OUTER])]
        else:
            beside = refs.spread.at[:, here[1]]
            pairs = [(PAIR, move, beside, beside) for move in range(1, sizes[PAIR])]
        for dim, move, source, target in pairs:
            table.append(
                pltpu.make_async_remote_copy(
                    src_ref=source,
                    dst_ref=target,
                    send_sem=refs.spread_send.at[hop, move - 1],
                    recv_sem=refs.spread_recv.at[hop, move - 1],
                    device_id=peer_of(dims, here, (dim,), (move,)),
                    device_id_type=MESH,
                )
            )
        if hop:
            own.wait()
            for copy in last:
                copy.wait_recv()
        for copy in table:
            copy.start()
        last = table
        value = refs.shared[hop]
        for move, copy in enumerate(copies):
            copy.wait_recv()
            value = value + refs.shared_came[hop, move]
        if hop:
            refs.sums[...] = value
        else:
            refs.shared[1] = value
        waits += copies + table
    for copy in last:
        copy.wait_recv()
    for copy in waits:
        copy.wait_send()


def backward_all(dims, layers, lines, weights, saved, near, logit_width):
    sizes = tuple(size for axis, size, stride in dims)
    spots = sizes[0] * sizes[1]
    order = [(kind, layer) for layer in reversed(range(layers)) for kind in (CONTRACT, EXPAND, ATTEND)]
    depth, square = weights[order[0]].shape[-2:]
    model = depth * sizes[2] * sizes[3]
    chunks = [((HEAD, 0), depth, logit_width, False)]
    chunks += [(name, depth, square, name[0] == ATTEND) for name in order]
    chunks += [((TABLE, 0), lines, model, False)]
    reducer = Reducer(dims, chunks, reduce_cuts)
    parts = Parts()
    parts.put(True, **near)
    for name in order:
        parts.put(key=name, weight=weights[name])
    parts.put(**saved)
    for name, height, across, wide in chunks:
        parts.out(full, True, key=name, total=(height, across))
    tall = 16 * (model // 128 + 1)
    parts.out(low, True, spread=(sizes[0], sizes[1], lines, model))
    parts.out(full, True, sums=(tall, 128))
    parts.keep(total_low=pltpu.VMEM((lines, model), low))
    reducer.declare(parts)
    largest = max(sizes[0] * sizes[1], sizes[2] * sizes[3])
    dma = pltpu.SemaphoreType.DMA
    parts.keep(
        slots=pltpu.VMEM((len(order), *sizes, depth, square), low),
        head_blocks=pltpu.VMEM((*sizes, depth, logit_width), low),
        weight_sem=dma((len(order),)),
        mlp_sem=dma((4,)),
        attend_sem=dma((4,)),
        grad=pltpu.VMEM((TOKENS, model), full),
        grad_normed=pltpu.VMEM((TOKENS, model), full),
        grad_low=pltpu.VMEM((TOKENS, model), low),
        turned=pltpu.VMEM((model, TOKENS), low),
        turned_two=pltpu.VMEM((model, TOKENS), low),
        grad_hidden=pltpu.VMEM((spots, TOKENS, square), low),
        norm_grads=pltpu.VMEM((16, model), full),
        shared=pltpu.VMEM((2, tall, 128), full),
        shared_came=pltpu.VMEM((2, largest, tall, 128), full),
        shared_send=dma((2, largest)),
        shared_recv=dma((2, largest)),
        spread_send=dma((2, largest)),
        spread_recv=dma((2, largest)),
        spread_own=dma,
    )
    for name, value in saved.items():
        parts.keep(**{"near_" + name: pltpu.VMEM(value.shape[1:], value.dtype)})
    body = functools.partial(
        backward_kernel, dims, reducer, layers, HEADS // spots, model // HEADS
    )
    return parts.call(body, 1)


def adam_kernel(layers, share, norms, part, refs):
    groups = ((refs.weight, refs.new_weight), (refs.one, refs.new_one), (refs.two, refs.new_two))
    order = (2, 3, 0, 1, 4, 5, 6)

    def moves(at, back):
        found = []
        for group, (source, target) in enumerate(groups):
            near, sem = refs.near[(at, group)], refs.sems.at[int(back), at, group]
            ends = (near, target[at]) if back else (source[at], near)
            found.append(pltpu.make_async_copy(*ends, sem))
        return found

    for at in order:
        for copy in moves(at, False):
            copy.start()

    norm = jnp.sqrt(jnp.sum(refs.sums[:8]) + jnp.sum(refs.sums[16:] * refs.sums[16:]))
    factor = clip_limit / jnp.maximum(norm, clip_limit)
    refs.norm[...] = jnp.full((1, 1), norm)
    refs.loss[...] = jnp.full((1, 1), jnp.sum(refs.sums[8:16]))
    refs.masked[...] = refs.count[:1, :1]

    def update(name, spot, gradient, rate_here, decay_here):
        near = [refs.near[(name, group)] for group in range(3)]
        found = adam_step(*[ref[spot] for ref in near], gradient, factor, rate_here, decay_here)
        for target, value in zip(near, found):
            target[spot] = value

    def arrived(name):
        for copy in moves(name, False):
            copy.wait()

    def leave(name):
        for copy in moves(name, True):
            copy.start()

    for name, kind in ((2, EXPAND), (3, CONTRACT)):
        arrived(name)
        for layer in range(layers):
            update(name, layer, refs.total[(kind, layer)][...], matrix_rate, weight_decay)
        leave(name)
    arrived(0)
    for layer in range(layers):
        attend = refs.total[(ATTEND, layer)]
        for at in range(3):
            update(0, (layer, at), attend[:, at * part : (at + 1) * part], matrix_rate, weight_decay)
    leave(0)
    arrived(1)
    for layer in range(layers):
        update(1, layer, refs.total[(ATTEND, layer)][:, 3 * part :].T, matrix_rate, weight_decay)
    leave(1)
    arrived(4)
    for spot in range(refs.spread.shape[0]):
        update(4, pl.ds(spot * share, share), refs.spread[spot].astype(full)[:share], embed_rate, weight_decay)
    leave(4)
    arrived(5)
    update(5, slice(None), refs.total[(HEAD, 0)][...], matrix_rate, weight_decay)
    leave(5)
    arrived(6)
    across = refs.weight[6].shape[2]
    start = lax.axis_index("dp") * across
    lanes = lax.broadcasted_iota(jnp.int32, (refs.spread.shape[2], across), 0)
    own = (lanes == start + lax.broadcasted_iota(jnp.int32, lanes.shape, 1)).astype(full)
    lines = jnp.concatenate([refs.sums[at : at + 16] for at in range(16, refs.sums.shape[0], 16)], axis=1)
    lines = jnp.dot(lines, own, precision=lax.Precision.HIGHEST, preferred_element_type=full)
    for at in range(norms):
        for kind in range(2):
            update(6, (at, pl.ds(kind, 1)), lines[2 * at + kind : 2 * at + kind + 1], vector_rate, 0.0)
    leave(6)
    for at in order:
        for copy in moves(at, True):
            copy.wait()


def adam_all(layers, share, norms, found, count, params, moments_one, moments_two):
    parts = Parts()
    parts.put(True, count=count, sums=found.sums, spread=found.spread.reshape(-1, *found.spread.shape[2:]))
    for name, value in found.total.items():
        parts.put(True, key=name, total=value)
    for at in range(7):
        parts.put(key=at, weight=params[at], one=moments_one[at], two=moments_two[at])
        shape = params[at].shape
        parts.out(full, key=at, new_weight=shape, new_one=shape, new_two=shape)
        for group in range(3):
            parts.keep(key=(at, group), near=pltpu.VMEM(shape, full))
    parts.keep(sems=pltpu.SemaphoreType.DMA((2, 7, 3)))
    parts.out(full, True, norm=(1, 1), loss=(1, 1), masked=(1, 1))
    return parts.call(functools.partial(adam_kernel, layers, share, norms, params[0].shape[3]))


class Gatherer:
    def __init__(self, dims, shapes):
        self.dims, self.shapes = dims, shapes
        self.sizes = [size for axis, size, stride in dims]
        self.units, self.slots = [], 0
        for chunk, (rows, width) in enumerate(shapes):
            for unit in gather_units(rows):
                found = []
                for row, size, order in unit:
                    found.append((row, size, order, self.slots))
                    self.slots += sum(size - 1 for size in self.sizes)
                self.units.append((chunk, found))

    def declare(self, parts):
        for at, shape in enumerate(self.shapes):
            parts.keep(key=at, piece=pltpu.VMEM(shape, low))
            parts.out(low, key=at, whole=(*self.sizes, *shape))
        parts.keep(
            send=pltpu.SemaphoreType.DMA((self.slots,)),
            recv=pltpu.SemaphoreType.DMA((self.slots,)),
            own=pltpu.SemaphoreType.DMA((len(self.shapes),)),
        )

    def bind(self, refs, here, prepare):
        self.refs, self.here, self.started, self.prepare = refs, here, [], prepare
        self.copies_own = {}
        self.ready = set()

    def copies(self, chunk, part, stage):
        row, size, order, slot = part
        dim, done = ORDERS[order][stage], ORDERS[order][:stage]
        slot += sum(self.sizes[at] - 1 for at in done)
        block = self.refs.whole[chunk].at[
            (*[slice(None) if at in done else self.here[at] for at in range(4)], pl.ds(row, size))
        ]
        source = block if stage else self.refs.piece[chunk].at[pl.ds(row, size)]
        return [
            pltpu.make_async_remote_copy(
                src_ref=source,
                dst_ref=block,
                send_sem=self.refs.send.at[slot + move - 1],
                recv_sem=self.refs.recv.at[slot + move - 1],
                device_id=peer_of(self.dims, self.here, (dim,), (move,)),
                device_id_type=MESH,
            )
            for move in range(1, self.sizes[dim])
        ]

    def tick(self, now):
        for at, (chunk, found) in enumerate(self.units):
            if (now - at) % 2 or not 0 <= now - at <= 8:
                continue
            stage = (now - at) // 2
            for part in found:
                if stage:
                    for copy in self.copies(chunk, part, stage - 1):
                        copy.wait_recv()
            if stage == 0 and chunk not in self.copies_own:
                self.prepare(chunk)
                copy = pltpu.make_async_copy(
                    self.refs.piece[chunk], self.refs.whole[chunk].at[tuple(self.here)], self.refs.own.at[chunk]
                )
                copy.start()
                self.copies_own[chunk] = copy
            if stage == 1 and chunk not in self.ready:
                self.copies_own[chunk].wait()
                self.ready.add(chunk)
            for part in found:
                if stage < 4:
                    for copy in self.copies(chunk, part, stage):
                        copy.start()
                        self.started.append(copy)

    def complete(self, chunk):
        return max(at for at, (other, found) in enumerate(self.units) if other == chunk) + 8

    def finish(self):
        for copy in self.started:
            copy.wait_send()


def norm_rows(source, gain, offset, target):
    value = source[...]
    centred = value - jnp.mean(value, axis=-1, keepdims=True)
    spread = lax.rsqrt(jnp.mean(centred * centred, axis=-1, keepdims=True) + norm_epsilon)
    target[...] = (centred * spread * gain[...] + offset[...]).astype(low)


def heads_forward(joined, heads, width):
    scale = width ** (-0.5)
    known = lax.broadcasted_iota(jnp.int32, (TOKENS, 1), 0) < SEQ
    real = lax.broadcasted_iota(jnp.int32, (TOKENS, 1), 0) < SEQ
    found = []
    for head in range(heads):
        query, key, value = [
            joined[:, (at * heads + head) * width : (at * heads + head + 1) * width] for at in range(3)
        ]
        scores = jnp.where(known, matmul_right(key, query) * scale, -1e30)
        probs = jnp.exp(scores - jnp.max(scores, axis=0, keepdims=True))
        probs = probs * (1.0 / jnp.sum(probs, axis=0, keepdims=True))
        found.append(jnp.where(real, matmul_left(probs.astype(low), value), 0.0).astype(low))
    return jnp.concatenate(found, axis=1)


def as_column(row):
    shape = (row.shape[1], row.shape[1])
    same = lax.broadcasted_iota(jnp.int32, shape, 0) == lax.broadcasted_iota(jnp.int32, shape, 1)
    return jnp.sum(jnp.where(same, row, 0.0), axis=1, keepdims=True)


def index_rows(refs, own, share, tensor, dp, lines):
    codes = refs.codes[pl.ds(own, 1), :].astype(full)
    flags = refs.flags[pl.ds(own, 1), :].astype(full)
    lanes = lax.broadcasted_iota(jnp.int32, refs.labels.shape, 1)
    label = jnp.sum(jnp.where(lanes == own, refs.labels[...].astype(full), 0.0), axis=1, keepdims=True)
    padding = jnp.zeros((1, TOKENS - SEQ), full)
    first = jnp.zeros((1, 1), full)
    token = lax.broadcasted_iota(jnp.int32, (1, TOKENS), 1)
    index = jnp.concatenate([label + (CODES + 1.0), jnp.where(flags == 1.0, float(CODES), codes), padding], axis=1)
    places = token.astype(full) + float(CODES + 1 + CLASSES)
    for at, values in enumerate((index, places)):
        block = jnp.floor((values + 0.5) * (1.0 / (share * tensor)))
        inside = values - block * (share * tensor)
        part = jnp.floor((inside + 0.5) * (1.0 / share))
        spot = part * (lines * dp) + block * lines + (inside - part * share)
        spot = jnp.where(token < SEQ, spot, -1.0)
        refs.rows[at : at + 1, :] = spot.astype(jnp.int32)
        refs.columns[:, at : at + 1] = as_column(spot).astype(jnp.int32)
    refs.columns[:, 2:3] = as_column(jnp.concatenate([first, codes, padding], axis=1)).astype(jnp.int32)
    refs.columns[:, 3:4] = as_column(jnp.concatenate([first, flags, padding], axis=1)).astype(jnp.int32)


def table_piece(refs, share, lines):
    norms, kinds, across = refs.norms.shape
    model = refs.table_own.shape[1]
    rows = []
    for norm in range(norms):
        both = refs.norms[norm]
        line = [both[0:1], jnp.zeros((1, 128 - across), full), both[1:2], jnp.zeros((1, model - 128 - across), full)]
        rows.append(jnp.concatenate(line, axis=1))
    masked = jnp.sum(refs.flags[...].astype(full), axis=1, keepdims=True)
    masked = jnp.sum(masked, axis=0, keepdims=True)
    high = jnp.floor(masked * (1.0 / 64.0))
    rows.append(jnp.concatenate([high, masked - high * 64.0, jnp.zeros((1, model - 2), full)], axis=1))
    rows.append(jnp.zeros((lines - share - norms - 1, model), full))
    refs.piece[0][...] = jnp.concatenate([refs.table_own[...]] + rows, axis=0).astype(low)


def forward_kernel(dims, gatherer, layers, share, heads, width, norms, refs):
    here = place_of(dims)
    sizes = gatherer.sizes
    spots = sizes[0] * sizes[1]
    part = heads * width
    last = len(gatherer.shapes) - 1
    lines = gatherer.shapes[0][0]
    own = here[0] * sizes[1] + here[1]
    fetch = pltpu.make_async_copy(
        refs.table.at[pl.ds(pl.multiple_of(own * share, 8), share)], refs.table_own, refs.table_sem
    )
    fetch.start()

    def prepare(chunk):
        piece = refs.piece[chunk]
        layer, kind = (chunk - 1) // 3, (chunk - 1) % 3
        if chunk == 0:
            fetch.wait()
            table_piece(refs, share, lines)
        elif chunk == last:
            piece[...] = refs.logit[...].astype(low)
        elif kind == 0:
            planes = [refs.attend_in[layer, at] for at in range(3)]
            piece[...] = jnp.concatenate(planes + [refs.attend_out[layer].T], axis=1).astype(low)
        else:
            piece[...] = (refs.expand, refs.contract)[kind - 1][layer].astype(low)

    gatherer.bind(refs, here, prepare)
    greet(dims, here)
    clock = [0]

    def run(until):
        while clock[0] <= until:
            gatherer.tick(clock[0])
            clock[0] += 1

    def load(chunk):
        run(gatherer.complete(chunk))
        near = refs.near_head if chunk == last else refs.slots.at[chunk % 3]
        if chunk == 0:
            near = near.at[:, :, :, :, pl.ds(0, gatherer.shapes[0][0])]
        copies = [
            pltpu.make_async_copy(refs.whole[chunk].at[outer], near.at[outer], refs.load_sem.at[chunk, outer])
            for outer in range(sizes[0])
        ]
        for copy in copies:
            copy.start()
        copies[0].wait()
        return near, copies[1:]

    def halves(chunk, step):
        near, later = load(chunk)

        def one(spot, carry):
            outer, pair = spot // sizes[1], spot % sizes[1]
            step(spot, square_block(near[outer, pair]))
            return carry

        lax.fori_loop(0, spots // 2, one, 0)
        run(min(clock[0], gatherer.complete(last)))
        for copy in later:
            copy.wait()
        lax.fori_loop(spots // 2, spots, one, 0)

    def load_whole(chunk):
        near, later = load(chunk)
        for copy in later:
            copy.wait()
        return near

    saves = []

    def save(near, far):
        copy = pltpu.make_async_copy(near, far, refs.save_sem.at[len(saves)])
        copy.start()
        saves.append(copy)

    run(1)
    index_rows(refs, own, share, spots, sizes[2] * sizes[3], lines)
    near = load_whole(0)
    block_rows = sizes[2] * sizes[3] * lines
    stream = refs.near_stream.at[0]
    stream[...] = jnp.zeros_like(stream)

    def table_step(spot, carry):
        column = spot * block_rows + lax.broadcasted_iota(jnp.int32, (TOKENS, block_rows), 1)
        picks = (column == refs.columns[:, 0:1]).astype(full) + (column == refs.columns[:, 1:2]).astype(full)
        stream[...] += matmul(picks.astype(low), square_block(near[spot // sizes[1], spot % sizes[1]]))
        return carry

    lax.fori_loop(0, spots, table_step, 0)
    save(stream, refs.stream.at[0])
    base = share // 16 * 16
    depth = gatherer.shapes[1][0]
    refs.gains[...] = jnp.zeros_like(refs.gains)
    count = jnp.zeros((1, 1), full)
    for far in range(sizes[2]):
        for close in range(sizes[3]):
            at = (far * sizes[3] + close) * depth
            rows = near[0, 0, far, close, base:lines, :256].astype(full)[share - base :]
            for norm in range(norms):
                for kind in range(2):
                    refs.gains[2 * norm + kind : 2 * norm + kind + 1, at : at + depth] = rows[
                        norm : norm + 1, kind * 128 : kind * 128 + depth
                    ]
            count = count + rows[norms : norms + 1, 0:1] * 64.0 + rows[norms : norms + 1, 1:2]
    refs.count[...] = jnp.broadcast_to(count, (8, 128))

    total = refs.running
    for layer in range(layers):
        stream, middle = refs.near_stream.at[layer], refs.near_middle.at[layer]
        gains = [refs.gains.at[pl.ds(4 * layer + at, 1)] for at in range(4)]

        normed = refs.near_normed.at[layer]
        norm_rows(stream, gains[0], gains[1], normed)
        save(normed, refs.normed.at[layer])
        middle[...] = stream[...]

        def attend_step(spot, held):
            joined = matmul(normed[...], held[:, : 3 * part]).astype(low)
            refs.near_joined[layer, spot] = joined
            blended = heads_forward(joined, heads, width)
            refs.near_blended[layer, spot] = blended
            middle[...] += matmul_right(blended, held[:, 3 * part :])

        halves(1 + 3 * layer, attend_step)
        save(refs.near_joined.at[layer], refs.joined.at[layer])
        save(refs.near_blended.at[layer], refs.blended.at[layer])
        save(middle, refs.middle.at[layer])
        normed_two = refs.near_normed_two.at[layer]
        norm_rows(middle, gains[2], gains[3], normed_two)
        save(normed_two, refs.normed_two.at[layer])

        def expand_step(spot, held):
            hidden = matmul(normed_two[...], held)
            side = 0.5 * (1.0 + lax.erf(hidden * (0.5**0.5)))
            refs.near_active[layer, spot] = (hidden * side).astype(low)
            refs.near_slope[layer, spot] = side + hidden * jnp.exp(-0.5 * hidden * hidden) * (0.5 / jnp.pi) ** 0.5

        halves(2 + 3 * layer, expand_step)
        save(refs.near_active.at[layer], refs.active.at[layer])
        save(refs.near_slope.at[layer], refs.slope.at[layer])
        after = refs.near_stream.at[layer + 1]
        after[...] = middle[...]

        def contract_step(spot, held):
            after[...] += matmul_right(refs.near_active[layer, spot], held)

        halves(3 + 3 * layer, contract_step)
        if layer + 1 < layers:
            save(after, refs.stream.at[layer + 1])

    near = load_whole(last)
    top = refs.near_stream.at[layers]
    norm_rows(top, refs.gains.at[pl.ds(4 * layers, 1)], refs.gains.at[pl.ds(4 * layers + 1, 1)], refs.final)
    local = near.shape[-1]
    for spot in range(spots):
        held = square_block(near[spot // sizes[1], spot % sizes[1]])
        refs.logits[:, spot * local : (spot + 1) * local] = matmul(refs.final[...], held)

    logits = refs.logits[...]
    wanted = refs.columns[:, 2:3] == lax.broadcasted_iota(jnp.int32, logits.shape, 1)
    weight = refs.columns[:, 3:4].astype(full)
    peak = jnp.max(logits, axis=-1, keepdims=True)
    log_total = peak + jnp.log(jnp.sum(jnp.exp(logits - peak), axis=-1, keepdims=True))
    picked = jnp.sum(jnp.where(wanted, logits, 0.0), axis=-1, keepdims=True)
    share_here = jnp.exp(logits - log_total) - wanted.astype(full)
    refs.grad_logits[...] = (share_here * (weight / count)).astype(low)
    loss = jnp.sum((log_total - picked) * weight, axis=0, keepdims=True)
    corner = (lax.broadcasted_iota(jnp.int32, (8, 128), 0) + lax.broadcasted_iota(jnp.int32, (8, 128), 1)) == 0
    refs.loss[...] = jnp.where(corner, jnp.broadcast_to(loss, (8, 128)), 0.0)
    total[...] = jnp.zeros_like(total)
    for spot in range(spots):
        held = square_block(near[spot // sizes[1], spot % sizes[1]])
        total[...] += matmul_right(refs.grad_logits[:, spot * local : (spot + 1) * local], held)
    refs.grad_top[...] = jnp.zeros_like(refs.grad_top)
    norm_back_rows(refs.grad_top, total, top, refs.gains.at[pl.ds(4 * layers, 1)], refs.final_grads, 0)
    for copy in saves:
        copy.wait()
    gatherer.finish()


def forward_all(dims, layers, share, lines, norms, params, codes, labels, flags):
    attend_in, attend_out, expand, contract, table, logit, norm_params = params
    sizes = tuple(size for axis, size, stride in dims)
    spots = sizes[0] * sizes[1]
    depth, square = expand.shape[1:]
    model = depth * sizes[2] * sizes[3]
    part = attend_in.shape[3]
    shapes = [(lines, model)] + [(depth, square)] * (3 * layers) + [logit.shape]
    gatherer = Gatherer(dims, shapes)
    parts = Parts()
    gatherer.declare(parts)
    parts.put(table=table)
    parts.put(True, attend_in=attend_in, attend_out=attend_out, expand=expand, contract=contract)
    parts.put(True, logit=logit, norms=norm_params, codes=codes, labels=labels, flags=flags)
    wide = dict(stream=(layers, TOKENS, model), middle=(layers, TOKENS, model), slope=(layers, spots, TOKENS, square))
    slim = dict(
        normed=(layers, TOKENS, model),
        normed_two=(layers, TOKENS, model),
        joined=(layers, spots, TOKENS, 3 * part),
        blended=(layers, spots, TOKENS, part),
        active=(layers, spots, TOKENS, square),
    )
    parts.out(full, **wide)
    parts.out(low, **slim)
    parts.out(full, True, gains=(16, model), grad_top=(TOKENS, model), final_grads=(2, model), loss=(8, 128), count=(8, 128))
    parts.out(jnp.int32, True, rows=(2, TOKENS))
    parts.out(low, True, final=(TOKENS, model), grad_logits=(TOKENS, spots * shapes[-1][1]))
    dma = pltpu.SemaphoreType.DMA
    for name, shape in wide.items():
        more = (layers + 1, *shape[1:]) if shape[1] == TOKENS else shape
        parts.keep(**{"near_" + name: pltpu.VMEM(more, full)})
    for name, shape in slim.items():
        parts.keep(**{"near_" + name: pltpu.VMEM(shape, low)})
    parts.keep(
        slots=pltpu.VMEM((3, *sizes, depth, square), low),
        near_head=pltpu.VMEM((*sizes, *shapes[-1]), low),
        columns=pltpu.VMEM((TOKENS, 4), jnp.int32),
        table_own=pltpu.VMEM((share, model), full),
        table_sem=dma,
        load_sem=dma((len(shapes), sizes[0])),
        save_sem=dma((8 * layers,)),
        running=pltpu.VMEM((TOKENS, model), full),
        logits=pltpu.VMEM((TOKENS, spots * shapes[-1][1]), full),
    )
    body = functools.partial(forward_kernel, dims, gatherer, layers, share, HEADS // spots, model // HEADS, norms)
    return parts.call(body, 0)


def body(dp, tensor, *args):
    (image_codes, labels, mask_flags), state = args[:3], args[3:]
    params, moments_one, moments_two = state[0::3], state[1::3], state[2::3]
    attend_in, attend_out, expand, contract, embed_table, logit_table, norm_params = params
    dims = factors(dp, tensor)
    sizes = tuple(size for axis, size, stride in dims)
    spots = list(range(tensor))
    own = lax.axis_index("tensor")
    depth = attend_in.shape[1]
    model = depth * dp
    part = attend_in.shape[3]
    norms = norm_params.shape[0]

    share = embed_table.shape[0] // tensor
    lines = -(-(share + norms + 1) // 16) * 16

    def turn(values):
        return [
            values[0].transpose(0, 2, 1, 3),
            values[1],
            values[2],
            values[3].transpose(0, 2, 1),
            *values[4:],
        ]

    params = turn(params)
    ahead = forward_all(
        dims, LAYERS, share, lines, norms, params, image_codes, labels.reshape(1, -1), mask_flags
    )
    kinds = [(kind, layer) for layer in range(LAYERS) for kind in (ATTEND, EXPAND, CONTRACT)]
    found = backward_all(
        dims,
        LAYERS,
        lines,
        {name: ahead.whole[at + 1] for at, name in enumerate(kinds)},
        dict(
            slope=ahead.slope,
            active=ahead.active,
            normed_two=ahead.normed_two,
            middle=ahead.middle,
            joined=ahead.joined,
            blended=ahead.blended,
            normed=ahead.normed,
            stream=ahead.stream,
        ),
        dict(
            rows=ahead.rows,
            gains=ahead.gains,
            grad_top=ahead.grad_top,
            final=ahead.final,
            grad_logits=ahead.grad_logits,
            final_grads=ahead.final_grads,
            loss=ahead.loss,
        ),
        logit_table.shape[1],
    )

    new = adam_all(LAYERS, share, norms, found, ahead.count, params, turn(moments_one), turn(moments_two))
    results = []
    for index in range(7):
        for group in (new.new_weight, new.new_one, new.new_two):
            value = group[index]
            results.append(
                value.transpose(0, 2, 1, 3) if index == 0 else value.transpose(0, 2, 1) if index == 3 else value
            )
    return (*results, new.loss.reshape(()), new.masked.reshape(()), new.norm.reshape(()))


def solution(mesh):
    dp, tensor = mesh.shape["dp"], mesh.shape["tensor"]
    in_specs = (
        (P("dp", None), P("dp"), P("dp", None))
        + (P(None, "dp", None, "tensor"),) * 3
        + (P(None, "tensor", "dp"),) * 3
        + (P(None, "dp", "tensor"),) * 3
        + (P(None, "tensor", "dp"),) * 3
        + (P("dp", None),) * 3
        + (P("dp", "tensor"),) * 3
        + (P(None, None, "dp"),) * 3
    )

    def either(*args):
        whole_tiles = args[3].shape[1] % 16 == 0 and args[1].shape[0] == tensor
        return body(dp, tensor, *args) if whole_tiles else plain_body(*args)

    return jax.shard_map(
        either,
        mesh=mesh,
        in_specs=in_specs,
        out_specs=in_specs[3:] + (P(), P(), P()),
        check_vma=False,
    )
```
